32 devices in a mesh: pipe: 4 (over y, core), ctx: 2 (over x), tp: 4 (over z).
Axes of the slice: x: 2, y: 2, z: 4, core: 2. Of those that a mesh axis runs over, the one named last changes fastest.
Arguments:
- hidden_in: bfloat16 [4, 256, 4096], P('pipe', 'ctx', 'tp'), may hold values from -8 to 8
- doc_ids: int32 [256], P('ctx'), may hold values from 0 to 3, never falling along the last dimension, each value on 1 to 128 neighbouring positions
- layer_kind: int32 [4], P('pipe'), may hold values from 0 to 1, as said below
- norm_gain: float32 [4, 4096], P('pipe', 'tp'), may hold values from 0.5 to 1.5
- q_weight: bfloat16 [4, 4096, 4096], P('pipe', 'ctx', 'tp'), may hold values from -2 to 2
- k_weight: bfloat16 [4, 4096, 512], P('pipe', 'ctx', 'tp'), may hold values from -1 to 1
- v_weight: bfloat16 [4, 4096, 512], P('pipe', 'ctx', 'tp'), may hold values from -0.09375 to 0.09375
- bc_weight: bfloat16 [4, 4096, 32], P('pipe', 'tp'), may hold values from -0.046875 to 0.046875
- dt_weight: bfloat16 [4, 4096, 64], P('pipe', 'tp'), may hold values from -0.09375 to 0.09375
- dt_bias: float32 [4, 64], P('pipe', 'tp'), may hold values from -1 to 1
- decay_rate: float32 [4, 64], P('pipe', 'tp'), may hold values from 0.0001953125 to 0.05
- skip_gain: float32 [4, 64], P('pipe', 'tp'), may hold values from 0.5 to 1.5
Outputs:
- section_out: bfloat16 [4, 256, 4096], P('pipe', 'ctx', 'tp')
- passed: bfloat16 [4, 256, 4096], P('pipe', 'ctx', 'tp')
The draws below stay inside these ranges and needn't reach their ends.
Inputs may be any that keep to these rules, and one draw needn't show every extreme that they name: `layer_kind`: every draw has at least one attention section and at least one state-space section.
All inputs are finite; a program needn't handle non-finite values.
Results may differ from the reference program's by a relative error of at most 0.011.
Values may be sent and summed in bfloat16 or wider, within the bound.
A program may use at most 64 MiB of HBM per device.

```python
import math
import jax
import jax.numpy as jnp
import numpy as np
from jax import lax

D = 4096
HEADS = 32
KVH = 4
HD = 128
STATE = 16
SSM_P = 64
SEQ = 256
SECTIONS = 4
SSM_HEADS = 64


def draw_layer_kind(key, part):
    base = jnp.array([0, 1], jnp.int32)
    extra = jax.random.randint(jax.random.fold_in(key, 11), (SECTIONS - 2,), 0, 2).astype(jnp.int32)
    full = jnp.concatenate([base, extra])
    return jax.random.permutation(jax.random.fold_in(key, 12), full).astype(jnp.int32)


def draw_hidden_in(key, part):
    drawn = jnp.clip(jax.random.normal(jax.random.fold_in(key, 31), (SECTIONS, SEQ, D), jnp.float32), -6.0, 6.0)
    return drawn.astype(jnp.bfloat16)


def draw_q_weight(key, part):
    columns = HEADS * HD
    drawn = jnp.clip(jax.random.normal(jax.random.fold_in(key, 21), (SECTIONS, D, columns), jnp.float32), -6.0, 6.0) * (3.0 * D ** (-0.5))
    return drawn.astype(jnp.bfloat16)


def draw_k_weight(key, part):
    columns = KVH * HD
    drawn = jnp.clip(jax.random.normal(jax.random.fold_in(key, 22), (SECTIONS, D, columns), jnp.float32), -6.0, 6.0) * D ** (-0.5)
    return drawn.astype(jnp.bfloat16)


def block_scale(own_key, shape, shards, least, largest):
    def one(axis_at, blocks):
        steps = jax.random.uniform(jax.random.fold_in(jax.random.fold_in(own_key, 6), axis_at), (blocks,), jnp.float32, least / len(shards), largest / len(shards))
        return jnp.repeat(jnp.exp(steps), shape[axis_at] // blocks).reshape((-1,) + (1,) * (len(shape) - axis_at - 1))

    level = one(*shards[0])
    for cut in shards[1:]:
        level = level * one(*cut)
    return level


def split_up(number_of, total, reach, skew):
    weights = [(1 << 20) // math.isqrt(grade ** skew) + 1 for grade in range(2, number_of + 1)]
    spare, given = total - reach - (number_of - 1), [1] * (number_of - 1)
    while spare > 0:
        movable = [i for i in range(number_of - 1) if given[i] < reach]
        mass, remaining = sum([weights[i] for i in movable]), spare
        for i in movable:
            more = min(reach - given[i], max(1, remaining * weights[i] // mass), spare)
            given[i] = given[i] + more
            spare = spare - more
    return np.array([reach] + given)


def ragged(key, count, total, reach, lean):
    if count == 2:
        one = jax.random.randint(key, (), max(1, total - reach), min(reach, total - 1) + 1)
        return jnp.stack([one, total - one])
    tallies = jnp.asarray(split_up(count, total, reach, lean), jnp.int32)
    pairs = (count - 1) // 2
    donor, receiver = tallies[1:1 + 2 * pairs:2], tallies[2:2 + 2 * pairs:2]
    room = jnp.minimum(donor - 1, reach - receiver)
    shifted = jax.random.randint(jax.random.fold_in(key, 1), (pairs,), 0, 1 << 20) % (room + 1)
    tallies = tallies.at[1:1 + 2 * pairs:2].set(donor - shifted).at[2:2 + 2 * pairs:2].set(receiver + shifted)
    return tallies[jax.random.permutation(jax.random.fold_in(key, 2), count)]


def normal_values(key, extent, width, most, cuts=(), kind=jnp.bfloat16):
    values = width * jax.random.normal(key, extent, jnp.float32)
    if cuts:
        values = values * block_scale(key, extent, cuts, -0.22, 0.18)
    return jnp.clip(values, -most, most).astype(kind)


def setup_inputs(seed: int = 0) -> dict:
    splits = jax.random.split(jax.random.key(seed), 13)
    hidden_in = draw_hidden_in(jax.random.fold_in(splits[12], 71), 0)
    doc_ids = jnp.searchsorted(jnp.cumsum(ragged(splits[1], 4, SEQ, SEQ // 2, 1)), jnp.arange(SEQ), side="right").astype(jnp.int32)
    layer_kind = draw_layer_kind(jax.random.fold_in(splits[12], 71), 0)
    norm_gain = jnp.clip(1.0 + 0.1 * jax.random.normal(splits[3], (SECTIONS, D), jnp.float32), 0.5, 1.5)
    q_weight = draw_q_weight(jax.random.fold_in(splits[12], 71), 0)
    k_weight = draw_k_weight(jax.random.fold_in(splits[12], 71), 0)
    v_weight = normal_values(splits[6], (SECTIONS, D, KVH * HD), D ** -0.5, 0.09375, ((0, 4), (1, 2), (2, 4)))
    bc_weight = normal_values(splits[7], (SECTIONS, D, 2 * STATE), (4 * D) ** -0.5, 0.046875, ((0, 4), (1, 4)))
    dt_weight = normal_values(splits[8], (SECTIONS, D, SSM_HEADS), D ** -0.5, 0.09375, ((0, 4), (1, 4)))
    dt_bias = jnp.clip(jax.random.uniform(splits[9], (SECTIONS, SSM_HEADS), jnp.float32, -1.0, 1.0) * block_scale(splits[9], (SECTIONS, SSM_HEADS), ((0, 4), (1, 4)), -0.4, 0.0), -1.0, 1.0)
    decay_rate = jnp.clip(jnp.exp(math.log(0.05) - 5.5451774 * jax.random.uniform(splits[10], (SECTIONS, SSM_HEADS), jnp.float32) ** block_scale(splits[10], (SECTIONS, SSM_HEADS), ((0, 4), (1, 4)), -0.2, 0.2)), 0.0001953125, 0.05)
    skip_gain = jnp.clip(0.5 + 1.0 * jax.random.uniform(splits[11], (SECTIONS, SSM_HEADS), jnp.float32) ** block_scale(splits[11], (SECTIONS, SSM_HEADS), ((0, 4), (1, 4)), -0.2, 0.2), 0.5, 1.5)
    return dict(hidden_in=hidden_in, doc_ids=doc_ids, layer_kind=layer_kind, norm_gain=norm_gain, q_weight=q_weight, k_weight=k_weight, v_weight=v_weight, bc_weight=bc_weight, dt_weight=dt_weight, dt_bias=dt_bias, decay_rate=decay_rate, skip_gain=skip_gain)


def normed(h, gain):
    hf = h.astype(jnp.float32)
    mean_sq = lax.optimization_barrier(jnp.mean(hf * hf, axis=1, keepdims=True))
    return (hf * lax.rsqrt(mean_sq + 1e-05) * gain[None, :]).astype(jnp.bfloat16)

def attention_layer(h, xn, wq, wk, wv, doc_ids):
    group = HEADS // KVH
    query = jnp.dot(xn, wq, preferred_element_type=jnp.float32).astype(jnp.bfloat16)
    query = jnp.transpose(query.reshape(SEQ, HEADS, HD), (1, 0, 2))
    keys = jnp.dot(xn, wk, preferred_element_type=jnp.float32).astype(jnp.bfloat16)
    keys = jnp.transpose(keys.reshape(SEQ, KVH, HD), (1, 0, 2))
    values = jnp.dot(xn, wv, preferred_element_type=jnp.float32).astype(jnp.bfloat16)
    values = jnp.transpose(values.reshape(SEQ, KVH, HD), (1, 0, 2))
    positions = jnp.arange(SEQ)
    block = 512 if SEQ % 512 == 0 else SEQ
    scale = HD ** (-0.5)

    def one_head(item):
        q_head, head = item
        kv_index = (head // group).astype(jnp.int32)
        k_head = lax.dynamic_index_in_dim(keys, kv_index, 0, keepdims=False)
        v_head = lax.dynamic_index_in_dim(values, kv_index, 0, keepdims=False)
        pieces = []
        for start in range(0, SEQ, block):
            end = start + block
            scores = jnp.dot(q_head[start:end], k_head[:end].T, preferred_element_type=jnp.float32) * scale
            allowed = (positions[None, :end] <= positions[start:end, None]) & (doc_ids[None, :end] == doc_ids[start:end, None])
            scores = jnp.where(allowed, scores, -jnp.inf)
            top = lax.optimization_barrier(jnp.max(scores, axis=1, keepdims=True))
            probs = jnp.where(allowed, jnp.exp(scores - top), 0.0)
            denom = lax.optimization_barrier(jnp.sum(probs, axis=1, keepdims=True))
            mixed = jnp.dot(probs.astype(jnp.bfloat16), v_head[:end], preferred_element_type=jnp.float32)
            pieces.append((mixed / denom).astype(jnp.bfloat16))
        return jnp.concatenate(pieces, axis=0)
    outputs = lax.map(one_head, (query, jnp.arange(HEADS).astype(jnp.int32)))
    attended = jnp.transpose(outputs, (1, 0, 2)).reshape(SEQ, D)
    return (h.astype(jnp.float32) + attended.astype(jnp.float32)).astype(jnp.bfloat16)

def state_layer(h, xn, wbc, wdt, bias, rate, skip, doc_ids):
    inputs = xn.astype(jnp.float32).reshape(SEQ, SSM_HEADS, SSM_P)
    step = jax.nn.softplus(jnp.dot(xn, wdt, preferred_element_type=jnp.float32) + bias[None, :])
    maps = jnp.dot(xn, wbc, preferred_element_type=jnp.float32)
    in_map = maps[:, :STATE]
    out_map = maps[:, STATE:]
    before = jnp.concatenate([jnp.full((1,), -1, jnp.int32), doc_ids[:-1].astype(jnp.int32)])
    keep = (doc_ids == before).astype(jnp.float32)
    decay = jnp.exp(-step * rate[None, :]) * keep[:, None]

    def advance(carry, item):
        dec, stp, b_row, c_row, x_row = item
        carry = dec[:, None, None] * carry + stp[:, None, None] * b_row[None, :, None] * x_row[:, None, :]
        return (carry, jnp.einsum('n,hnp->hp', c_row, carry))
    start = jnp.zeros((SSM_HEADS, STATE, SSM_P), jnp.float32)
    _, outputs = lax.scan(advance, start, (decay, step, in_map, out_map, inputs))
    outputs = outputs + skip[None, :, None] * inputs
    outputs = outputs * lax.rsqrt(lax.optimization_barrier(jnp.mean(outputs * outputs, axis=2, keepdims=True)) + 1e-05)
    return (h.astype(jnp.float32) + outputs.reshape(SEQ, D)).astype(jnp.bfloat16)

def reference(hidden_in, doc_ids, layer_kind, norm_gain, q_weight, k_weight, v_weight, bc_weight, dt_weight, dt_bias, decay_rate, skip_gain):
    results = []
    for section in range(SECTIONS):
        current = hidden_in[section]
        xn = normed(current, norm_gain[section])

        def attend_fn(h, xn=xn, section=section):
            return attention_layer(h, xn, q_weight[section], k_weight[section], v_weight[section], doc_ids)

        def state_fn(h, xn=xn, section=section):
            return state_layer(h, xn, bc_weight[section], dt_weight[section], dt_bias[section], decay_rate[section], skip_gain[section], doc_ids)
        results.append(lax.cond(layer_kind[section] == 1, attend_fn, state_fn, current))
    section_out = jnp.stack(results, axis=0)
    passed = jnp.concatenate([jnp.zeros((1, SEQ, D), jnp.bfloat16), section_out[:-1]], axis=0)
    return (section_out, passed)
```

```python
import jax
import jax.numpy as jnp
from jax import lax
from jax.experimental import pallas as pl
from jax.experimental.pallas import tpu as pltpu
from jax.sharding import PartitionSpec as P

D = 4096
HD = 128


def entering(x, axis, combine, identity):
    devices, index = (lax.axis_size(axis), lax.axis_index(axis))
    everything = jax.tree.map(
        lambda part, kind: lax.all_gather(part.astype(kind), axis), x, (jnp.bfloat16, jnp.bfloat16)
    )
    start = jax.tree.map(
        lambda part, zero: jnp.broadcast_to(jnp.asarray(zero, part.dtype), part.shape), x, identity
    )

    def turn(k, before):
        reached = k < index
        new = combine(
            before, jax.tree.map(lambda part, own: part[k].astype(own.dtype), everything, x)
        )
        return jax.tree.map(lambda a, b: jnp.where(reached, a, b), new, before)

    return lax.fori_loop(0, devices, turn, start)


def passed_along(x, axis, by):
    devices = lax.axis_size(axis)
    pairs = [(i, i + by) for i in range(devices) if 0 <= i + by < devices]
    return lax.ppermute(x, axis, pairs)


def make_fold(q_rows, q_pos, q_ids, ids_all, groups, head_size, active):
    rows = q_rows.shape[0]
    gsize = rows // groups
    q_top = jnp.max(q_pos.reshape(groups, gsize), axis=1)
    scale = head_size ** (-0.5)

    def update(state, piece_k, piece_v, key_pos, key_ids):
        top, denom, total = state
        scores = (
            jnp.einsum("tkjd,skd->kjts", q_rows, piece_k, preferred_element_type=jnp.float32)
            * scale
        )
        allowed = (key_pos[None, :] <= q_pos[:, None]) & (key_ids[None, :] == q_ids[:, None])
        scores = jnp.where(allowed[None, None], scores, -1e30)
        new_top = jnp.maximum(top, jnp.max(scores, axis=-1))
        probs = jnp.where(allowed[None, None], jnp.exp(scores - new_top[..., None]), 0.0)
        factor = jnp.exp(top - new_top)
        denom = denom * factor + jnp.sum(probs, axis=-1)
        total = total * factor[..., None] + jnp.einsum(
            "kjts,skd->kjtd",
            probs.astype(jnp.bfloat16),
            piece_v,
            preferred_element_type=jnp.float32,
        )
        return (new_top, denom, total)

    def fold(carry, piece, start):
        piece_k, piece_v = piece
        count = piece_k.shape[0]
        block = 512 if count % 512 == 0 else count
        for offset in range(0, count, block):
            key_start = start + offset
            key_pos = key_start + jnp.arange(block)
            key_ids = lax.dynamic_slice_in_dim(ids_all, key_start, block)
            block_k = piece_k[offset : offset + block]
            block_v = piece_v[offset : offset + block]
            low = 0

            def compute(state, low=low):
                return update(state, block_k, block_v, key_pos, key_ids)

            wanted = jnp.logical_and(active, key_start <= q_top[0])
            updated = [lax.cond(wanted, compute, lambda state: state, carry[0])]
            carry = tuple(updated)
        return carry

    def initial(kv_count, group):
        return tuple(
            (
                (
                    jnp.full((kv_count, group, gsize), -1e30, jnp.float32),
                    jnp.zeros((kv_count, group, gsize), jnp.float32),
                    jnp.zeros((kv_count, group, gsize, head_size), jnp.float32),
                )
                for index in range(groups)
            )
        )

    def finish(carry):
        parts = [
            total / jnp.where(denom > 0.0, denom, 1.0)[..., None] for top, denom, total in carry
        ]
        joined = parts[0]
        kv_count, group = (joined.shape[0], joined.shape[1])
        return (
            jnp.transpose(joined, (2, 0, 1, 3))
            .reshape(rows, kv_count * group * head_size)
            .astype(jnp.bfloat16)
        )

    return (fold, initial, finish)


def shards(
    hidden_in,
    doc_ids,
    layer_kind,
    norm_gain,
    q_weight,
    k_weight,
    v_weight,
    bc_weight,
    dt_weight,
    dt_bias,
    decay_rate,
    skip_gain,
):
    current = hidden_in[0]
    rows, width = current.shape
    ctx_pos = lax.axis_index("ctx")
    tp_pos = lax.axis_index("tp")
    ids_all = lax.all_gather(doc_ids, "ctx", axis=0, tiled=True)
    first = ctx_pos * rows
    prev_id = jnp.where(
        ctx_pos > 0,
        lax.dynamic_index_in_dim(ids_all, jnp.maximum(first - 1, 0), 0, keepdims=False),
        -1,
    )
    gain = norm_gain[0]
    head_size = HD
    q_cols = q_weight.shape[2]
    kv_cols = k_weight.shape[2]
    heads_local = q_cols // head_size
    kv_local = kv_cols // head_size
    group = heads_local // kv_local
    is_attention = layer_kind[0] == 1
    hf = current.astype(jnp.float32)
    squares = lax.psum(jnp.sum(hf * hf, axis=1), "tp")
    xn = (hf * lax.rsqrt(squares / D + 1e-05)[:, None] * gain[None, :]).astype(jnp.bfloat16)
    whole = lax.all_gather(xn, "tp", axis=1, tiled=True)
    empty = (
        jnp.zeros((rows, q_cols), jnp.float32),
        jnp.zeros((rows, kv_cols), jnp.float32),
        jnp.zeros((rows, kv_cols), jnp.float32),
    )
    pieces = (
        lax.all_gather(q_weight[0], "ctx", axis=0, tiled=True),
        lax.all_gather(k_weight[0], "ctx", axis=0, tiled=True),
        lax.all_gather(v_weight[0], "ctx", axis=0, tiled=True),
    )

    def really(values):
        return tuple(
            (jnp.dot(whole, piece, preferred_element_type=jnp.float32) for piece in pieces)
        )

    q_sum, k_sum, v_sum = lax.cond(is_attention, really, lambda values: values, empty)
    query = q_sum.astype(jnp.bfloat16).reshape(rows, kv_local, group, head_size)
    keys = k_sum.astype(jnp.bfloat16).reshape(rows, kv_local, head_size)
    values = v_sum.astype(jnp.bfloat16).reshape(rows, kv_local, head_size)
    q_pos = first + jnp.arange(rows)
    fold, initial, finish = make_fold(query, q_pos, doc_ids, ids_all, 1, head_size, is_attention)
    carry = fold(
        initial(kv_local, group),
        (
            lax.all_gather(keys, "ctx", axis=0, tiled=True),
            lax.all_gather(values, "ctx", axis=0, tiled=True),
        ),
        jnp.int32(0),
    )
    attended = finish(carry)
    attention_result = (current.astype(jnp.float32) + attended.astype(jnp.float32)).astype(
        jnp.bfloat16
    )
    ssm_local = dt_bias.shape[1]
    channels = width // ssm_local
    inputs = xn.astype(jnp.float32).reshape(rows, ssm_local, channels)
    maps, step_all = lax.psum(
        (
            jnp.dot(xn, bc_weight[0], preferred_element_type=jnp.float32),
            jnp.dot(xn, dt_weight[0], preferred_element_type=jnp.float32),
        ),
        "tp",
    )
    step = jax.nn.softplus(
        lax.dynamic_slice_in_dim(step_all, tp_pos * ssm_local, ssm_local, 1) + dt_bias[0][None, :]
    )
    state_size = maps.shape[1] // 2
    in_map = maps[:, :state_size]
    out_map = maps[:, state_size:]
    cumulative = jnp.cumsum(-step * decay_rate[0][None, :], axis=0)
    order = jnp.arange(rows)
    pairs = (doc_ids[:, None] == doc_ids[None, :]) & (order[:, None] >= order[None, :])
    exponent = jnp.where(
        pairs[:, :, None], cumulative[:, None, :] - cumulative[None, :, :], -jnp.inf
    )
    intersection = jnp.dot(out_map, in_map.T, precision=lax.Precision.HIGHEST)
    weighted = inputs * step[:, :, None]
    inner = jnp.einsum(
        "tsh,shp->thp",
        jnp.exp(exponent) * intersection[:, :, None],
        weighted,
        precision=lax.Precision.HIGHEST,
    )
    end_weight = (
        jnp.exp(cumulative[-1][None, :] - cumulative)
        * (doc_ids == doc_ids[-1]).astype(jnp.float32)[:, None]
    )
    end_state = jnp.einsum(
        "sh,sn,shp->hnp", end_weight, in_map, weighted, precision=lax.Precision.HIGHEST
    )
    total_decay = jnp.exp(cumulative[-1]) * (doc_ids[-1] == prev_id).astype(jnp.float32)

    def combine(earlier, later):
        return (earlier[0] * later[0], earlier[1] * later[0][:, None, None] + later[1])

    identity = (jnp.ones_like(total_decay), jnp.zeros_like(end_state))
    incoming = entering((total_decay, end_state), "ctx", combine, identity)[1]
    reach = jnp.exp(cumulative) * (doc_ids == prev_id).astype(jnp.float32)[:, None]
    carried = (
        jnp.einsum("tn,hnp->thp", out_map, incoming, precision=lax.Precision.HIGHEST)
        * reach[:, :, None]
    )
    outputs = inner + carried + skip_gain[0][None, :, None] * inputs
    outputs = outputs * lax.rsqrt(jnp.mean(outputs * outputs, axis=2, keepdims=True) + 1e-05)
    state_result = (current.astype(jnp.float32) + outputs.reshape(rows, width)).astype(jnp.bfloat16)
    produced = jnp.where(is_attention, attention_result, state_result)
    moved = passed_along(produced, "pipe", 1)
    return (produced[None], moved[None])


CHUNKS = 2
MESH = pl.DeviceIdType.MESH
F32 = jnp.float32
BF16 = jnp.bfloat16


def dot(a, b):
    return jnp.dot(a, b, preferred_element_type=F32)


def exact(a, b):
    return jnp.dot(a, b, preferred_element_type=F32, precision=lax.Precision.HIGHEST)


def column_of(row, count):
    same = lax.broadcasted_iota(jnp.int32, (count, count), 0) == lax.broadcasted_iota(
        jnp.int32, (count, count), 1
    )
    return jnp.sum(jnp.where(same, row, 0.0), axis=1, keepdims=True)


def kernel(
    h_ref,
    ids_ref,
    kind_ref,
    gain_ref,
    q_hbm,
    k_hbm,
    v_hbm,
    bc_ref,
    dt_ref,
    bias_ref,
    rate_ref,
    skip_ref,
    out_ref,
    passed_ref,
    blocks,
    wq,
    wkv,
    xn_ref,
    squares_out,
    squares_in,
    sums_out,
    sums_in,
    info_out,
    info_in,
    state_out,
    state_in,
    part_out,
    part_in,
    kvpart_out,
    kvpart_in,
    own_q,
    own_kv,
    kv_all,
    q_all,
    state_res,
    cols_ref,
    rows_ref,
    direct_ref,
    gram_ref,
    prod,
    prev,
    w_sem,
    right_sem,
    left_sem,
    across_sem,
    z_recv,
    x_recv,
    squares_ssem,
    squares_rsem,
    sums_ssem,
    sums_rsem,
    small_ssem,
    small_rsem,
    part_ssem,
    part_rsem,
    pipe_ssem,
    pipe_rsem,
):
    p, c, t = lax.axis_index("pipe"), lax.axis_index("ctx"), lax.axis_index("tp")
    pipes, tps = lax.axis_size("pipe"), lax.axis_size("tp")
    oc = 1 - c
    rows, width = h_ref.shape
    step_rows = rows // CHUNKS
    heads = bias_ref.shape[1]
    pairs = heads // 2
    channels = width // heads
    n_state = bc_ref.shape[1] // 2
    half = tps // 2
    q_cols = wq.shape[1]
    q_heads = q_cols // HD

    loads = [
        pltpu.make_async_copy(q_hbm, wq, w_sem.at[0]),
        pltpu.make_async_copy(k_hbm, wkv.at[0], w_sem.at[1]),
        pltpu.make_async_copy(v_hbm, wkv.at[1], w_sem.at[2]),
    ]
    for load in loads:
        load.start()

    barrier = pltpu.get_barrier_semaphore()
    for other in range(1, tps):
        pl.semaphore_signal(
            barrier, inc=1, device_id={"tp": lax.rem(t + other, tps)}, device_id_type=MESH
        )
    pl.semaphore_signal(barrier, inc=1, device_id={"ctx": oc}, device_id_type=MESH)

    @pl.when(p > 0)
    def _():
        pl.semaphore_signal(barrier, inc=1, device_id={"pipe": p - 1}, device_id_type=MESH)

    @pl.when(p < pipes - 1)
    def _():
        pl.semaphore_signal(barrier, inc=1, device_id={"pipe": p + 1}, device_id_type=MESH)

    hf = h_ref[...].astype(F32)
    gain = gain_ref[...]
    hg = (hf * gain).astype(BF16)
    blocks[c, t] = hg
    squares = jnp.sum(hf * hf, axis=1, keepdims=True)
    squares_out[...] = jnp.broadcast_to(squares, (rows, 128)).T[0:8]
    squares_in[t] = squares_out[...]

    neighbours = (p > 0).astype(jnp.int32) + (p < pipes - 1).astype(jnp.int32)
    pl.semaphore_wait(barrier, tps + neighbours)

    def span(ch):
        return pl.ds(ch * step_rows, step_rows)

    def to_tp(b, ch, target, sem):
        ref = blocks.at[c, b, span(ch)]
        return pltpu.make_async_remote_copy(
            ref, ref, sem, z_recv.at[b, ch], device_id={"tp": target}, device_id_type=MESH
        )

    def to_ctx(b, ch):
        ref = blocks.at[c, b, span(ch)]
        j = lax.rem(b, half)
        return pltpu.make_async_remote_copy(
            ref,
            ref,
            across_sem.at[j, ch],
            x_recv.at[j, ch],
            device_id={"ctx": oc},
            device_id_type=MESH,
        )

    def send_right(d, ch, go=True):
        @pl.when((t - d >= 0) & (t < tps - 1))
        def _():
            copy = to_tp(t - d, ch, t + 1, right_sem.at[d, ch])
            copy.start() if go else copy.wait_send()

    def send_left(d, ch, go=True):
        @pl.when((t + d < tps) & (t > 0))
        def _():
            copy = to_tp(t + d, ch, t - 1, left_sem.at[d, ch])
            copy.start() if go else copy.wait_send()

    def send_across(b, ch):
        @pl.when((b >= 0) & (b < tps) & (b // half == oc))
        def _():
            to_ctx(b, ch).start()

    def own_sends(ch):
        send_right(0, ch)
        send_left(0, ch)
        send_across(t, ch)

    def forward(d, ch):
        @pl.when(t - d >= 0)
        def _():
            to_tp(t - d, ch, t, right_sem.at[0, ch]).wait_recv()

        send_right(d, ch)
        send_across(t - d, ch)

        @pl.when(t + d < tps)
        def _():
            to_tp(t + d, ch, t, left_sem.at[0, ch]).wait_recv()

        send_left(d, ch)
        send_across(t + d, ch)

    def gathered(out, into, ssem, rsem, k, mine):
        source = out.at[k] if len(out.shape) == 3 else out
        place = t if mine else k
        return pltpu.make_async_remote_copy(
            source,
            into.at[place],
            ssem.at[k],
            rsem.at[place],
            device_id={"tp": k},
            device_id_type=MESH,
        )

    def squares_copy(k, mine):
        return gathered(squares_out, squares_in, squares_ssem, squares_rsem, k, mine)

    def sums_copy(k, mine):
        return gathered(sums_out, sums_in, sums_ssem, sums_rsem, k, mine)

    peers = [lax.rem(t + other, tps) for other in range(1, tps)]
    for k in peers:
        squares_copy(k, True).start()
    own_sends(0)
    for k in peers:
        squares_copy(k, False).wait_recv()
    squares = squares_in[0]
    for k in range(1, tps):
        squares = squares + squares_in[k]
    r_row = lax.rsqrt(squares / D + 1e-05)
    r_wide = jnp.broadcast_to(r_row[0:1], (128, rows)).T
    xn = (hf * r_wide[:, 0:1] * gain).astype(BF16)
    xn_ref[...] = xn
    dt_at = 2 * n_state
    packed = jnp.concatenate(
        [
            dot(xn, bc_ref[...]),
            dot(xn, dt_ref[...]),
            jnp.zeros((rows, 128 - dt_at - heads * tps), F32),
        ],
        axis=1,
    ).T
    for k in range(tps):
        dt_row = dt_at + k * heads
        sums_out[k] = jnp.concatenate([packed[:dt_at], packed[dt_row : dt_row + heads]], axis=0)
    sums_in[t] = sums_out[t]
    for k in peers:
        sums_copy(k, True).start()
    ids_row = ids_ref[...].astype(F32)
    info_out[0:8] = r_row
    info_out[8:16] = jnp.broadcast_to(ids_row, (8, rows))
    info_copy = pltpu.make_async_remote_copy(
        info_out,
        info_in,
        small_ssem.at[0],
        small_rsem.at[0],
        device_id={"ctx": oc},
        device_id_type=MESH,
    )
    info_copy.start()
    for ch in range(1, CHUNKS):
        own_sends(ch)
    for k in peers:
        sums_copy(k, False).wait_recv()

    total = sums_in[0]
    for k in range(1, tps):
        total = total + sums_in[k]
    maps = total[:dt_at]
    drive = total[dt_at : dt_at + heads] + column_of(bias_ref[...], heads)
    step = jnp.maximum(drive, 0.0) + jnp.log1p(jnp.exp(-jnp.abs(drive)))
    upper = (
        lax.broadcasted_iota(jnp.int32, (rows, rows), 0)
        <= lax.broadcasted_iota(jnp.int32, (rows, rows), 1)
    ).astype(F32)
    cum = exact(-step * column_of(rate_ref[...], heads), upper)
    cols = jnp.concatenate(
        [
            maps,
            cum,
            r_row,
            jnp.broadcast_to(ids_row, (8, rows)),
            step,
            jnp.zeros((128 - dt_at - 2 * heads - 16, rows), F32),
        ],
        axis=0,
    ).T
    cols_ref[...] = cols
    r_at = dt_at + heads
    ids_col = cols[:, r_at + 8 : r_at + 9]
    low = lax.broadcasted_iota(jnp.int32, (rows, rows), 0) > lax.broadcasted_iota(
        jnp.int32, (rows, rows), 1
    )
    allowed = (ids_col == ids_row) & low
    gram_ref[0] = jnp.where(allowed, exact(cols[:, n_state:dt_at], maps[:n_state]), 0.0)
    in_cols, out_cols = cols[:, :n_state], cols[:, n_state:dt_at]
    own_term = jnp.sum(in_cols * out_cols, axis=1, keepdims=True)
    direct_ref[...] = cols[:, r_at + 16 : r_at + 16 + heads] * own_term + skip_ref[...]
    gram_ref[1] = jnp.where(allowed, 0.0, -1e30)
    rows_ref[0:heads] = cum
    rows_ref[heads : 2 * heads] = step
    tail = (
        jnp.exp(cum[:, rows - 1 : rows] - cum)
        * jnp.where(ids_row == ids_row[:, rows - 1 : rows], 1.0, 0.0)
        * step
    )
    left_lanes = lax.broadcasted_iota(jnp.int32, (1, 2 * channels), 1) < channels
    for i in range(pairs):
        x_pair = xn_ref[:, i * 2 * channels : (i + 1) * 2 * channels]
        weights = jnp.concatenate(
            [maps[:n_state] * tail[2 * i + k : 2 * i + k + 1] for k in range(2)], axis=0
        ).astype(BF16)
        ends = dot(weights, x_pair)
        state_out[i] = jnp.where(left_lanes, ends[:n_state], ends[n_state:]).astype(BF16)
    state_copy = pltpu.make_async_remote_copy(
        state_out,
        state_in,
        small_ssem.at[1],
        small_rsem.at[1],
        device_id={"ctx": oc},
        device_id_type=MESH,
    )
    state_copy.start()

    def state_pair(i):
        x_pair = xn_ref[:, i * 2 * channels : (i + 1) * 2 * channels]
        outs, decays = [], []
        reach = jnp.where(
            (cols_ref[:, r_at + 8 : r_at + 9] == info_in[8:9, rows - 1 : rows]) & (c > 0), 1.0, 0.0
        )
        for head in (2 * i, 2 * i + 1):
            cum_col = cols_ref[:, dt_at + head : dt_at + head + 1]
            decay = jnp.exp(cum_col - rows_ref[head : head + 1] + gram_ref[1])
            mixed = decay * gram_ref[0] * rows_ref[heads + head : heads + head + 1]
            outs.append(dot(mixed.astype(BF16), x_pair))
            decays.append(jnp.exp(cum_col) * reach)
        skips = [direct_ref[:, 2 * i + k : 2 * i + k + 1] for k in range(2)]
        carried = dot(cols_ref[:, n_state:dt_at].astype(BF16), state_in[i])
        y = (
            jnp.where(left_lanes, outs[0], outs[1])
            + carried * jnp.where(left_lanes, decays[0], decays[1])
            + jnp.where(left_lanes, skips[0], skips[1]) * x_pair.astype(F32)
        )
        squared = y * y
        first = jnp.sum(jnp.where(left_lanes, squared, 0.0), axis=1, keepdims=True)
        second = jnp.sum(jnp.where(left_lanes, 0.0, squared), axis=1, keepdims=True)
        mean = jnp.where(left_lanes, first, second) / channels
        z = y * lax.rsqrt(mean + 1e-05)
        lanes = slice(i * 2 * channels, (i + 1) * 2 * channels)
        state_res[:, lanes] = (h_ref[:, lanes].astype(F32) + z).astype(BF16)

    def project(tok, ch, column):
        total = None
        for j in range(half):
            x = blocks[tok, half * c + j, span(ch)]
            depth = slice(j * width, (j + 1) * width)
            if column < q_cols:
                w = wq[depth, column : column + 256]
            else:
                w = jnp.concatenate([wkv[0, depth], wkv[1, depth]], axis=1)
            term = dot(x, w)
            total = term if total is None else total + term
        return total

    def part_copy(ch):
        return pltpu.make_async_remote_copy(
            part_out.at[span(ch)],
            part_in.at[span(ch)],
            part_ssem.at[0, ch],
            part_rsem.at[0, ch],
            device_id={"ctx": oc},
            device_id_type=MESH,
        )

    def kvpart_copy(ch):
        return pltpu.make_async_remote_copy(
            kvpart_out.at[span(ch)],
            kvpart_in.at[span(ch)],
            part_ssem.at[1, ch],
            part_rsem.at[1, ch],
            device_id={"ctx": oc},
            device_id_type=MESH,
        )

    def x_arrival(j, ch):
        ref = blocks.at[oc, half * c + j, span(ch)]
        return pltpu.make_async_remote_copy(
            ref,
            ref,
            across_sem.at[j, ch],
            x_recv.at[j, ch],
            device_id={"ctx": oc},
            device_id_type=MESH,
        )

    def project_theirs(ch):
        for j in range(half):
            x_arrival(j, ch).wait_recv()
        for column in range(0, q_cols + 256, 256):
            value = project(oc, ch, column)
            part_out[span(ch), column : column + 256] = value.astype(BF16)
            if column == q_cols:
                own_kv[oc, span(ch)] = value
        part_copy(ch).start()

    def project_ours(ch):
        value = project(c, ch, q_cols)
        own_kv[c, span(ch)] = value
        kvpart_out[span(ch)] = value.astype(BF16)
        kvpart_copy(ch).start()
        for column in range(0, q_cols, 256):
            own_q[span(ch), column : column + 256] = project(c, ch, column)

    done = 0
    steps = [(ch, d) for ch in range(CHUNKS) for d in range(1, tps)]
    for n, (ch, d) in enumerate(steps):
        forward(d, ch)
        if n == 0:
            info_copy.wait_recv()
            state_copy.wait_recv()
            for load in loads:
                load.wait()
        upto = pairs * (n + 1) // len(steps)
        for i in range(done, upto):
            state_pair(i)
        done = upto
        if d == tps - 1:
            project_theirs(ch)
            project_ours(ch)

    r_col = cols_ref[:, r_at : r_at + 1]
    their_r = jnp.broadcast_to(info_in[0:1], (128, rows)).T[:, 0:1]
    for ch in range(CHUNKS):
        part_copy(ch).wait_recv()
        kvpart_copy(ch).wait_recv()
    q_all[...] = ((own_q[...] + part_in[:, :q_cols].astype(F32)) * r_col).astype(BF16)
    kv_all[c] = ((own_kv[c] + part_in[:, q_cols:].astype(F32)) * r_col).astype(BF16)
    kv_all[oc] = ((own_kv[oc] + kvpart_in[...].astype(F32)) * their_r).astype(BF16)

    key_pos = lax.broadcasted_iota(jnp.int32, (rows, 2 * rows), 1)
    query_pos = c * rows + lax.broadcasted_iota(jnp.int32, (rows, 2 * rows), 0)
    my_ids, their_ids = ids_row, info_in[8:9]
    at_first = jnp.where(c == 0, my_ids, their_ids)
    at_second = jnp.where(c == 0, their_ids, my_ids)
    key_ids = jnp.concatenate([at_first, at_second], axis=1)
    wanted = (key_pos <= query_pos) & (key_ids == cols_ref[:, r_at + 8 : r_at + 9])
    keys = kv_all[:, :, :HD].reshape(2 * rows, HD)
    values = kv_all[:, :, HD:].reshape(2 * rows, HD)
    attention = kind_ref[...] == 1
    per = prod.shape[2] // HD

    def pipe_copy(k):
        return pltpu.make_async_remote_copy(
            prod.at[k],
            prev.at[k],
            pipe_ssem.at[k],
            pipe_rsem.at[k],
            device_id={"pipe": p + 1},
            device_id_type=MESH,
        )

    for head in range(q_heads):
        lanes = slice(head * HD, (head + 1) * HD)
        scores = lax.dot_general(
            q_all[:, lanes], keys, (((1,), (1,)), ((), ())), preferred_element_type=F32
        ) * (HD ** (-0.5))
        scores = jnp.where(wanted, scores, -1e30)
        top = jnp.max(scores, axis=1, keepdims=True)
        probs = jnp.where(wanted, jnp.exp(scores - top), 0.0)
        denom = jnp.sum(probs, axis=1, keepdims=True)
        mixed = (dot(probs.astype(BF16), values) / denom).astype(BF16)
        attended = (h_ref[:, lanes].astype(F32) + mixed.astype(F32)).astype(BF16)
        result = jnp.where(
            jnp.broadcast_to(attention, (rows, HD)),
            attended.astype(F32),
            state_res[:, lanes].astype(F32),
        ).astype(BF16)
        out_ref[:, lanes] = result
        inner = head % per
        prod[head // per, :, inner * HD : (inner + 1) * HD] = result
        if inner == per - 1:

            @pl.when(p < pipes - 1)
            def _(k=head // per):
                pipe_copy(k).start()

    for ch in range(CHUNKS):
        for d in range(tps):
            send_right(d, ch, False)
            send_left(d, ch, False)
        for j in range(half):
            to_ctx(half * oc + j, ch).wait_send()
        part_copy(ch).wait_send()
        kvpart_copy(ch).wait_send()
    for k in peers:
        squares_copy(k, True).wait_send()
        sums_copy(k, True).wait_send()
    info_copy.wait_send()
    state_copy.wait_send()

    span_p = prod.shape[2]

    @pl.when(p > 0)
    def _():
        for k in range(q_heads // per):
            pipe_copy(k).wait_recv()
            passed_ref[:, k * span_p : (k + 1) * span_p] = prev[k]

    @pl.when(p == 0)
    def _():
        passed_ref[...] = jnp.zeros(passed_ref.shape, BF16)

    @pl.when(p < pipes - 1)
    def _():
        for k in range(q_heads // per):
            pipe_copy(k).wait_send()


def fused(
    hidden_in,
    doc_ids,
    layer_kind,
    norm_gain,
    q_weight,
    k_weight,
    v_weight,
    bc_weight,
    dt_weight,
    dt_bias,
    decay_rate,
    skip_gain,
):
    _, rows, width = hidden_in.shape
    depth, q_cols = q_weight.shape[1:]
    kv_cols = k_weight.shape[2]
    heads = dt_bias.shape[1]
    n_state = bc_weight.shape[2] // 2
    tps = lax.axis_size("tp")
    vmem = pl.BlockSpec(memory_space=pltpu.VMEM)
    anywhere = pl.BlockSpec(memory_space=pl.ANY)
    small = 2 * n_state + heads
    dma = pltpu.SemaphoreType.DMA
    shape = jax.ShapeDtypeStruct((rows, width), BF16)
    out, passed = pl.pallas_call(
        kernel,
        out_shape=(shape, shape),
        in_specs=[vmem] * 4 + [anywhere] * 3 + [vmem] * 5,
        out_specs=(vmem, vmem),
        scratch_shapes=[
            pltpu.VMEM((2, tps, rows, width), BF16),
            pltpu.VMEM((depth, q_cols), BF16),
            pltpu.VMEM((2, depth, kv_cols), BF16),
            pltpu.VMEM((rows, width), BF16),
            pltpu.VMEM((8, rows), F32),
            pltpu.VMEM((tps, 8, rows), F32),
            pltpu.VMEM((tps, small, rows), F32),
            pltpu.VMEM((tps, small, rows), F32),
            pltpu.VMEM((16, rows), F32),
            pltpu.VMEM((16, rows), F32),
            pltpu.VMEM((heads // 2, n_state, 2 * width // heads), BF16),
            pltpu.VMEM((heads // 2, n_state, 2 * width // heads), BF16),
            pltpu.VMEM((rows, q_cols + 2 * kv_cols), BF16),
            pltpu.VMEM((rows, q_cols + 2 * kv_cols), BF16),
            pltpu.VMEM((rows, 2 * kv_cols), BF16),
            pltpu.VMEM((rows, 2 * kv_cols), BF16),
            pltpu.VMEM((rows, q_cols), F32),
            pltpu.VMEM((2, rows, 2 * kv_cols), F32),
            pltpu.VMEM((2, rows, 2 * kv_cols), BF16),
            pltpu.VMEM((rows, q_cols), BF16),
            pltpu.VMEM((rows, width), BF16),
            pltpu.VMEM((rows, 128), F32),
            pltpu.VMEM((2 * heads, rows), F32),
            pltpu.VMEM((rows, heads), F32),
            pltpu.VMEM((2, rows, rows), F32),
            pltpu.VMEM((4, rows, width // 4), BF16),
            pltpu.VMEM((4, rows, width // 4), BF16),
            dma((3,)),
            dma((tps, CHUNKS)),
            dma((tps, CHUNKS)),
            dma((tps // 2, CHUNKS)),
            dma((tps, CHUNKS)),
            dma((tps // 2, CHUNKS)),
            dma((tps,)),
            dma((tps,)),
            dma((tps,)),
            dma((tps,)),
            dma((2,)),
            dma((2,)),
            dma((2, CHUNKS)),
            dma((2, CHUNKS)),
            dma((4,)),
            dma((4,)),
        ],
        compiler_params=pltpu.CompilerParams(
            collective_id=0, has_side_effects=True, vmem_limit_bytes=40 * 2**20
        ),
        cost_estimate=pl.CostEstimate(
            flops=4 * rows * depth * (q_cols + 2 * kv_cols),
            bytes_accessed=2 * depth * (q_cols + 2 * kv_cols),
            transcendentals=0,
        ),
    )(
        hidden_in[0],
        doc_ids[None],
        layer_kind[None],
        norm_gain,
        q_weight[0],
        k_weight[0],
        v_weight[0],
        bc_weight[0],
        dt_weight[0],
        dt_bias,
        decay_rate,
        skip_gain,
    )
    return out[None], passed[None]


def solution(mesh):
    in_specs = (
        P("pipe", "ctx", "tp"),
        P("ctx"),
        P("pipe"),
        P("pipe", "tp"),
        P("pipe", "ctx", "tp"),
        P("pipe", "ctx", "tp"),
        P("pipe", "ctx", "tp"),
        P("pipe", "tp", None),
        P("pipe", "tp", None),
        P("pipe", "tp"),
        P("pipe", "tp"),
        P("pipe", "tp"),
    )
    out_specs = (P("pipe", "ctx", "tp"), P("pipe", "ctx", "tp"))
    body = fused if mesh.shape["ctx"] == 2 and mesh.shape["tp"] == 4 else shards
    return jax.shard_map(body, mesh=mesh, in_specs=in_specs, out_specs=out_specs, check_vma=False)
```

```python
import jax
import jax.numpy as jnp
from jax import lax
from jax.experimental import pallas as pl
from jax.experimental.pallas import tpu as pltpu
from jax.sharding import PartitionSpec as P

D = 4096
HD = 128


def entering(x, axis, combine, identity):
    devices, index = (lax.axis_size(axis), lax.axis_index(axis))
    everything = jax.tree.map(
        lambda part, kind: lax.all_gather(part.astype(kind), axis), x, (jnp.bfloat16, jnp.bfloat16)
    )
    start = jax.tree.map(
        lambda part, zero: jnp.broadcast_to(jnp.asarray(zero, part.dtype), part.shape), x, identity
    )

    def turn(k, before):
        reached = k < index
        new = combine(
            before, jax.tree.map(lambda part, own: part[k].astype(own.dtype), everything, x)
        )
        return jax.tree.map(lambda a, b: jnp.where(reached, a, b), new, before)

    return lax.fori_loop(0, devices, turn, start)


def passed_along(x, axis, by):
    devices = lax.axis_size(axis)
    pairs = [(i, i + by) for i in range(devices) if 0 <= i + by < devices]
    return lax.ppermute(x, axis, pairs)


def make_fold(q_rows, q_pos, q_ids, ids_all, groups, head_size, active):
    rows = q_rows.shape[0]
    gsize = rows // groups
    q_top = jnp.max(q_pos.reshape(groups, gsize), axis=1)
    scale = head_size ** (-0.5)

    def update(state, piece_k, piece_v, key_pos, key_ids):
        top, denom, total = state
        scores = (
            jnp.einsum("tkjd,skd->kjts", q_rows, piece_k, preferred_element_type=jnp.float32)
            * scale
        )
        allowed = (key_pos[None, :] <= q_pos[:, None]) & (key_ids[None, :] == q_ids[:, None])
        scores = jnp.where(allowed[None, None], scores, -1e30)
        new_top = jnp.maximum(top, jnp.max(scores, axis=-1))
        probs = jnp.where(allowed[None, None], jnp.exp(scores - new_top[..., None]), 0.0)
        factor = jnp.exp(top - new_top)
        denom = denom * factor + jnp.sum(probs, axis=-1)
        total = total * factor[..., None] + jnp.einsum(
            "kjts,skd->kjtd",
            probs.astype(jnp.bfloat16),
            piece_v,
            preferred_element_type=jnp.float32,
        )
        return (new_top, denom, total)

    def fold(carry, piece, start):
        piece_k, piece_v = piece
        count = piece_k.shape[0]
        block = 512 if count % 512 == 0 else count
        for offset in range(0, count, block):
            key_start = start + offset
            key_pos = key_start + jnp.arange(block)
            key_ids = lax.dynamic_slice_in_dim(ids_all, key_start, block)
            block_k = piece_k[offset : offset + block]
            block_v = piece_v[offset : offset + block]
            low = 0

            def compute(state, low=low):
                return update(state, block_k, block_v, key_pos, key_ids)

            wanted = jnp.logical_and(active, key_start <= q_top[0])
            updated = [lax.cond(wanted, compute, lambda state: state, carry[0])]
            carry = tuple(updated)
        return carry

    def initial(kv_count, group):
        return tuple(
            (
                (
                    jnp.full((kv_count, group, gsize), -1e30, jnp.float32),
                    jnp.zeros((kv_count, group, gsize), jnp.float32),
                    jnp.zeros((kv_count, group, gsize, head_size), jnp.float32),
                )
                for index in range(groups)
            )
        )

    def finish(carry):
        parts = [
            total / jnp.where(denom > 0.0, denom, 1.0)[..., None] for top, denom, total in carry
        ]
        joined = parts[0]
        kv_count, group = (joined.shape[0], joined.shape[1])
        return (
            jnp.transpose(joined, (2, 0, 1, 3))
            .reshape(rows, kv_count * group * head_size)
            .astype(jnp.bfloat16)
        )

    return (fold, initial, finish)


def shards(
    hidden_in,
    doc_ids,
    layer_kind,
    norm_gain,
    q_weight,
    k_weight,
    v_weight,
    bc_weight,
    dt_weight,
    dt_bias,
    decay_rate,
    skip_gain,
):
    current = hidden_in[0]
    rows, width = current.shape
    ctx_pos = lax.axis_index("ctx")
    tp_pos = lax.axis_index("tp")
    ids_all = lax.all_gather(doc_ids, "ctx", axis=0, tiled=True)
    first = ctx_pos * rows
    prev_id = jnp.where(
        ctx_pos > 0,
        lax.dynamic_index_in_dim(ids_all, jnp.maximum(first - 1, 0), 0, keepdims=False),
        -1,
    )
    gain = norm_gain[0]
    head_size = HD
    q_cols = q_weight.shape[2]
    kv_cols = k_weight.shape[2]
    heads_local = q_cols // head_size
    kv_local = kv_cols // head_size
    group = heads_local // kv_local
    is_attention = layer_kind[0] == 1
    hf = current.astype(jnp.float32)
    squares = lax.psum(jnp.sum(hf * hf, axis=1), "tp")
    xn = (hf * lax.rsqrt(squares / D + 1e-05)[:, None] * gain[None, :]).astype(jnp.bfloat16)
    whole = lax.all_gather(xn, "tp", axis=1, tiled=True)
    empty = (
        jnp.zeros((rows, q_cols), jnp.float32),
        jnp.zeros((rows, kv_cols), jnp.float32),
        jnp.zeros((rows, kv_cols), jnp.float32),
    )
    pieces = (
        lax.all_gather(q_weight[0], "ctx", axis=0, tiled=True),
        lax.all_gather(k_weight[0], "ctx", axis=0, tiled=True),
        lax.all_gather(v_weight[0], "ctx", axis=0, tiled=True),
    )

    def really(values):
        return tuple(
            (jnp.dot(whole, piece, preferred_element_type=jnp.float32) for piece in pieces)
        )

    q_sum, k_sum, v_sum = lax.cond(is_attention, really, lambda values: values, empty)
    query = q_sum.astype(jnp.bfloat16).reshape(rows, kv_local, group, head_size)
    keys = k_sum.astype(jnp.bfloat16).reshape(rows, kv_local, head_size)
    values = v_sum.astype(jnp.bfloat16).reshape(rows, kv_local, head_size)
    q_pos = first + jnp.arange(rows)
    fold, initial, finish = make_fold(query, q_pos, doc_ids, ids_all, 1, head_size, is_attention)
    carry = fold(
        initial(kv_local, group),
        (
            lax.all_gather(keys, "ctx", axis=0, tiled=True),
            lax.all_gather(values, "ctx", axis=0, tiled=True),
        ),
        jnp.int32(0),
    )
    attended = finish(carry)
    attention_result = (current.astype(jnp.float32) + attended.astype(jnp.float32)).astype(
        jnp.bfloat16
    )
    ssm_local = dt_bias.shape[1]
    channels = width // ssm_local
    inputs = xn.astype(jnp.float32).reshape(rows, ssm_local, channels)
    maps, step_all = lax.psum(
        (
            jnp.dot(xn, bc_weight[0], preferred_element_type=jnp.float32),
            jnp.dot(xn, dt_weight[0], preferred_element_type=jnp.float32),
        ),
        "tp",
    )
    step = jax.nn.softplus(
        lax.dynamic_slice_in_dim(step_all, tp_pos * ssm_local, ssm_local, 1) + dt_bias[0][None, :]
    )
    state_size = maps.shape[1] // 2
    in_map = maps[:, :state_size]
    out_map = maps[:, state_size:]
    cumulative = jnp.cumsum(-step * decay_rate[0][None, :], axis=0)
    order = jnp.arange(rows)
    pairs = (doc_ids[:, None] == doc_ids[None, :]) & (order[:, None] >= order[None, :])
    exponent = jnp.where(
        pairs[:, :, None], cumulative[:, None, :] - cumulative[None, :, :], -jnp.inf
    )
    intersection = jnp.dot(out_map, in_map.T, precision=lax.Precision.HIGHEST)
    weighted = inputs * step[:, :, None]
    inner = jnp.einsum(
        "tsh,shp->thp",
        jnp.exp(exponent) * intersection[:, :, None],
        weighted,
        precision=lax.Precision.HIGHEST,
    )
    end_weight = (
        jnp.exp(cumulative[-1][None, :] - cumulative)
        * (doc_ids == doc_ids[-1]).astype(jnp.float32)[:, None]
    )
    end_state = jnp.einsum(
        "sh,sn,shp->hnp", end_weight, in_map, weighted, precision=lax.Precision.HIGHEST
    )
    total_decay = jnp.exp(cumulative[-1]) * (doc_ids[-1] == prev_id).astype(jnp.float32)

    def combine(earlier, later):
        return (earlier[0] * later[0], earlier[1] * later[0][:, None, None] + later[1])

    identity = (jnp.ones_like(total_decay), jnp.zeros_like(end_state))
    incoming = entering((total_decay, end_state), "ctx", combine, identity)[1]
    reach = jnp.exp(cumulative) * (doc_ids == prev_id).astype(jnp.float32)[:, None]
    carried = (
        jnp.einsum("tn,hnp->thp", out_map, incoming, precision=lax.Precision.HIGHEST)
        * reach[:, :, None]
    )
    outputs = inner + carried + skip_gain[0][None, :, None] * inputs
    outputs = outputs * lax.rsqrt(jnp.mean(outputs * outputs, axis=2, keepdims=True) + 1e-05)
    state_result = (current.astype(jnp.float32) + outputs.reshape(rows, width)).astype(jnp.bfloat16)
    produced = jnp.where(is_attention, attention_result, state_result)
    moved = passed_along(produced, "pipe", 1)
    return (produced[None], moved[None])


CHUNKS = 2
MESH = pl.DeviceIdType.MESH
F32 = jnp.float32
BF16 = jnp.bfloat16


def dot(a, b):
    return jnp.dot(a, b, preferred_element_type=F32)


def exact(a, b):
    return jnp.dot(a, b, preferred_element_type=F32, precision=lax.Precision.HIGHEST)


def column_of(row, count):
    same = lax.broadcasted_iota(jnp.int32, (count, count), 0) == lax.broadcasted_iota(
        jnp.int32, (count, count), 1
    )
    return jnp.sum(jnp.where(same, row, 0.0), axis=1, keepdims=True)


def kernel(
    h_hbm,
    gain_hbm,
    bc_hbm,
    dt_hbm,
    ids_hbm,
    kind_hbm,
    bias_hbm,
    rate_hbm,
    skip_hbm,
    q_hbm,
    k_hbm,
    v_hbm,
    out_ref,
    passed_ref,
    h_ref,
    gain_ref,
    bc_ref,
    dt_ref,
    ids_ref,
    kind_ref,
    bias_ref,
    rate_ref,
    skip_ref,
    blocks,
    weight,
    xn_ref,
    squares_out,
    squares_in,
    sums_out,
    sums_in,
    info_out,
    info_in,
    state_out,
    state_in,
    part_out,
    part_in,
    kvpart_out,
    kvpart_in,
    sums_q,
    kv_all,
    q_all,
    state_res,
    cols_ref,
    rows_ref,
    direct_ref,
    gram_ref,
    prod,
    prev,
    w_sem,
    right_sem,
    left_sem,
    across_sem,
    z_recv,
    x_recv,
    squares_ssem,
    squares_rsem,
    sums_ssem,
    sums_rsem,
    small_ssem,
    small_rsem,
    part_ssem,
    part_rsem,
    pipe_ssem,
    pipe_rsem,
):
    p, c, t = lax.axis_index("pipe"), lax.axis_index("ctx"), lax.axis_index("tp")
    pipes, tps = lax.axis_size("pipe"), lax.axis_size("tp")
    oc = 1 - c
    rows, width = h_ref.shape
    step_rows = rows // CHUNKS
    heads = bias_ref.shape[1]
    pairs = heads // 2
    channels = width // heads
    n_state = bc_ref.shape[0] // 2
    half = tps // 2
    q_cols = q_hbm.shape[1]
    kv_cols = k_hbm.shape[1]
    all_cols = q_cols + 2 * kv_cols
    q_heads = q_cols // HD

    pairs_in = [
        (h_hbm, h_ref),
        (gain_hbm, gain_ref),
        (bc_hbm, bc_ref),
        (dt_hbm, dt_ref),
        (ids_hbm, ids_ref),
        (kind_hbm, kind_ref),
        (bias_hbm, bias_ref),
        (rate_hbm, rate_ref),
        (skip_hbm, skip_ref),
        (q_hbm, weight.at[:, pl.ds(0, q_cols)]),
        (k_hbm, weight.at[:, pl.ds(q_cols, kv_cols)]),
        (v_hbm, weight.at[:, pl.ds(q_cols + kv_cols, kv_cols)]),
    ]
    loads = [
        pltpu.make_async_copy(source, into, w_sem.at[n])
        for n, (source, into) in enumerate(pairs_in)
    ]
    for load in loads:
        load.start()

    barrier = pltpu.get_barrier_semaphore()
    for other in range(1, tps):
        pl.semaphore_signal(
            barrier, inc=1, device_id={"tp": lax.rem(t + other, tps)}, device_id_type=MESH
        )
    pl.semaphore_signal(barrier, inc=1, device_id={"ctx": oc}, device_id_type=MESH)

    @pl.when(p > 0)
    def _():
        pl.semaphore_signal(barrier, inc=1, device_id={"pipe": p - 1}, device_id_type=MESH)

    @pl.when(p < pipes - 1)
    def _():
        pl.semaphore_signal(barrier, inc=1, device_id={"pipe": p + 1}, device_id_type=MESH)

    loads[0].wait()
    loads[1].wait()
    hf = h_ref[...].astype(F32)
    gain = gain_ref[...]
    hg = (hf * gain).astype(BF16)
    blocks[c, t] = hg
    squares = jnp.sum(hf * hf, axis=1, keepdims=True)
    squares_out[...] = jnp.broadcast_to(squares, (rows, 128)).T[0:8]
    squares_in[t] = squares_out[...]

    neighbours = (p > 0).astype(jnp.int32) + (p < pipes - 1).astype(jnp.int32)
    pl.semaphore_wait(barrier, tps + neighbours)

    def span(ch):
        return pl.ds(ch * step_rows, step_rows)

    def to_tp(b, ch, target, sem):
        ref = blocks.at[c, b, span(ch)]
        return pltpu.make_async_remote_copy(
            ref, ref, sem, z_recv.at[b, ch], device_id={"tp": target}, device_id_type=MESH
        )

    def to_ctx(b, ch):
        ref = blocks.at[c, b, span(ch)]
        j = lax.rem(b, half)
        return pltpu.make_async_remote_copy(
            ref,
            ref,
            across_sem.at[j, ch],
            x_recv.at[j, ch],
            device_id={"ctx": oc},
            device_id_type=MESH,
        )

    def send_right(d, ch, go=True):
        @pl.when((t - d >= 0) & (t < tps - 1))
        def _():
            copy = to_tp(t - d, ch, t + 1, right_sem.at[d, ch])
            copy.start() if go else copy.wait_send()

    def send_left(d, ch, go=True):
        @pl.when((t + d < tps) & (t > 0))
        def _():
            copy = to_tp(t + d, ch, t - 1, left_sem.at[d, ch])
            copy.start() if go else copy.wait_send()

    def send_across(b, ch):
        @pl.when((b >= 0) & (b < tps) & (b // half == oc))
        def _():
            to_ctx(b, ch).start()

    def own_sends(ch):
        send_right(0, ch)
        send_left(0, ch)
        send_across(t, ch)

    def forward(d, ch):
        @pl.when(t - d >= 0)
        def _():
            to_tp(t - d, ch, t, right_sem.at[0, ch]).wait_recv()

        send_right(d, ch)
        send_across(t - d, ch)

        @pl.when(t + d < tps)
        def _():
            to_tp(t + d, ch, t, left_sem.at[0, ch]).wait_recv()

        send_left(d, ch)
        send_across(t + d, ch)

    def gathered(out, into, ssem, rsem, k, mine):
        source = out.at[k] if len(out.shape) == 3 else out
        place = t if mine else k
        return pltpu.make_async_remote_copy(
            source,
            into.at[place],
            ssem.at[k],
            rsem.at[place],
            device_id={"tp": k},
            device_id_type=MESH,
        )

    def squares_copy(k, mine):
        return gathered(squares_out, squares_in, squares_ssem, squares_rsem, k, mine)

    def sums_copy(k, mine):
        return gathered(sums_out, sums_in, sums_ssem, sums_rsem, k, mine)

    peers = [lax.rem(t + other, tps) for other in range(1, tps)]
    for k in peers:
        squares_copy(k, True).start()
    own_sends(0)
    for k in peers:
        squares_copy(k, False).wait_recv()
    squares = squares_in[0]
    for k in range(1, tps):
        squares = squares + squares_in[k]
    r_row = lax.rsqrt(squares / D + 1e-05)
    r_wide = jnp.broadcast_to(r_row[0:1], (128, rows)).T
    xn = (hf * r_wide[:, 0:1] * gain).astype(BF16)
    xn_ref[...] = xn
    dt_at = 2 * n_state
    for load in loads[2:9]:
        load.wait()

    def against(w):
        return lax.dot_general(w, xn, (((1,), (1,)), ((), ())), preferred_element_type=F32)

    packed = jnp.concatenate([against(bc_ref[...]), against(dt_ref[...])], axis=0)
    for k in range(tps):
        dt_row = dt_at + k * heads
        sums_out[k] = jnp.concatenate([packed[:dt_at], packed[dt_row : dt_row + heads]], axis=0)
    sums_in[t] = sums_out[t]
    for k in peers:
        sums_copy(k, True).start()
    ids_row = ids_ref[...].astype(F32)
    info_out[0:8] = r_row
    info_out[8:16] = jnp.broadcast_to(ids_row, (8, rows))
    info_copy = pltpu.make_async_remote_copy(
        info_out,
        info_in,
        small_ssem.at[0],
        small_rsem.at[0],
        device_id={"ctx": oc},
        device_id_type=MESH,
    )
    info_copy.start()
    for ch in range(1, CHUNKS):
        own_sends(ch)
    for k in peers:
        sums_copy(k, False).wait_recv()

    total = sums_in[0]
    for k in range(1, tps):
        total = total + sums_in[k]
    maps = total[:dt_at]
    drive = total[dt_at : dt_at + heads] + column_of(bias_ref[...], heads)
    step = jnp.maximum(drive, 0.0) + jnp.log1p(jnp.exp(-jnp.abs(drive)))
    upper = (
        lax.broadcasted_iota(jnp.int32, (rows, rows), 0)
        <= lax.broadcasted_iota(jnp.int32, (rows, rows), 1)
    ).astype(F32)
    cum = exact(-step * column_of(rate_ref[...], heads), upper)
    cols = jnp.concatenate(
        [
            maps,
            cum,
            r_row,
            jnp.broadcast_to(ids_row, (8, rows)),
            step,
            jnp.zeros((128 - dt_at - 2 * heads - 16, rows), F32),
        ],
        axis=0,
    ).T
    cols_ref[...] = cols
    r_at = dt_at + heads
    ids_col = cols[:, r_at + 8 : r_at + 9]
    low = lax.broadcasted_iota(jnp.int32, (rows, rows), 0) > lax.broadcasted_iota(
        jnp.int32, (rows, rows), 1
    )
    allowed = (ids_col == ids_row) & low
    gram_ref[0] = jnp.where(allowed, exact(cols[:, n_state:dt_at], maps[:n_state]), 0.0)
    in_cols, out_cols = cols[:, :n_state], cols[:, n_state:dt_at]
    own_term = jnp.sum(in_cols * out_cols, axis=1, keepdims=True)
    direct_ref[...] = cols[:, r_at + 16 : r_at + 16 + heads] * own_term + skip_ref[...]
    gram_ref[1] = jnp.where(allowed, 0.0, -1e30)
    rows_ref[0:heads] = cum
    rows_ref[heads : 2 * heads] = step
    tail = (
        jnp.exp(cum[:, rows - 1 : rows] - cum)
        * jnp.where(ids_row == ids_row[:, rows - 1 : rows], 1.0, 0.0)
        * step
    )
    left_lanes = lax.broadcasted_iota(jnp.int32, (1, 2 * channels), 1) < channels
    for i in range(pairs):
        x_pair = xn_ref[:, i * 2 * channels : (i + 1) * 2 * channels]
        weights = jnp.concatenate(
            [maps[:n_state] * tail[2 * i + k : 2 * i + k + 1] for k in range(2)], axis=0
        ).astype(BF16)
        ends = dot(weights, x_pair)
        state_out[i] = jnp.where(left_lanes, ends[:n_state], ends[n_state:]).astype(BF16)
    state_copy = pltpu.make_async_remote_copy(
        state_out,
        state_in,
        small_ssem.at[1],
        small_rsem.at[1],
        device_id={"ctx": oc},
        device_id_type=MESH,
    )
    state_copy.start()

    def state_pair(i):
        x_pair = xn_ref[:, i * 2 * channels : (i + 1) * 2 * channels]
        outs, decays = [], []
        reach = jnp.where(
            (cols_ref[:, r_at + 8 : r_at + 9] == info_in[8:9, rows - 1 : rows]) & (c > 0), 1.0, 0.0
        )
        for head in (2 * i, 2 * i + 1):
            cum_col = cols_ref[:, dt_at + head : dt_at + head + 1]
            decay = jnp.exp(cum_col - rows_ref[head : head + 1] + gram_ref[1])
            mixed = decay * gram_ref[0] * rows_ref[heads + head : heads + head + 1]
            outs.append(dot(mixed.astype(BF16), x_pair))
            decays.append(jnp.exp(cum_col) * reach)
        skips = [direct_ref[:, 2 * i + k : 2 * i + k + 1] for k in range(2)]
        carried = dot(cols_ref[:, n_state:dt_at].astype(BF16), state_in[i])
        y = (
            jnp.where(left_lanes, outs[0], outs[1])
            + carried * jnp.where(left_lanes, decays[0], decays[1])
            + jnp.where(left_lanes, skips[0], skips[1]) * x_pair.astype(F32)
        )
        squared = y * y
        first = jnp.sum(jnp.where(left_lanes, squared, 0.0), axis=1, keepdims=True)
        second = jnp.sum(jnp.where(left_lanes, 0.0, squared), axis=1, keepdims=True)
        mean = jnp.where(left_lanes, first, second) / channels
        z = y * lax.rsqrt(mean + 1e-05)
        lanes = slice(i * 2 * channels, (i + 1) * 2 * channels)
        state_res[:, lanes] = (h_ref[:, lanes].astype(F32) + z).astype(BF16)

    near = jnp.clip(t, half * c, half * c + half - 1) - half * c
    far = half - 1 - near

    def weight_rows(j, column):
        return weight[pl.ds(pl.multiple_of(j * width, width), width), column : column + 256]

    def project_near(tok):
        x = blocks[tok, half * c + near]
        for column in range(0, all_cols, 256):
            sums_q[tok, :, column : column + 256] = dot(x, weight_rows(near, column))

    def part_copy(ch):
        return pltpu.make_async_remote_copy(
            part_out.at[span(ch)],
            part_in.at[span(ch)],
            part_ssem.at[0, ch],
            part_rsem.at[0, ch],
            device_id={"ctx": oc},
            device_id_type=MESH,
        )

    def kvpart_copy(ch):
        return pltpu.make_async_remote_copy(
            kvpart_out.at[span(ch)],
            kvpart_in.at[span(ch)],
            part_ssem.at[1, ch],
            part_rsem.at[1, ch],
            device_id={"ctx": oc},
            device_id_type=MESH,
        )

    def x_arrival(j, ch):
        ref = blocks.at[oc, half * c + j, span(ch)]
        return pltpu.make_async_remote_copy(
            ref,
            ref,
            across_sem.at[j, ch],
            x_recv.at[j, ch],
            device_id={"ctx": oc},
            device_id_type=MESH,
        )

    def project_far(ch):
        x_arrival(far, ch).wait_recv()
        block = half * c + far
        x = jnp.concatenate([blocks[oc, block, span(ch)], blocks[c, block, span(ch)]], axis=0)
        for column in (*range(q_cols, all_cols, 256), *range(0, q_cols, 256)):
            lanes = slice(column, column + 256)
            value = dot(x, weight_rows(far, column))
            theirs = value[:step_rows] + sums_q[oc, span(ch), lanes]
            ours = value[step_rows:] + sums_q[c, span(ch), lanes]
            part_out[span(ch), lanes] = theirs.astype(BF16)
            sums_q[c, span(ch), lanes] = ours
            if column >= q_cols:
                sums_q[oc, span(ch), lanes] = theirs
                kvpart_out[span(ch)] = ours.astype(BF16)
                kvpart_copy(ch).start()
        part_copy(ch).start()

    for ch in range(CHUNKS):
        forward(1, ch)
    info_copy.wait_recv()
    state_copy.wait_recv()
    for i in range(0, pairs // 4):
        state_pair(i)
    for ch in range(CHUNKS):
        forward(2, ch)
        for i in range(pairs // 4 + ch * pairs // 4, pairs // 4 + (ch + 1) * pairs // 4):
            if CHUNKS == 2:
                state_pair(i)
        if CHUNKS == 4:
            state_pair(pairs // 4 + ch)
    for load in loads[9:]:
        load.wait()
    project_near(c)
    rest = list(range(3 * pairs // 4 if CHUNKS != 4 else pairs // 4 + 4, pairs))
    for ch in range(CHUNKS):
        forward(3, ch)
        if ch == CHUNKS // 2 - 1:
            for j in range(CHUNKS):
                x_arrival(near, j).wait_recv()
            project_near(oc)
        if ch == 0:
            for i in rest:
                state_pair(i)
    for ch in range(CHUNKS):
        project_far(ch)

    r_col = cols_ref[:, r_at : r_at + 1]
    their_r = jnp.broadcast_to(info_in[0:1], (128, rows)).T[:, 0:1]
    for ch in range(CHUNKS):
        part_copy(ch).wait_recv()
        kvpart_copy(ch).wait_recv()
    ours = (sums_q[c] + part_in[...].astype(F32)) * r_col
    q_all[...] = ours[:, :q_cols].astype(BF16)
    kv_all[c] = ours[:, q_cols:].astype(BF16)
    kv_all[oc] = ((sums_q[oc, :, q_cols:] + kvpart_in[...].astype(F32)) * their_r).astype(BF16)

    key_pos = lax.broadcasted_iota(jnp.int32, (rows, 2 * rows), 1)
    query_pos = c * rows + lax.broadcasted_iota(jnp.int32, (rows, 2 * rows), 0)
    my_ids, their_ids = ids_row, info_in[8:9]
    at_first = jnp.where(c == 0, my_ids, their_ids)
    at_second = jnp.where(c == 0, their_ids, my_ids)
    key_ids = jnp.concatenate([at_first, at_second], axis=1)
    wanted = (key_pos <= query_pos) & (key_ids == cols_ref[:, r_at + 8 : r_at + 9])
    keys = kv_all[:, :, :HD].reshape(2 * rows, HD)
    values = kv_all[:, :, HD:].reshape(2 * rows, HD)
    attention = kind_ref[...] == 1
    per = prod.shape[2] // HD

    def pipe_copy(k):
        return pltpu.make_async_remote_copy(
            prod.at[k],
            prev.at[k],
            pipe_ssem.at[k],
            pipe_rsem.at[k],
            device_id={"pipe": p + 1},
            device_id_type=MESH,
        )

    for head in range(q_heads):
        lanes = slice(head * HD, (head + 1) * HD)
        scores = lax.dot_general(
            q_all[:, lanes], keys, (((1,), (1,)), ((), ())), preferred_element_type=F32
        ) * (HD ** (-0.5))
        scores = jnp.where(wanted, scores, -1e30)
        top = jnp.max(scores, axis=1, keepdims=True)
        probs = jnp.exp(scores - top)
        denom = jnp.sum(probs, axis=1, keepdims=True)
        mixed = (dot(probs.astype(BF16), values) / denom).astype(BF16)
        attended = (h_ref[:, lanes].astype(F32) + mixed.astype(F32)).astype(BF16)
        result = jnp.where(
            jnp.broadcast_to(attention, (rows, HD)),
            attended.astype(F32),
            state_res[:, lanes].astype(F32),
        ).astype(BF16)
        out_ref[:, lanes] = result
        inner = head % per
        prod[head // per, :, inner * HD : (inner + 1) * HD] = result
        if inner == per - 1:

            @pl.when(p < pipes - 1)
            def _(k=head // per):
                pipe_copy(k).start()

    for ch in range(CHUNKS):
        for d in range(tps):
            send_right(d, ch, False)
            send_left(d, ch, False)
        for j in range(half):
            to_ctx(half * oc + j, ch).wait_send()
        part_copy(ch).wait_send()
        kvpart_copy(ch).wait_send()
    for k in peers:
        squares_copy(k, True).wait_send()
        sums_copy(k, True).wait_send()
    info_copy.wait_send()
    state_copy.wait_send()

    span_p = prod.shape[2]

    @pl.when(p > 0)
    def _():
        for k in range(q_heads // per):
            pipe_copy(k).wait_recv()
            passed_ref[:, k * span_p : (k + 1) * span_p] = prev[k]

    @pl.when(p == 0)
    def _():
        passed_ref[...] = jnp.zeros(passed_ref.shape, BF16)

    @pl.when(p < pipes - 1)
    def _():
        for k in range(q_heads // per):
            pipe_copy(k).wait_send()


def fused(
    hidden_in,
    doc_ids,
    layer_kind,
    norm_gain,
    q_weight,
    k_weight,
    v_weight,
    bc_weight,
    dt_weight,
    dt_bias,
    decay_rate,
    skip_gain,
):
    _, rows, width = hidden_in.shape
    depth, q_cols = q_weight.shape[1:]
    kv_cols = k_weight.shape[2]
    heads = dt_bias.shape[1]
    n_state = bc_weight.shape[2] // 2
    tps = lax.axis_size("tp")
    vmem = pl.BlockSpec(memory_space=pltpu.VMEM)
    anywhere = pl.BlockSpec(memory_space=pl.ANY)
    small = 2 * n_state + heads
    dma = pltpu.SemaphoreType.DMA
    shape = jax.ShapeDtypeStruct((rows, width), BF16)
    out, passed = pl.pallas_call(
        kernel,
        out_shape=(shape, shape),
        in_specs=[anywhere] * 12,
        out_specs=(vmem, vmem),
        scratch_shapes=[
            pltpu.VMEM((rows, width), BF16),
            pltpu.VMEM((1, width), F32),
            pltpu.VMEM((2 * n_state, width), BF16),
            pltpu.VMEM((heads * tps, width), BF16),
            pltpu.VMEM((1, rows), jnp.int32),
            pltpu.VMEM((1, 1), jnp.int32),
            pltpu.VMEM((1, heads), F32),
            pltpu.VMEM((1, heads), F32),
            pltpu.VMEM((1, heads), F32),
            pltpu.VMEM((2, tps, rows, width), BF16),
            pltpu.VMEM((depth, q_cols + 2 * kv_cols), BF16),
            pltpu.VMEM((rows, width), BF16),
            pltpu.VMEM((8, rows), F32),
            pltpu.VMEM((tps, 8, rows), F32),
            pltpu.VMEM((tps, small, rows), F32),
            pltpu.VMEM((tps, small, rows), F32),
            pltpu.VMEM((16, rows), F32),
            pltpu.VMEM((16, rows), F32),
            pltpu.VMEM((heads // 2, n_state, 2 * width // heads), BF16),
            pltpu.VMEM((heads // 2, n_state, 2 * width // heads), BF16),
            pltpu.VMEM((rows, q_cols + 2 * kv_cols), BF16),
            pltpu.VMEM((rows, q_cols + 2 * kv_cols), BF16),
            pltpu.VMEM((rows, 2 * kv_cols), BF16),
            pltpu.VMEM((rows, 2 * kv_cols), BF16),
            pltpu.VMEM((2, rows, q_cols + 2 * kv_cols), F32),
            pltpu.VMEM((2, rows, 2 * kv_cols), BF16),
            pltpu.VMEM((rows, q_cols), BF16),
            pltpu.VMEM((rows, width), BF16),
            pltpu.VMEM((rows, 128), F32),
            pltpu.VMEM((2 * heads, rows), F32),
            pltpu.VMEM((rows, heads), F32),
            pltpu.VMEM((2, rows, rows), F32),
            pltpu.VMEM((4, rows, width // 4), BF16),
            pltpu.VMEM((4, rows, width // 4), BF16),
            dma((12,)),
            dma((tps, CHUNKS)),
            dma((tps, CHUNKS)),
            dma((tps // 2, CHUNKS)),
            dma((tps, CHUNKS)),
            dma((tps // 2, CHUNKS)),
            dma((tps,)),
            dma((tps,)),
            dma((tps,)),
            dma((tps,)),
            dma((2,)),
            dma((2,)),
            dma((2, CHUNKS)),
            dma((2, CHUNKS)),
            dma((4,)),
            dma((4,)),
        ],
        compiler_params=pltpu.CompilerParams(
            collective_id=0, has_side_effects=True, vmem_limit_bytes=60 * 2**20
        ),
        cost_estimate=pl.CostEstimate(
            flops=4 * rows * depth * (q_cols + 2 * kv_cols),
            bytes_accessed=2 * depth * (q_cols + 2 * kv_cols),
            transcendentals=0,
        ),
    )(
        hidden_in[0],
        norm_gain,
        bc_weight[0].T,
        dt_weight[0].T,
        doc_ids[None],
        layer_kind[None],
        dt_bias,
        decay_rate,
        skip_gain,
        q_weight[0],
        k_weight[0],
        v_weight[0],
    )
    return out[None], passed[None]


def solution(mesh):
    in_specs = (
        P("pipe", "ctx", "tp"),
        P("ctx"),
        P("pipe"),
        P("pipe", "tp"),
        P("pipe", "ctx", "tp"),
        P("pipe", "ctx", "tp"),
        P("pipe", "ctx", "tp"),
        P("pipe", "tp", None),
        P("pipe", "tp", None),
        P("pipe", "tp"),
        P("pipe", "tp"),
        P("pipe", "tp"),
    )
    out_specs = (P("pipe", "ctx", "tp"), P("pipe", "ctx", "tp"))
    body = fused if mesh.shape["ctx"] == 2 and mesh.shape["tp"] == 4 else shards
    return jax.shard_map(body, mesh=mesh, in_specs=in_specs, out_specs=out_specs, check_vma=False)
```

```python
import jax
import jax.numpy as jnp
from jax import lax
from jax.experimental import pallas as pl
from jax.experimental.pallas import tpu as pltpu
from jax.sharding import PartitionSpec as P

D = 4096
HD = 128


def entering(x, axis, combine, identity):
    devices, index = (lax.axis_size(axis), lax.axis_index(axis))
    everything = jax.tree.map(
        lambda part, kind: lax.all_gather(part.astype(kind), axis), x, (jnp.bfloat16, jnp.bfloat16)
    )
    start = jax.tree.map(
        lambda part, zero: jnp.broadcast_to(jnp.asarray(zero, part.dtype), part.shape), x, identity
    )

    def turn(k, before):
        reached = k < index
        new = combine(
            before, jax.tree.map(lambda part, own: part[k].astype(own.dtype), everything, x)
        )
        return jax.tree.map(lambda a, b: jnp.where(reached, a, b), new, before)

    return lax.fori_loop(0, devices, turn, start)


def passed_along(x, axis, by):
    devices = lax.axis_size(axis)
    pairs = [(i, i + by) for i in range(devices) if 0 <= i + by < devices]
    return lax.ppermute(x, axis, pairs)


def make_fold(q_rows, q_pos, q_ids, ids_all, groups, head_size, active):
    rows = q_rows.shape[0]
    gsize = rows // groups
    q_top = jnp.max(q_pos.reshape(groups, gsize), axis=1)
    scale = head_size ** (-0.5)

    def update(state, piece_k, piece_v, key_pos, key_ids):
        top, denom, total = state
        scores = (
            jnp.einsum("tkjd,skd->kjts", q_rows, piece_k, preferred_element_type=jnp.float32)
            * scale
        )
        allowed = (key_pos[None, :] <= q_pos[:, None]) & (key_ids[None, :] == q_ids[:, None])
        scores = jnp.where(allowed[None, None], scores, -1e30)
        new_top = jnp.maximum(top, jnp.max(scores, axis=-1))
        probs = jnp.where(allowed[None, None], jnp.exp(scores - new_top[..., None]), 0.0)
        factor = jnp.exp(top - new_top)
        denom = denom * factor + jnp.sum(probs, axis=-1)
        total = total * factor[..., None] + jnp.einsum(
            "kjts,skd->kjtd",
            probs.astype(jnp.bfloat16),
            piece_v,
            preferred_element_type=jnp.float32,
        )
        return (new_top, denom, total)

    def fold(carry, piece, start):
        piece_k, piece_v = piece
        count = piece_k.shape[0]
        block = 512 if count % 512 == 0 else count
        for offset in range(0, count, block):
            key_start = start + offset
            key_pos = key_start + jnp.arange(block)
            key_ids = lax.dynamic_slice_in_dim(ids_all, key_start, block)
            block_k = piece_k[offset : offset + block]
            block_v = piece_v[offset : offset + block]
            low = 0

            def compute(state, low=low):
                return update(state, block_k, block_v, key_pos, key_ids)

            wanted = jnp.logical_and(active, key_start <= q_top[0])
            updated = [lax.cond(wanted, compute, lambda state: state, carry[0])]
            carry = tuple(updated)
        return carry

    def initial(kv_count, group):
        return tuple(
            (
                (
                    jnp.full((kv_count, group, gsize), -1e30, jnp.float32),
                    jnp.zeros((kv_count, group, gsize), jnp.float32),
                    jnp.zeros((kv_count, group, gsize, head_size), jnp.float32),
                )
                for index in range(groups)
            )
        )

    def finish(carry):
        parts = [
            total / jnp.where(denom > 0.0, denom, 1.0)[..., None] for top, denom, total in carry
        ]
        joined = parts[0]
        kv_count, group = (joined.shape[0], joined.shape[1])
        return (
            jnp.transpose(joined, (2, 0, 1, 3))
            .reshape(rows, kv_count * group * head_size)
            .astype(jnp.bfloat16)
        )

    return (fold, initial, finish)


def shards(
    hidden_in,
    doc_ids,
    layer_kind,
    norm_gain,
    q_weight,
    k_weight,
    v_weight,
    bc_weight,
    dt_weight,
    dt_bias,
    decay_rate,
    skip_gain,
):
    current = hidden_in[0]
    rows, width = current.shape
    ctx_pos = lax.axis_index("ctx")
    tp_pos = lax.axis_index("tp")
    ids_all = lax.all_gather(doc_ids, "ctx", axis=0, tiled=True)
    first = ctx_pos * rows
    prev_id = jnp.where(
        ctx_pos > 0,
        lax.dynamic_index_in_dim(ids_all, jnp.maximum(first - 1, 0), 0, keepdims=False),
        -1,
    )
    gain = norm_gain[0]
    head_size = HD
    q_cols = q_weight.shape[2]
    kv_cols = k_weight.shape[2]
    heads_local = q_cols // head_size
    kv_local = kv_cols // head_size
    group = heads_local // kv_local
    is_attention = layer_kind[0] == 1
    hf = current.astype(jnp.float32)
    squares = lax.psum(jnp.sum(hf * hf, axis=1), "tp")
    xn = (hf * lax.rsqrt(squares / D + 1e-05)[:, None] * gain[None, :]).astype(jnp.bfloat16)
    whole = lax.all_gather(xn, "tp", axis=1, tiled=True)
    empty = (
        jnp.zeros((rows, q_cols), jnp.float32),
        jnp.zeros((rows, kv_cols), jnp.float32),
        jnp.zeros((rows, kv_cols), jnp.float32),
    )
    pieces = (
        lax.all_gather(q_weight[0], "ctx", axis=0, tiled=True),
        lax.all_gather(k_weight[0], "ctx", axis=0, tiled=True),
        lax.all_gather(v_weight[0], "ctx", axis=0, tiled=True),
    )

    def really(values):
        return tuple(
            (jnp.dot(whole, piece, preferred_element_type=jnp.float32) for piece in pieces)
        )

    q_sum, k_sum, v_sum = lax.cond(is_attention, really, lambda values: values, empty)
    query = q_sum.astype(jnp.bfloat16).reshape(rows, kv_local, group, head_size)
    keys = k_sum.astype(jnp.bfloat16).reshape(rows, kv_local, head_size)
    values = v_sum.astype(jnp.bfloat16).reshape(rows, kv_local, head_size)
    q_pos = first + jnp.arange(rows)
    fold, initial, finish = make_fold(query, q_pos, doc_ids, ids_all, 1, head_size, is_attention)
    carry = fold(
        initial(kv_local, group),
        (
            lax.all_gather(keys, "ctx", axis=0, tiled=True),
            lax.all_gather(values, "ctx", axis=0, tiled=True),
        ),
        jnp.int32(0),
    )
    attended = finish(carry)
    attention_result = (current.astype(jnp.float32) + attended.astype(jnp.float32)).astype(
        jnp.bfloat16
    )
    ssm_local = dt_bias.shape[1]
    channels = width // ssm_local
    inputs = xn.astype(jnp.float32).reshape(rows, ssm_local, channels)
    maps, step_all = lax.psum(
        (
            jnp.dot(xn, bc_weight[0], preferred_element_type=jnp.float32),
            jnp.dot(xn, dt_weight[0], preferred_element_type=jnp.float32),
        ),
        "tp",
    )
    step = jax.nn.softplus(
        lax.dynamic_slice_in_dim(step_all, tp_pos * ssm_local, ssm_local, 1) + dt_bias[0][None, :]
    )
    state_size = maps.shape[1] // 2
    in_map = maps[:, :state_size]
    out_map = maps[:, state_size:]
    cumulative = jnp.cumsum(-step * decay_rate[0][None, :], axis=0)
    order = jnp.arange(rows)
    pairs = (doc_ids[:, None] == doc_ids[None, :]) & (order[:, None] >= order[None, :])
    exponent = jnp.where(
        pairs[:, :, None], cumulative[:, None, :] - cumulative[None, :, :], -jnp.inf
    )
    intersection = jnp.dot(out_map, in_map.T, precision=lax.Precision.HIGHEST)
    weighted = inputs * step[:, :, None]
    inner = jnp.einsum(
        "tsh,shp->thp",
        jnp.exp(exponent) * intersection[:, :, None],
        weighted,
        precision=lax.Precision.HIGHEST,
    )
    end_weight = (
        jnp.exp(cumulative[-1][None, :] - cumulative)
        * (doc_ids == doc_ids[-1]).astype(jnp.float32)[:, None]
    )
    end_state = jnp.einsum(
        "sh,sn,shp->hnp", end_weight, in_map, weighted, precision=lax.Precision.HIGHEST
    )
    total_decay = jnp.exp(cumulative[-1]) * (doc_ids[-1] == prev_id).astype(jnp.float32)

    def combine(earlier, later):
        return (earlier[0] * later[0], earlier[1] * later[0][:, None, None] + later[1])

    identity = (jnp.ones_like(total_decay), jnp.zeros_like(end_state))
    incoming = entering((total_decay, end_state), "ctx", combine, identity)[1]
    reach = jnp.exp(cumulative) * (doc_ids == prev_id).astype(jnp.float32)[:, None]
    carried = (
        jnp.einsum("tn,hnp->thp", out_map, incoming, precision=lax.Precision.HIGHEST)
        * reach[:, :, None]
    )
    outputs = inner + carried + skip_gain[0][None, :, None] * inputs
    outputs = outputs * lax.rsqrt(jnp.mean(outputs * outputs, axis=2, keepdims=True) + 1e-05)
    state_result = (current.astype(jnp.float32) + outputs.reshape(rows, width)).astype(jnp.bfloat16)
    produced = jnp.where(is_attention, attention_result, state_result)
    moved = passed_along(produced, "pipe", 1)
    return (produced[None], moved[None])


CHUNKS = 2
MESH = pl.DeviceIdType.MESH
F32 = jnp.float32
BF16 = jnp.bfloat16


def dot(a, b):
    return jnp.dot(a, b, preferred_element_type=F32)


def exact(a, b):
    return jnp.dot(a, b, preferred_element_type=F32, precision=lax.Precision.HIGHEST)


def column_of(row, count):
    same = lax.broadcasted_iota(jnp.int32, (count, count), 0) == lax.broadcasted_iota(
        jnp.int32, (count, count), 1
    )
    return jnp.sum(jnp.where(same, row, 0.0), axis=1, keepdims=True)


def kernel(
    h_hbm,
    gain_hbm,
    bc_hbm,
    dt_hbm,
    ids_hbm,
    kind_hbm,
    bias_hbm,
    rate_hbm,
    skip_hbm,
    q_hbm,
    k_hbm,
    v_hbm,
    out_hbm,
    passed_hbm,
    h_ref,
    gain_ref,
    bc_ref,
    dt_ref,
    ids_ref,
    kind_ref,
    bias_ref,
    rate_ref,
    skip_ref,
    blocks,
    weight,
    xn_ref,
    squares_out,
    squares_in,
    sums_out,
    sums_in,
    info_out,
    info_in,
    state_out,
    state_in,
    part_out,
    part_in,
    kvpart_out,
    kvpart_in,
    sums_q,
    kv_all,
    q_all,
    state_res,
    cols_ref,
    rows_ref,
    direct_ref,
    gram_ref,
    prod,
    prev,
    w_sem,
    ahead_sem,
    behind_sem,
    across_sem,
    b_recv,
    squares_ssem,
    squares_rsem,
    sums_ssem,
    sums_rsem,
    small_ssem,
    small_rsem,
    part_ssem,
    part_rsem,
    kvpart_sem,
    pipe_ssem,
    pipe_rsem,
    out_sem,
):
    p, c, t = lax.axis_index("pipe"), lax.axis_index("ctx"), lax.axis_index("tp")
    pipes, tps = lax.axis_size("pipe"), lax.axis_size("tp")
    oc = 1 - c
    rows, width = h_ref.shape
    step_rows = rows // CHUNKS
    heads = bias_ref.shape[1]
    pairs = heads // 2
    channels = width // heads
    n_state = bc_ref.shape[0] // 2
    half = tps // 2
    q_cols = q_hbm.shape[1]
    kv_cols = k_hbm.shape[1]
    all_cols = q_cols + 2 * kv_cols
    q_heads = q_cols // HD

    pairs_in = [
        (h_hbm, h_ref),
        (gain_hbm, gain_ref),
        (bc_hbm, bc_ref),
        (dt_hbm, dt_ref),
        (ids_hbm, ids_ref),
        (kind_hbm, kind_ref),
        (bias_hbm, bias_ref),
        (rate_hbm, rate_ref),
        (skip_hbm, skip_ref),
        (q_hbm, weight.at[:, pl.ds(0, q_cols)]),
        (k_hbm, weight.at[:, pl.ds(q_cols, kv_cols)]),
        (v_hbm, weight.at[:, pl.ds(q_cols + kv_cols, kv_cols)]),
    ]
    loads = [
        pltpu.make_async_copy(source, into, w_sem.at[n])
        for n, (source, into) in enumerate(pairs_in)
    ]
    for load in loads:
        load.start()

    barrier = pltpu.get_barrier_semaphore()
    for other in range(1, tps):
        pl.semaphore_signal(
            barrier, inc=1, device_id={"tp": lax.rem(t + other, tps)}, device_id_type=MESH
        )
    pl.semaphore_signal(barrier, inc=1, device_id={"ctx": oc}, device_id_type=MESH)

    @pl.when(p > 0)
    def _():
        pl.semaphore_signal(barrier, inc=1, device_id={"pipe": p - 1}, device_id_type=MESH)

    @pl.when(p < pipes - 1)
    def _():
        pl.semaphore_signal(barrier, inc=1, device_id={"pipe": p + 1}, device_id_type=MESH)

    loads[0].wait()
    loads[1].wait()
    hf = h_ref[...].astype(F32)
    gain = gain_ref[...]
    hg = (hf * gain).astype(BF16)
    blocks[c, t] = hg
    squares = jnp.sum(hf * hf, axis=1, keepdims=True)
    squares_out[...] = jnp.broadcast_to(squares, (rows, 128)).T[0:8]
    squares_in[t] = squares_out[...]

    neighbours = (p > 0).astype(jnp.int32) + (p < pipes - 1).astype(jnp.int32)
    pl.semaphore_wait(barrier, tps + neighbours)

    def span(ch):
        return pl.ds(ch * step_rows, step_rows)

    turn = 1 - 2 * c
    place = c * (tps - 1) + t * turn

    def block_at(kind, e):
        return (c if kind == "O" else oc), c * (tps - 1) + e * turn

    def block_copy(item, ch, sem, device):
        tok, b = block_at(*item)
        ref = blocks.at[tok, b, span(ch)]
        return pltpu.make_async_remote_copy(
            ref, ref, sem, b_recv.at[tok, b, ch], device_id=device, device_id_type=MESH
        )

    O0, O1, O2, O3, F0, F1 = ("O", 0), ("O", 1), ("O", 2), ("O", 3), ("F", 0), ("F", 1)
    ahead, behind = (O0, O1, F0), (O1, O2, F1)

    def ahead_copy(item, ch):
        return block_copy(item, ch, ahead_sem.at[ahead.index(item), ch], {"tp": t + turn})

    def behind_copy(item, ch):
        return block_copy(item, ch, behind_sem.at[behind.index(item), ch], {"tp": t - turn})

    def across_copy(item, ch):
        return block_copy(item, ch, across_sem.at[ch], {"ctx": oc})

    def own_sends(ch):
        @pl.when(place == 0)
        def _():
            ahead_copy(O0, ch).start()

        @pl.when(place == 1)
        def _():
            behind_copy(O1, ch).start()
            ahead_copy(O1, ch).start()

        @pl.when(place == 2)
        def _():
            across_copy(O2, ch).start()
            behind_copy(O2, ch).start()

        @pl.when(place == 3)
        def _():
            across_copy(O3, ch).start()

    def arrive(item, at, ch, then=()):
        @pl.when(place == at)
        def _():
            block_copy(item, ch, across_sem.at[ch], {"ctx": oc}).wait_recv()
            for onward in then:
                onward(item, ch).start()

    def gathered(out, into, ssem, rsem, k, mine):
        source = out.at[k] if len(out.shape) == 3 else out
        place = t if mine else k
        return pltpu.make_async_remote_copy(
            source,
            into.at[place],
            ssem.at[k],
            rsem.at[place],
            device_id={"tp": k},
            device_id_type=MESH,
        )

    def squares_copy(k, mine):
        return gathered(squares_out, squares_in, squares_ssem, squares_rsem, k, mine)

    def sums_copy(k, mine):
        return gathered(sums_out, sums_in, sums_ssem, sums_rsem, k, mine)

    peers = [lax.rem(t + other, tps) for other in range(1, tps)]
    for k in peers:
        squares_copy(k, True).start()
    own_sends(0)
    for k in peers:
        squares_copy(k, False).wait_recv()
    squares = squares_in[0]
    for k in range(1, tps):
        squares = squares + squares_in[k]
    r_row = lax.rsqrt(squares / D + 1e-05)
    r_wide = jnp.broadcast_to(r_row[0:1], (128, rows)).T
    xn = (hf * r_wide[:, 0:1] * gain).astype(BF16)
    xn_ref[...] = xn
    dt_at = 2 * n_state
    for load in loads[2:9]:
        load.wait()

    def against(w):
        return lax.dot_general(w, xn, (((1,), (1,)), ((), ())), preferred_element_type=F32)

    packed = jnp.concatenate([against(bc_ref[...]), against(dt_ref[...])], axis=0)
    for k in range(tps):
        dt_row = dt_at + k * heads
        sums_out[k] = jnp.concatenate([packed[:dt_at], packed[dt_row : dt_row + heads]], axis=0)
    sums_in[t] = sums_out[t]
    for k in peers:
        sums_copy(k, True).start()
    ids_row = ids_ref[...].astype(F32)
    info_out[0:8] = r_row
    info_out[8:16] = jnp.broadcast_to(ids_row, (8, rows))
    info_copy = pltpu.make_async_remote_copy(
        info_out,
        info_in,
        small_ssem.at[0],
        small_rsem.at[0],
        device_id={"ctx": oc},
        device_id_type=MESH,
    )
    info_copy.start()
    for ch in range(1, CHUNKS):
        own_sends(ch)
    for k in peers:
        sums_copy(k, False).wait_recv()

    total = sums_in[0]
    for k in range(1, tps):
        total = total + sums_in[k]
    maps = total[:dt_at]
    drive = total[dt_at : dt_at + heads] + column_of(bias_ref[...], heads)
    step = jnp.maximum(drive, 0.0) + jnp.log1p(jnp.exp(-jnp.abs(drive)))
    upper = (
        lax.broadcasted_iota(jnp.int32, (rows, rows), 0)
        <= lax.broadcasted_iota(jnp.int32, (rows, rows), 1)
    ).astype(F32)
    cum = exact(-step * column_of(rate_ref[...], heads), upper)
    cols = jnp.concatenate(
        [
            maps,
            cum,
            r_row,
            jnp.broadcast_to(ids_row, (8, rows)),
            step,
            jnp.zeros((128 - dt_at - 2 * heads - 16, rows), F32),
        ],
        axis=0,
    ).T
    cols_ref[...] = cols
    r_at = dt_at + heads
    ids_col = cols[:, r_at + 8 : r_at + 9]
    low = lax.broadcasted_iota(jnp.int32, (rows, rows), 0) > lax.broadcasted_iota(
        jnp.int32, (rows, rows), 1
    )
    allowed = (ids_col == ids_row) & low
    gram_ref[0] = jnp.where(allowed, exact(cols[:, n_state:dt_at], maps[:n_state]), 0.0)
    in_cols, out_cols = cols[:, :n_state], cols[:, n_state:dt_at]
    own_term = jnp.sum(in_cols * out_cols, axis=1, keepdims=True)
    direct_ref[...] = cols[:, r_at + 16 : r_at + 16 + heads] * own_term + skip_ref[...]
    gram_ref[1] = jnp.where(allowed, 0.0, -1e30)
    rows_ref[0:heads] = cum
    rows_ref[heads : 2 * heads] = step
    tail = (
        jnp.exp(cum[:, rows - 1 : rows] - cum)
        * jnp.where(ids_row == ids_row[:, rows - 1 : rows], 1.0, 0.0)
        * step
    )
    left_lanes = lax.broadcasted_iota(jnp.int32, (1, 2 * channels), 1) < channels
    for i in range(pairs):
        x_pair = xn_ref[:, i * 2 * channels : (i + 1) * 2 * channels]
        weights = jnp.concatenate(
            [maps[:n_state] * tail[2 * i + k : 2 * i + k + 1] for k in range(2)], axis=0
        ).astype(BF16)
        ends = dot(weights, x_pair)
        state_out[i] = jnp.where(left_lanes, ends[:n_state], ends[n_state:]).astype(BF16)
    state_copy = pltpu.make_async_remote_copy(
        state_out,
        state_in,
        small_ssem.at[1],
        small_rsem.at[1],
        device_id={"ctx": oc},
        device_id_type=MESH,
    )
    state_copy.start()

    def state_pair(i):
        x_pair = xn_ref[:, i * 2 * channels : (i + 1) * 2 * channels]
        outs, decays = [], []
        reach = jnp.where(
            (cols_ref[:, r_at + 8 : r_at + 9] == info_in[8:9, rows - 1 : rows]) & (c > 0), 1.0, 0.0
        )
        for head in (2 * i, 2 * i + 1):
            cum_col = cols_ref[:, dt_at + head : dt_at + head + 1]
            decay = jnp.exp(cum_col - rows_ref[head : head + 1] + gram_ref[1])
            mixed = decay * gram_ref[0] * rows_ref[heads + head : heads + head + 1]
            outs.append(dot(mixed.astype(BF16), x_pair))
            decays.append(jnp.exp(cum_col) * reach)
        skips = [direct_ref[:, 2 * i + k : 2 * i + k + 1] for k in range(2)]
        carried = dot(cols_ref[:, n_state:dt_at].astype(BF16), state_in[i])
        y = (
            jnp.where(left_lanes, outs[0], outs[1])
            + carried * jnp.where(left_lanes, decays[0], decays[1])
            + jnp.where(left_lanes, skips[0], skips[1]) * x_pair.astype(F32)
        )
        squared = y * y
        first = jnp.sum(jnp.where(left_lanes, squared, 0.0), axis=1, keepdims=True)
        second = jnp.sum(jnp.where(left_lanes, 0.0, squared), axis=1, keepdims=True)
        mean = jnp.where(left_lanes, first, second) / channels
        z = y * lax.rsqrt(mean + 1e-05)
        lanes = slice(i * 2 * channels, (i + 1) * 2 * channels)
        state_res[:, lanes] = (h_ref[:, lanes].astype(F32) + z).astype(BF16)

    first_half = half * c

    def project(x, j, column):
        depth = slice(j * width, (j + 1) * width)
        return dot(x, weight[depth, column : column + 256])

    def project_ours():
        x = [blocks[c, first_half + j] for j in range(half)]
        for column in (*range(q_cols, all_cols, 256), *range(0, q_cols, 256)):
            value = sum([project(x[j], j, column) for j in range(1, half)], project(x[0], 0, column))
            sums_q[c, :, column : column + 256] = value
            if column == q_cols:
                kvpart_out[...] = value.astype(BF16)
                kvpart_copy().start()

    def part_copy(ch):
        return pltpu.make_async_remote_copy(
            part_out.at[span(ch)],
            part_in.at[span(ch)],
            part_ssem.at[ch],
            part_rsem.at[ch],
            device_id={"ctx": oc},
            device_id_type=MESH,
        )

    def kvpart_copy():
        return pltpu.make_async_remote_copy(
            kvpart_out,
            kvpart_in,
            kvpart_sem.at[0],
            kvpart_sem.at[1],
            device_id={"ctx": oc},
            device_id_type=MESH,
        )

    def project_theirs(ch):
        x = [blocks[oc, first_half + j, span(ch)] for j in range(half)]
        for column in range(0, all_cols, 256):
            value = sum([project(x[j], j, column) for j in range(1, half)], project(x[0], 0, column))
            part_out[span(ch), column : column + 256] = value.astype(BF16)
            if column == q_cols:
                sums_q[oc, span(ch), column : column + 256] = value
        part_copy(ch).start()

    for ch in range(CHUNKS):
        arrive(F0, 0, ch, (ahead_copy,))
        arrive(F1, 1, ch, (behind_copy,))
        arrive(O2, 1, ch, (behind_copy, across_copy))
        arrive(O0, 1, ch, (ahead_copy,))
        arrive(O1, 2, ch, (ahead_copy,))
        arrive(O1, 0, ch)
    info_copy.wait_recv()
    state_copy.wait_recv()
    for i in range(0, pairs // 4):
        state_pair(i)
    for ch in range(CHUNKS):
        arrive(O2, 0, ch, (across_copy,))
        arrive(F0, 1, ch, (ahead_copy,))
        arrive(O0, 2, ch, (ahead_copy,))
        arrive(O1, 3, ch)
        for i in range(pairs // 4 * (CHUNKS + ch) // CHUNKS, pairs // 4 * (CHUNKS + ch + 1) // CHUNKS):
            state_pair(i)
    for load in loads[9:]:
        load.wait()
    for ch in range(CHUNKS):
        arrive(F0, 2, ch, (ahead_copy,))
        arrive(O0, 3, ch)
        for i in range(pairs // 2 * (CHUNKS + ch) // CHUNKS, pairs // 2 * (CHUNKS + ch + 1) // CHUNKS):
            state_pair(i)
    project_ours()
    for ch in range(CHUNKS):
        arrive(F1, 0, ch)
        arrive(F1, 2, ch)
        arrive(F1, 3, ch)
        arrive(F0, 3, ch)
        project_theirs(ch)

    r_col = cols_ref[:, r_at : r_at + 1]
    kvpart_copy().wait_recv()
    their_r = jnp.broadcast_to(info_in[0:1], (128, rows)).T[:, 0:1]
    for ch in range(CHUNKS):
        part_copy(ch).wait_recv()
    ours = (sums_q[c] + part_in[...].astype(F32)) * r_col
    q_all[...] = ours[:, :q_cols].astype(BF16)
    kv_all[c] = ours[:, q_cols:].astype(BF16)
    kv_all[oc] = ((sums_q[oc, :, q_cols:] + kvpart_in[...].astype(F32)) * their_r).astype(BF16)

    key_pos = lax.broadcasted_iota(jnp.int32, (rows, 2 * rows), 1)
    query_pos = c * rows + lax.broadcasted_iota(jnp.int32, (rows, 2 * rows), 0)
    my_ids, their_ids = ids_row, info_in[8:9]
    at_first = jnp.where(c == 0, my_ids, their_ids)
    at_second = jnp.where(c == 0, their_ids, my_ids)
    key_ids = jnp.concatenate([at_first, at_second], axis=1)
    wanted = (key_pos <= query_pos) & (key_ids == cols_ref[:, r_at + 8 : r_at + 9])
    keys = kv_all[:, :, :HD].reshape(2 * rows, HD)
    values = kv_all[:, :, HD:].reshape(2 * rows, HD)
    attention = kind_ref[...] == 1
    per = prod.shape[2] // HD

    def pipe_copy(k):
        return pltpu.make_async_remote_copy(
            prod.at[k],
            prev.at[k],
            pipe_ssem.at[k],
            pipe_rsem.at[k],
            device_id={"pipe": p + 1},
            device_id_type=MESH,
        )

    span_p = prod.shape[2]

    def out_copy(k):
        lanes = pl.ds(k * span_p, span_p)
        return pltpu.make_async_copy(prod.at[k], out_hbm.at[:, lanes], out_sem.at[0, k])

    def passed_copy(k):
        lanes = pl.ds(k * span_p, span_p)
        return pltpu.make_async_copy(prev.at[k], passed_hbm.at[:, lanes], out_sem.at[1, k])

    for head in range(q_heads):
        lanes = slice(head * HD, (head + 1) * HD)
        scores = lax.dot_general(
            q_all[:, lanes], keys, (((1,), (1,)), ((), ())), preferred_element_type=F32
        ) * (HD ** (-0.5))
        scores = jnp.where(wanted, scores, -1e30)
        top = jnp.max(scores, axis=1, keepdims=True)
        probs = jnp.exp(scores - top)
        denom = jnp.sum(probs, axis=1, keepdims=True)
        mixed = (dot(probs.astype(BF16), values) / denom).astype(BF16)
        attended = (h_ref[:, lanes].astype(F32) + mixed.astype(F32)).astype(BF16)
        result = jnp.where(
            jnp.broadcast_to(attention, (rows, HD)),
            attended.astype(F32),
            state_res[:, lanes].astype(F32),
        ).astype(BF16)
        inner = head % per
        prod[head // per, :, inner * HD : (inner + 1) * HD] = result
        if inner == per - 1:
            out_copy(head // per).start()

            @pl.when(p < pipes - 1)
            def _(k=head // per):
                pipe_copy(k).start()

    for ch in range(CHUNKS):
        across_copy(O2, ch).wait_send()

        @pl.when(place < 3)
        def _(ch=ch):
            ahead_copy(F0, ch).wait_send()
            ahead_copy(O0, ch).wait_send()

        @pl.when((place == 1) | (place == 2))
        def _(ch=ch):
            ahead_copy(O1, ch).wait_send()
            behind_copy(O2, ch).wait_send()

        @pl.when(place == 1)
        def _(ch=ch):
            behind_copy(O1, ch).wait_send()
            behind_copy(F1, ch).wait_send()

        part_copy(ch).wait_send()
    kvpart_copy().wait_send()
    for k in peers:
        squares_copy(k, True).wait_send()
        sums_copy(k, True).wait_send()
    info_copy.wait_send()
    state_copy.wait_send()

    @pl.when(p == 0)
    def _():
        prev[...] = jnp.zeros(prev.shape, BF16)

    for k in range(q_heads // per):

        @pl.when(p > 0)
        def _(k=k):
            pipe_copy(k).wait_recv()

        passed_copy(k).start()
    for k in range(q_heads // per):
        out_copy(k).wait()
        passed_copy(k).wait()

    @pl.when(p < pipes - 1)
    def _():
        for k in range(q_heads // per):
            pipe_copy(k).wait_send()


def deliver(out_from, passed_from, out_to, passed_to, sem):
    copies = [
        pltpu.make_async_copy(out_from, out_to, sem.at[0]),
        pltpu.make_async_copy(passed_from, passed_to, sem.at[1]),
    ]
    for copy in copies:
        copy.start()
    for copy in copies:
        copy.wait()


def fused(
    hidden_in,
    doc_ids,
    layer_kind,
    norm_gain,
    q_weight,
    k_weight,
    v_weight,
    bc_weight,
    dt_weight,
    dt_bias,
    decay_rate,
    skip_gain,
):
    _, rows, width = hidden_in.shape
    depth, q_cols = q_weight.shape[1:]
    kv_cols = k_weight.shape[2]
    heads = dt_bias.shape[1]
    n_state = bc_weight.shape[2] // 2
    tps = lax.axis_size("tp")
    anywhere = pl.BlockSpec(memory_space=pl.ANY)
    small = 2 * n_state + heads
    dma = pltpu.SemaphoreType.DMA
    shape = jax.ShapeDtypeStruct((rows, width), BF16)
    out, passed = pl.pallas_call(
        kernel,
        out_shape=(shape, shape),
        in_specs=[anywhere] * 12,
        out_specs=(anywhere, anywhere),
        scratch_shapes=[
            pltpu.VMEM((rows, width), BF16),
            pltpu.VMEM((1, width), F32),
            pltpu.VMEM((2 * n_state, width), BF16),
            pltpu.VMEM((heads * tps, width), BF16),
            pltpu.VMEM((1, rows), jnp.int32),
            pltpu.VMEM((1, 1), jnp.int32),
            pltpu.VMEM((1, heads), F32),
            pltpu.VMEM((1, heads), F32),
            pltpu.VMEM((1, heads), F32),
            pltpu.VMEM((2, tps, rows, width), BF16),
            pltpu.VMEM((depth, q_cols + 2 * kv_cols), BF16),
            pltpu.VMEM((rows, width), BF16),
            pltpu.VMEM((8, rows), F32),
            pltpu.VMEM((tps, 8, rows), F32),
            pltpu.VMEM((tps, small, rows), F32),
            pltpu.VMEM((tps, small, rows), F32),
            pltpu.VMEM((16, rows), F32),
            pltpu.VMEM((16, rows), F32),
            pltpu.VMEM((heads // 2, n_state, 2 * width // heads), BF16),
            pltpu.VMEM((heads // 2, n_state, 2 * width // heads), BF16),
            pltpu.VMEM((rows, q_cols + 2 * kv_cols), BF16),
            pltpu.VMEM((rows, q_cols + 2 * kv_cols), BF16),
            pltpu.VMEM((rows, 2 * kv_cols), BF16),
            pltpu.VMEM((rows, 2 * kv_cols), BF16),
            pltpu.VMEM((2, rows, q_cols + 2 * kv_cols), F32),
            pltpu.VMEM((2, rows, 2 * kv_cols), BF16),
            pltpu.VMEM((rows, q_cols), BF16),
            pltpu.VMEM((rows, width), BF16),
            pltpu.VMEM((rows, 128), F32),
            pltpu.VMEM((2 * heads, rows), F32),
            pltpu.VMEM((rows, heads), F32),
            pltpu.VMEM((2, rows, rows), F32),
            pltpu.VMEM((4, rows, width // 4), BF16),
            pltpu.VMEM((4, rows, width // 4), BF16),
            dma((12,)),
            dma((3, CHUNKS)),
            dma((3, CHUNKS)),
            dma((CHUNKS,)),
            dma((2, tps, CHUNKS)),
            dma((tps,)),
            dma((tps,)),
            dma((tps,)),
            dma((tps,)),
            dma((2,)),
            dma((2,)),
            dma((CHUNKS,)),
            dma((CHUNKS,)),
            dma((2,)),
            dma((4,)),
            dma((4,)),
            dma((2, 4)),
        ],
        compiler_params=pltpu.CompilerParams(
            collective_id=0, has_side_effects=True, vmem_limit_bytes=60 * 2**20
        ),
        cost_estimate=pl.CostEstimate(
            flops=4 * rows * depth * (q_cols + 2 * kv_cols),
            bytes_accessed=2 * depth * (q_cols + 2 * kv_cols),
            transcendentals=0,
        ),
    )(
        hidden_in[0],
        norm_gain,
        bc_weight[0].T,
        dt_weight[0].T,
        doc_ids[None],
        layer_kind[None],
        dt_bias,
        decay_rate,
        skip_gain,
        q_weight[0],
        k_weight[0],
        v_weight[0],
    )
    out, passed = pl.pallas_call(
        deliver,
        out_shape=(shape, shape),
        in_specs=[anywhere] * 2,
        out_specs=(anywhere, anywhere),
        scratch_shapes=[dma((2,))],
    )(out, passed)
    return out[None], passed[None]


def solution(mesh):
    in_specs = (
        P("pipe", "ctx", "tp"),
        P("ctx"),
        P("pipe"),
        P("pipe", "tp"),
        P("pipe", "ctx", "tp"),
        P("pipe", "ctx", "tp"),
        P("pipe", "ctx", "tp"),
        P("pipe", "tp", None),
        P("pipe", "tp", None),
        P("pipe", "tp"),
        P("pipe", "tp"),
        P("pipe", "tp"),
    )
    out_specs = (P("pipe", "ctx", "tp"), P("pipe", "ctx", "tp"))
    body = fused if mesh.shape["ctx"] == 2 and mesh.shape["tp"] == 4 else shards
    return jax.shard_map(body, mesh=mesh, in_specs=in_specs, out_specs=out_specs, check_vma=False)
```

```python
import jax
import jax.numpy as jnp
from jax import lax
from jax.experimental import pallas as pl
from jax.experimental.pallas import tpu as pltpu
from jax.sharding import PartitionSpec as P

D = 4096
HD = 128


def entering(x, axis, combine, identity):
    devices, index = (lax.axis_size(axis), lax.axis_index(axis))
    everything = jax.tree.map(
        lambda part, kind: lax.all_gather(part.astype(kind), axis), x, (jnp.bfloat16, jnp.bfloat16)
    )
    start = jax.tree.map(
        lambda part, zero: jnp.broadcast_to(jnp.asarray(zero, part.dtype), part.shape), x, identity
    )

    def turn(k, before):
        reached = k < index
        new = combine(
            before, jax.tree.map(lambda part, own: part[k].astype(own.dtype), everything, x)
        )
        return jax.tree.map(lambda a, b: jnp.where(reached, a, b), new, before)

    return lax.fori_loop(0, devices, turn, start)


def passed_along(x, axis, by):
    devices = lax.axis_size(axis)
    pairs = [(i, i + by) for i in range(devices) if 0 <= i + by < devices]
    return lax.ppermute(x, axis, pairs)


def make_fold(q_rows, q_pos, q_ids, ids_all, groups, head_size, active):
    rows = q_rows.shape[0]
    gsize = rows // groups
    q_top = jnp.max(q_pos.reshape(groups, gsize), axis=1)
    scale = head_size ** (-0.5)

    def update(state, piece_k, piece_v, key_pos, key_ids):
        top, denom, total = state
        scores = (
            jnp.einsum("tkjd,skd->kjts", q_rows, piece_k, preferred_element_type=jnp.float32)
            * scale
        )
        allowed = (key_pos[None, :] <= q_pos[:, None]) & (key_ids[None, :] == q_ids[:, None])
        scores = jnp.where(allowed[None, None], scores, -1e30)
        new_top = jnp.maximum(top, jnp.max(scores, axis=-1))
        probs = jnp.where(allowed[None, None], jnp.exp(scores - new_top[..., None]), 0.0)
        factor = jnp.exp(top - new_top)
        denom = denom * factor + jnp.sum(probs, axis=-1)
        total = total * factor[..., None] + jnp.einsum(
            "kjts,skd->kjtd",
            probs.astype(jnp.bfloat16),
            piece_v,
            preferred_element_type=jnp.float32,
        )
        return (new_top, denom, total)

    def fold(carry, piece, start):
        piece_k, piece_v = piece
        count = piece_k.shape[0]
        block = 512 if count % 512 == 0 else count
        for offset in range(0, count, block):
            key_start = start + offset
            key_pos = key_start + jnp.arange(block)
            key_ids = lax.dynamic_slice_in_dim(ids_all, key_start, block)
            block_k = piece_k[offset : offset + block]
            block_v = piece_v[offset : offset + block]
            low = 0

            def compute(state, low=low):
                return update(state, block_k, block_v, key_pos, key_ids)

            wanted = jnp.logical_and(active, key_start <= q_top[0])
            updated = [lax.cond(wanted, compute, lambda state: state, carry[0])]
            carry = tuple(updated)
        return carry

    def initial(kv_count, group):
        return tuple(
            (
                (
                    jnp.full((kv_count, group, gsize), -1e30, jnp.float32),
                    jnp.zeros((kv_count, group, gsize), jnp.float32),
                    jnp.zeros((kv_count, group, gsize, head_size), jnp.float32),
                )
                for index in range(groups)
            )
        )

    def finish(carry):
        parts = [
            total / jnp.where(denom > 0.0, denom, 1.0)[..., None] for top, denom, total in carry
        ]
        joined = parts[0]
        kv_count, group = (joined.shape[0], joined.shape[1])
        return (
            jnp.transpose(joined, (2, 0, 1, 3))
            .reshape(rows, kv_count * group * head_size)
            .astype(jnp.bfloat16)
        )

    return (fold, initial, finish)


def shards(
    hidden_in,
    doc_ids,
    layer_kind,
    norm_gain,
    q_weight,
    k_weight,
    v_weight,
    bc_weight,
    dt_weight,
    dt_bias,
    decay_rate,
    skip_gain,
):
    current = hidden_in[0]
    rows, width = current.shape
    ctx_pos = lax.axis_index("ctx")
    tp_pos = lax.axis_index("tp")
    ids_all = lax.all_gather(doc_ids, "ctx", axis=0, tiled=True)
    first = ctx_pos * rows
    prev_id = jnp.where(
        ctx_pos > 0,
        lax.dynamic_index_in_dim(ids_all, jnp.maximum(first - 1, 0), 0, keepdims=False),
        -1,
    )
    gain = norm_gain[0]
    head_size = HD
    q_cols = q_weight.shape[2]
    kv_cols = k_weight.shape[2]
    heads_local = q_cols // head_size
    kv_local = kv_cols // head_size
    group = heads_local // kv_local
    is_attention = layer_kind[0] == 1
    hf = current.astype(jnp.float32)
    squares = lax.psum(jnp.sum(hf * hf, axis=1), "tp")
    xn = (hf * lax.rsqrt(squares / D + 1e-05)[:, None] * gain[None, :]).astype(jnp.bfloat16)
    whole = lax.all_gather(xn, "tp", axis=1, tiled=True)
    empty = (
        jnp.zeros((rows, q_cols), jnp.float32),
        jnp.zeros((rows, kv_cols), jnp.float32),
        jnp.zeros((rows, kv_cols), jnp.float32),
    )
    pieces = (
        lax.all_gather(q_weight[0], "ctx", axis=0, tiled=True),
        lax.all_gather(k_weight[0], "ctx", axis=0, tiled=True),
        lax.all_gather(v_weight[0], "ctx", axis=0, tiled=True),
    )

    def really(values):
        return tuple(
            (jnp.dot(whole, piece, preferred_element_type=jnp.float32) for piece in pieces)
        )

    q_sum, k_sum, v_sum = lax.cond(is_attention, really, lambda values: values, empty)
    query = q_sum.astype(jnp.bfloat16).reshape(rows, kv_local, group, head_size)
    keys = k_sum.astype(jnp.bfloat16).reshape(rows, kv_local, head_size)
    values = v_sum.astype(jnp.bfloat16).reshape(rows, kv_local, head_size)
    q_pos = first + jnp.arange(rows)
    fold, initial, finish = make_fold(query, q_pos, doc_ids, ids_all, 1, head_size, is_attention)
    carry = fold(
        initial(kv_local, group),
        (
            lax.all_gather(keys, "ctx", axis=0, tiled=True),
            lax.all_gather(values, "ctx", axis=0, tiled=True),
        ),
        jnp.int32(0),
    )
    attended = finish(carry)
    attention_result = (current.astype(jnp.float32) + attended.astype(jnp.float32)).astype(
        jnp.bfloat16
    )
    ssm_local = dt_bias.shape[1]
    channels = width // ssm_local
    inputs = xn.astype(jnp.float32).reshape(rows, ssm_local, channels)
    maps, step_all = lax.psum(
        (
            jnp.dot(xn, bc_weight[0], preferred_element_type=jnp.float32),
            jnp.dot(xn, dt_weight[0], preferred_element_type=jnp.float32),
        ),
        "tp",
    )
    step = jax.nn.softplus(
        lax.dynamic_slice_in_dim(step_all, tp_pos * ssm_local, ssm_local, 1) + dt_bias[0][None, :]
    )
    state_size = maps.shape[1] // 2
    in_map = maps[:, :state_size]
    out_map = maps[:, state_size:]
    cumulative = jnp.cumsum(-step * decay_rate[0][None, :], axis=0)
    order = jnp.arange(rows)
    pairs = (doc_ids[:, None] == doc_ids[None, :]) & (order[:, None] >= order[None, :])
    exponent = jnp.where(
        pairs[:, :, None], cumulative[:, None, :] - cumulative[None, :, :], -jnp.inf
    )
    intersection = jnp.dot(out_map, in_map.T, precision=lax.Precision.HIGHEST)
    weighted = inputs * step[:, :, None]
    inner = jnp.einsum(
        "tsh,shp->thp",
        jnp.exp(exponent) * intersection[:, :, None],
        weighted,
        precision=lax.Precision.HIGHEST,
    )
    end_weight = (
        jnp.exp(cumulative[-1][None, :] - cumulative)
        * (doc_ids == doc_ids[-1]).astype(jnp.float32)[:, None]
    )
    end_state = jnp.einsum(
        "sh,sn,shp->hnp", end_weight, in_map, weighted, precision=lax.Precision.HIGHEST
    )
    total_decay = jnp.exp(cumulative[-1]) * (doc_ids[-1] == prev_id).astype(jnp.float32)

    def combine(earlier, later):
        return (earlier[0] * later[0], earlier[1] * later[0][:, None, None] + later[1])

    identity = (jnp.ones_like(total_decay), jnp.zeros_like(end_state))
    incoming = entering((total_decay, end_state), "ctx", combine, identity)[1]
    reach = jnp.exp(cumulative) * (doc_ids == prev_id).astype(jnp.float32)[:, None]
    carried = (
        jnp.einsum("tn,hnp->thp", out_map, incoming, precision=lax.Precision.HIGHEST)
        * reach[:, :, None]
    )
    outputs = inner + carried + skip_gain[0][None, :, None] * inputs
    outputs = outputs * lax.rsqrt(jnp.mean(outputs * outputs, axis=2, keepdims=True) + 1e-05)
    state_result = (current.astype(jnp.float32) + outputs.reshape(rows, width)).astype(jnp.bfloat16)
    produced = jnp.where(is_attention, attention_result, state_result)
    moved = passed_along(produced, "pipe", 1)
    return (produced[None], moved[None])


CHUNKS = 4
MESH = pl.DeviceIdType.MESH
F32 = jnp.float32
BF16 = jnp.bfloat16


def dot(a, b):
    return jnp.dot(a, b, preferred_element_type=F32)


def exact(a, b):
    return jnp.dot(a, b, preferred_element_type=F32, precision=lax.Precision.HIGHEST)


def column_of(row, count):
    same = lax.broadcasted_iota(jnp.int32, (count, count), 0) == lax.broadcasted_iota(
        jnp.int32, (count, count), 1
    )
    return jnp.sum(jnp.where(same, row, 0.0), axis=1, keepdims=True)


def kernel(
    h_hbm,
    gain_hbm,
    bc_hbm,
    dt_hbm,
    ids_hbm,
    kind_hbm,
    bias_hbm,
    rate_hbm,
    skip_hbm,
    q_hbm,
    k_hbm,
    v_hbm,
    out_hbm,
    passed_hbm,
    h_ref,
    gain_ref,
    bc_ref,
    dt_ref,
    ids_ref,
    kind_ref,
    bias_ref,
    rate_ref,
    skip_ref,
    blocks,
    weight,
    xn_ref,
    squares_out,
    squares_in,
    sums_out,
    sums_in,
    info_out,
    info_in,
    state_out,
    state_in,
    part_out,
    part_in,
    kvpart_out,
    kvpart_in,
    sums_q,
    kv_all,
    q_all,
    state_res,
    cols_ref,
    rows_ref,
    direct_ref,
    gram_ref,
    prod,
    prev,
    w_sem,
    ahead_sem,
    behind_sem,
    across_sem,
    b_recv,
    squares_ssem,
    squares_rsem,
    sums_ssem,
    sums_rsem,
    small_ssem,
    small_rsem,
    part_ssem,
    part_rsem,
    kvpart_sem,
    pipe_ssem,
    pipe_rsem,
    out_sem,
):
    p, c, t = lax.axis_index("pipe"), lax.axis_index("ctx"), lax.axis_index("tp")
    pipes, tps = lax.axis_size("pipe"), lax.axis_size("tp")
    oc = 1 - c
    rows, width = h_ref.shape
    step_rows = rows // CHUNKS
    heads = bias_ref.shape[1]
    pairs = heads // 2
    channels = width // heads
    n_state = bc_ref.shape[0] // 2
    half = tps // 2
    q_cols = q_hbm.shape[1]
    kv_cols = k_hbm.shape[1]
    all_cols = q_cols + 2 * kv_cols
    q_heads = q_cols // HD

    pairs_in = [
        (h_hbm, h_ref),
        (gain_hbm, gain_ref),
        (bc_hbm, bc_ref),
        (dt_hbm, dt_ref),
        (ids_hbm, ids_ref),
        (kind_hbm, kind_ref),
        (bias_hbm, bias_ref),
        (rate_hbm, rate_ref),
        (skip_hbm, skip_ref),
        (q_hbm, weight.at[:, pl.ds(0, q_cols)]),
        (k_hbm, weight.at[:, pl.ds(q_cols, kv_cols)]),
        (v_hbm, weight.at[:, pl.ds(q_cols + kv_cols, kv_cols)]),
    ]
    loads = [
        pltpu.make_async_copy(source, into, w_sem.at[n])
        for n, (source, into) in enumerate(pairs_in)
    ]
    for load in loads:
        load.start()

    barrier = pltpu.get_barrier_semaphore()
    for other in range(1, tps):
        pl.semaphore_signal(
            barrier, inc=1, device_id={"tp": lax.rem(t + other, tps)}, device_id_type=MESH
        )
    pl.semaphore_signal(barrier, inc=1, device_id={"ctx": oc}, device_id_type=MESH)

    @pl.when(p > 0)
    def _():
        pl.semaphore_signal(barrier, inc=1, device_id={"pipe": p - 1}, device_id_type=MESH)

    @pl.when(p < pipes - 1)
    def _():
        pl.semaphore_signal(barrier, inc=1, device_id={"pipe": p + 1}, device_id_type=MESH)

    loads[0].wait()
    loads[1].wait()
    hf = h_ref[...].astype(F32)
    gain = gain_ref[...]
    hg = (hf * gain).astype(BF16)
    blocks[c, t] = hg
    squares = jnp.sum(hf * hf, axis=1, keepdims=True)
    squares_out[...] = jnp.broadcast_to(squares, (rows, 128)).T[0:8]
    squares_in[t] = squares_out[...]

    neighbours = (p > 0).astype(jnp.int32) + (p < pipes - 1).astype(jnp.int32)
    pl.semaphore_wait(barrier, tps + neighbours)

    def span(ch):
        return pl.ds(ch * step_rows, step_rows)

    turn = 1 - 2 * c
    place = c * (tps - 1) + t * turn

    def block_at(kind, e):
        return (c if kind == "O" else oc), c * (tps - 1) + e * turn

    def block_copy(item, ch, sem, device):
        tok, b = block_at(*item)
        ref = blocks.at[tok, b, span(ch)]
        return pltpu.make_async_remote_copy(
            ref, ref, sem, b_recv.at[tok, b, ch], device_id=device, device_id_type=MESH
        )

    O0, O1, O2, O3, F0, F1 = ("O", 0), ("O", 1), ("O", 2), ("O", 3), ("F", 0), ("F", 1)
    ahead, behind = (O0, O1, F0), (O1, O2, F1)

    def ahead_copy(item, ch):
        return block_copy(item, ch, ahead_sem.at[ahead.index(item), ch], {"tp": t + turn})

    def behind_copy(item, ch):
        return block_copy(item, ch, behind_sem.at[behind.index(item), ch], {"tp": t - turn})

    def across_copy(item, ch):
        return block_copy(item, ch, across_sem.at[ch], {"ctx": oc})

    def own_sends(ch):
        @pl.when(place == 0)
        def _():
            ahead_copy(O0, ch).start()

        @pl.when(place == 1)
        def _():
            behind_copy(O1, ch).start()
            ahead_copy(O1, ch).start()

        @pl.when(place == 2)
        def _():
            across_copy(O2, ch).start()
            behind_copy(O2, ch).start()

        @pl.when(place == 3)
        def _():
            across_copy(O3, ch).start()

    def arrive(item, at, ch, then=()):
        @pl.when(place == at)
        def _():
            block_copy(item, ch, across_sem.at[ch], {"ctx": oc}).wait_recv()
            for onward in then:
                onward(item, ch).start()

    def gathered(out, into, ssem, rsem, k, mine):
        source = out.at[k] if len(out.shape) == 3 else out
        place = t if mine else k
        return pltpu.make_async_remote_copy(
            source,
            into.at[place],
            ssem.at[k],
            rsem.at[place],
            device_id={"tp": k},
            device_id_type=MESH,
        )

    def squares_copy(k, mine):
        return gathered(squares_out, squares_in, squares_ssem, squares_rsem, k, mine)

    def sums_copy(k, mine):
        return gathered(sums_out, sums_in, sums_ssem, sums_rsem, k, mine)

    peers = [lax.rem(t + other, tps) for other in range(1, tps)]
    for k in peers:
        squares_copy(k, True).start()
    for ch in range(CHUNKS // 2):
        own_sends(ch)
    for k in peers:
        squares_copy(k, False).wait_recv()
    squares = squares_in[0]
    for k in range(1, tps):
        squares = squares + squares_in[k]
    r_row = lax.rsqrt(squares / D + 1e-05)
    r_wide = jnp.broadcast_to(r_row[0:1], (128, rows)).T
    xn = (hf * r_wide[:, 0:1] * gain).astype(BF16)
    xn_ref[...] = xn
    dt_at = 2 * n_state
    for load in loads[2:9]:
        load.wait()

    def against(w):
        return lax.dot_general(w, xn, (((1,), (1,)), ((), ())), preferred_element_type=F32)

    packed = jnp.concatenate([against(bc_ref[...]), against(dt_ref[...])], axis=0)
    for k in range(tps):
        dt_row = dt_at + k * heads
        sums_out[k] = jnp.concatenate([packed[:dt_at], packed[dt_row : dt_row + heads]], axis=0)
    sums_in[t] = sums_out[t]
    for k in peers:
        sums_copy(k, True).start()
    ids_row = ids_ref[...].astype(F32)
    info_out[0:8] = r_row
    info_out[8:16] = jnp.broadcast_to(ids_row, (8, rows))
    info_copy = pltpu.make_async_remote_copy(
        info_out,
        info_in,
        small_ssem.at[0],
        small_rsem.at[0],
        device_id={"ctx": oc},
        device_id_type=MESH,
    )
    info_copy.start()
    for ch in range(CHUNKS // 2, CHUNKS):
        own_sends(ch)

    def first_arrivals(ch):
        arrive(F0, 0, ch, (ahead_copy,))
        arrive(O2, 1, ch, (behind_copy, across_copy))
        arrive(O0, 1, ch, (ahead_copy,))
        arrive(F1, 1, ch, (behind_copy,))
        arrive(O1, 2, ch, (ahead_copy,))
        arrive(O1, 0, ch)

    for ch in range(CHUNKS // 2):
        first_arrivals(ch)
    for k in peers:
        sums_copy(k, False).wait_recv()

    total = sums_in[0]
    for k in range(1, tps):
        total = total + sums_in[k]
    maps = total[:dt_at]
    drive = total[dt_at : dt_at + heads] + column_of(bias_ref[...], heads)
    step = jnp.maximum(drive, 0.0) + jnp.log1p(jnp.exp(-jnp.abs(drive)))
    upper = (
        lax.broadcasted_iota(jnp.int32, (rows, rows), 0)
        <= lax.broadcasted_iota(jnp.int32, (rows, rows), 1)
    ).astype(F32)
    cum = exact(-step * column_of(rate_ref[...], heads), upper)
    cols = jnp.concatenate(
        [
            maps,
            cum,
            r_row,
            jnp.broadcast_to(ids_row, (8, rows)),
            step,
            jnp.zeros((128 - dt_at - 2 * heads - 16, rows), F32),
        ],
        axis=0,
    ).T
    cols_ref[...] = cols
    r_at = dt_at + heads
    ids_col = cols[:, r_at + 8 : r_at + 9]
    low = lax.broadcasted_iota(jnp.int32, (rows, rows), 0) > lax.broadcasted_iota(
        jnp.int32, (rows, rows), 1
    )
    allowed = (ids_col == ids_row) & low
    gram_ref[0] = jnp.where(allowed, exact(cols[:, n_state:dt_at], maps[:n_state]), 0.0)
    in_cols, out_cols = cols[:, :n_state], cols[:, n_state:dt_at]
    own_term = jnp.sum(in_cols * out_cols, axis=1, keepdims=True)
    direct_ref[...] = cols[:, r_at + 16 : r_at + 16 + heads] * own_term + skip_ref[...]
    gram_ref[1] = jnp.where(allowed, 0.0, -1e30)
    rows_ref[0:heads] = cum
    rows_ref[heads : 2 * heads] = step
    tail = (
        jnp.exp(cum[:, rows - 1 : rows] - cum)
        * jnp.where(ids_row == ids_row[:, rows - 1 : rows], 1.0, 0.0)
        * step
    )
    left_lanes = lax.broadcasted_iota(jnp.int32, (1, 2 * channels), 1) < channels
    for i in range(pairs):
        x_pair = xn_ref[:, i * 2 * channels : (i + 1) * 2 * channels]
        weights = jnp.concatenate(
            [maps[:n_state] * tail[2 * i + k : 2 * i + k + 1] for k in range(2)], axis=0
        ).astype(BF16)
        ends = dot(weights, x_pair)
        state_out[i] = jnp.where(left_lanes, ends[:n_state], ends[n_state:]).astype(BF16)
    state_copy = pltpu.make_async_remote_copy(
        state_out,
        state_in,
        small_ssem.at[1],
        small_rsem.at[1],
        device_id={"ctx": oc},
        device_id_type=MESH,
    )
    state_copy.start()

    def state_pair(i):
        x_pair = xn_ref[:, i * 2 * channels : (i + 1) * 2 * channels]
        outs, decays = [], []
        reach = jnp.where(
            (cols_ref[:, r_at + 8 : r_at + 9] == info_in[8:9, rows - 1 : rows]) & (c > 0), 1.0, 0.0
        )
        for head in (2 * i, 2 * i + 1):
            cum_col = cols_ref[:, dt_at + head : dt_at + head + 1]
            decay = jnp.exp(cum_col - rows_ref[head : head + 1] + gram_ref[1])
            mixed = decay * gram_ref[0] * rows_ref[heads + head : heads + head + 1]
            outs.append(dot(mixed.astype(BF16), x_pair))
            decays.append(jnp.exp(cum_col) * reach)
        skips = [direct_ref[:, 2 * i + k : 2 * i + k + 1] for k in range(2)]
        carried = dot(cols_ref[:, n_state:dt_at].astype(BF16), state_in[i])
        y = (
            jnp.where(left_lanes, outs[0], outs[1])
            + carried * jnp.where(left_lanes, decays[0], decays[1])
            + jnp.where(left_lanes, skips[0], skips[1]) * x_pair.astype(F32)
        )
        squared = y * y
        first = jnp.sum(jnp.where(left_lanes, squared, 0.0), axis=1, keepdims=True)
        second = jnp.sum(jnp.where(left_lanes, 0.0, squared), axis=1, keepdims=True)
        mean = jnp.where(left_lanes, first, second) / channels
        z = y * lax.rsqrt(mean + 1e-05)
        lanes = slice(i * 2 * channels, (i + 1) * 2 * channels)
        state_res[:, lanes] = (h_ref[:, lanes].astype(F32) + z).astype(BF16)

    first_half = half * c

    def project(x, j, column):
        depth = slice(j * width, (j + 1) * width)
        return dot(x, weight[depth, column : column + 256])

    def project_ours():
        x = [blocks[c, first_half + j] for j in range(half)]
        for column in (*range(q_cols, all_cols, 256), *range(0, q_cols, 256)):
            value = sum([project(x[j], j, column) for j in range(1, half)], project(x[0], 0, column))
            sums_q[c, :, column : column + 256] = value
            if column == q_cols:
                kvpart_out[...] = value.astype(BF16)
                kvpart_copy().start()

    def part_copy(ch):
        return pltpu.make_async_remote_copy(
            part_out.at[span(ch)],
            part_in.at[span(ch)],
            part_ssem.at[ch],
            part_rsem.at[ch],
            device_id={"ctx": oc},
            device_id_type=MESH,
        )

    def kvpart_copy():
        return pltpu.make_async_remote_copy(
            kvpart_out,
            kvpart_in,
            kvpart_sem.at[0],
            kvpart_sem.at[1],
            device_id={"ctx": oc},
            device_id_type=MESH,
        )

    early_block = block_at("F", jnp.where(place == 0, 0, 1))[1]
    late_block = block_at("F", jnp.where(place == 0, 1, 0))[1]

    def weight_rows(block, column):
        start = pl.multiple_of((block - first_half) * width, width)
        return weight[pl.ds(start, width), column : column + 256]

    def project_early():
        x = blocks[oc, early_block]
        for column in range(0, all_cols, 256):
            sums_q[oc, :, column : column + 256] = dot(x, weight_rows(early_block, column))

    def project_late(ch):
        x = blocks[oc, late_block, span(ch)]
        for column in range(0, all_cols, 256):
            lanes = slice(column, column + 256)
            value = sums_q[oc, span(ch), lanes] + dot(x, weight_rows(late_block, column))
            part_out[span(ch), lanes] = value.astype(BF16)
            if column == q_cols:
                sums_q[oc, span(ch), lanes] = value
        part_copy(ch).start()

    for ch in range(CHUNKS // 2, CHUNKS):
        first_arrivals(ch)
    info_copy.wait_recv()
    state_copy.wait_recv()
    done = 0

    def state_until(upto):
        for i in range(done, upto):
            state_pair(i)
        return upto

    for ch in range(CHUNKS):
        arrive(O2, 0, ch, (across_copy,))
        arrive(F0, 1, ch, (ahead_copy,))
        arrive(O0, 2, ch, (ahead_copy,))
        arrive(O1, 3, ch)
        done = state_until(pairs * (ch + 1) // (2 * CHUNKS))
    for load in loads[9:]:
        load.wait()
    for ch in range(CHUNKS):
        arrive(F0, 2, ch, (ahead_copy,))
        done = state_until(pairs * (CHUNKS + ch + 1) // (2 * CHUNKS))
    for ch in range(CHUNKS):
        arrive(O0, 3, ch)
    project_ours()
    for ch in range(CHUNKS):
        arrive(F1, 2, ch)
        arrive(F1, 3, ch)
    project_early()
    for ch in range(CHUNKS):
        arrive(F1, 0, ch)
        arrive(F0, 3, ch)
        project_late(ch)

    r_col = cols_ref[:, r_at : r_at + 1]
    kvpart_copy().wait_recv()
    their_r = jnp.broadcast_to(info_in[0:1], (128, rows)).T[:, 0:1]
    for ch in range(CHUNKS):
        part_copy(ch).wait_recv()
    ours = (sums_q[c] + part_in[...].astype(F32)) * r_col
    q_all[...] = ours[:, :q_cols].astype(BF16)
    kv_all[c] = ours[:, q_cols:].astype(BF16)
    kv_all[oc] = ((sums_q[oc, :, q_cols:] + kvpart_in[...].astype(F32)) * their_r).astype(BF16)

    key_pos = lax.broadcasted_iota(jnp.int32, (rows, 2 * rows), 1)
    query_pos = c * rows + lax.broadcasted_iota(jnp.int32, (rows, 2 * rows), 0)
    my_ids, their_ids = ids_row, info_in[8:9]
    at_first = jnp.where(c == 0, my_ids, their_ids)
    at_second = jnp.where(c == 0, their_ids, my_ids)
    key_ids = jnp.concatenate([at_first, at_second], axis=1)
    wanted = (key_pos <= query_pos) & (key_ids == cols_ref[:, r_at + 8 : r_at + 9])
    keys = kv_all[:, :, :HD].reshape(2 * rows, HD)
    values = kv_all[:, :, HD:].reshape(2 * rows, HD)
    attention = kind_ref[...] == 1
    per = prod.shape[2] // HD

    def pipe_copy(k):
        return pltpu.make_async_remote_copy(
            prod.at[k],
            prev.at[k],
            pipe_ssem.at[k],
            pipe_rsem.at[k],
            device_id={"pipe": p + 1},
            device_id_type=MESH,
        )

    span_p = prod.shape[2]

    def out_copy(k):
        lanes = pl.ds(k * span_p, span_p)
        return pltpu.make_async_copy(prod.at[k], out_hbm.at[:, lanes], out_sem.at[0, k])

    def passed_copy(k):
        lanes = pl.ds(k * span_p, span_p)
        return pltpu.make_async_copy(prev.at[k], passed_hbm.at[:, lanes], out_sem.at[1, k])

    for head in range(q_heads):
        lanes = slice(head * HD, (head + 1) * HD)
        scores = lax.dot_general(
            q_all[:, lanes], keys, (((1,), (1,)), ((), ())), preferred_element_type=F32
        ) * (HD ** (-0.5))
        scores = jnp.where(wanted, scores, -1e30)
        top = jnp.max(scores, axis=1, keepdims=True)
        probs = jnp.exp(scores - top)
        denom = jnp.sum(probs, axis=1, keepdims=True)
        mixed = (dot(probs.astype(BF16), values) / denom).astype(BF16)
        attended = (h_ref[:, lanes].astype(F32) + mixed.astype(F32)).astype(BF16)
        result = jnp.where(
            jnp.broadcast_to(attention, (rows, HD)),
            attended.astype(F32),
            state_res[:, lanes].astype(F32),
        ).astype(BF16)
        inner = head % per
        prod[head // per, :, inner * HD : (inner + 1) * HD] = result
        if inner == per - 1:
            out_copy(head // per).start()

            @pl.when(p < pipes - 1)
            def _(k=head // per):
                pipe_copy(k).start()

    for ch in range(CHUNKS):
        across_copy(O2, ch).wait_send()

        @pl.when(place < 3)
        def _(ch=ch):
            ahead_copy(F0, ch).wait_send()
            ahead_copy(O0, ch).wait_send()

        @pl.when((place == 1) | (place == 2))
        def _(ch=ch):
            ahead_copy(O1, ch).wait_send()
            behind_copy(O2, ch).wait_send()

        @pl.when(place == 1)
        def _(ch=ch):
            behind_copy(O1, ch).wait_send()
            behind_copy(F1, ch).wait_send()

        part_copy(ch).wait_send()
    kvpart_copy().wait_send()
    for k in peers:
        squares_copy(k, True).wait_send()
        sums_copy(k, True).wait_send()
    info_copy.wait_send()
    state_copy.wait_send()

    @pl.when(p == 0)
    def _():
        prev[...] = jnp.zeros(prev.shape, BF16)

    for k in range(q_heads // per):

        @pl.when(p > 0)
        def _(k=k):
            pipe_copy(k).wait_recv()

        passed_copy(k).start()
    for k in range(q_heads // per):
        out_copy(k).wait()
        passed_copy(k).wait()

    @pl.when(p < pipes - 1)
    def _():
        for k in range(q_heads // per):
            pipe_copy(k).wait_send()


def deliver(out_from, passed_from, out_to, passed_to, held, sem):
    rows = held.shape[1] // 2
    arriving, leaving = [], []
    for n, (source, into) in enumerate(((out_from, out_to), (passed_from, passed_to))):
        for k in range(2):
            part = pl.ds(k * rows, rows)
            place = held.at[n, part]
            arriving.append(pltpu.make_async_copy(source.at[part], place, sem.at[0, n, k]))
            leaving.append(pltpu.make_async_copy(place, into.at[part], sem.at[1, n, k]))
    for copy in arriving:
        copy.start()
    for before, after in zip(arriving, leaving):
        before.wait()
        after.start()
    for copy in leaving:
        copy.wait()


def fused(
    hidden_in,
    doc_ids,
    layer_kind,
    norm_gain,
    q_weight,
    k_weight,
    v_weight,
    bc_weight,
    dt_weight,
    dt_bias,
    decay_rate,
    skip_gain,
):
    _, rows, width = hidden_in.shape
    depth, q_cols = q_weight.shape[1:]
    kv_cols = k_weight.shape[2]
    heads = dt_bias.shape[1]
    n_state = bc_weight.shape[2] // 2
    tps = lax.axis_size("tp")
    anywhere = pl.BlockSpec(memory_space=pl.ANY)
    small = 2 * n_state + heads
    dma = pltpu.SemaphoreType.DMA
    shape = jax.ShapeDtypeStruct((rows, width), BF16)
    out, passed = pl.pallas_call(
        kernel,
        out_shape=(shape, shape),
        in_specs=[anywhere] * 12,
        out_specs=(anywhere, anywhere),
        scratch_shapes=[
            pltpu.VMEM((rows, width), BF16),
            pltpu.VMEM((1, width), F32),
            pltpu.VMEM((2 * n_state, width), BF16),
            pltpu.VMEM((heads * tps, width), BF16),
            pltpu.VMEM((1, rows), jnp.int32),
            pltpu.VMEM((1, 1), jnp.int32),
            pltpu.VMEM((1, heads), F32),
            pltpu.VMEM((1, heads), F32),
            pltpu.VMEM((1, heads), F32),
            pltpu.VMEM((2, tps, rows, width), BF16),
            pltpu.VMEM((depth, q_cols + 2 * kv_cols), BF16),
            pltpu.VMEM((rows, width), BF16),
            pltpu.VMEM((8, rows), F32),
            pltpu.VMEM((tps, 8, rows), F32),
            pltpu.VMEM((tps, small, rows), F32),
            pltpu.VMEM((tps, small, rows), F32),
            pltpu.VMEM((16, rows), F32),
            pltpu.VMEM((16, rows), F32),
            pltpu.VMEM((heads // 2, n_state, 2 * width // heads), BF16),
            pltpu.VMEM((heads // 2, n_state, 2 * width // heads), BF16),
            pltpu.VMEM((rows, q_cols + 2 * kv_cols), BF16),
            pltpu.VMEM((rows, q_cols + 2 * kv_cols), BF16),
            pltpu.VMEM((rows, 2 * kv_cols), BF16),
            pltpu.VMEM((rows, 2 * kv_cols), BF16),
            pltpu.VMEM((2, rows, q_cols + 2 * kv_cols), F32),
            pltpu.VMEM((2, rows, 2 * kv_cols), BF16),
            pltpu.VMEM((rows, q_cols), BF16),
            pltpu.VMEM((rows, width), BF16),
            pltpu.VMEM((rows, 128), F32),
            pltpu.VMEM((2 * heads, rows), F32),
            pltpu.VMEM((rows, heads), F32),
            pltpu.VMEM((2, rows, rows), F32),
            pltpu.VMEM((4, rows, width // 4), BF16),
            pltpu.VMEM((4, rows, width // 4), BF16),
            dma((12,)),
            dma((3, CHUNKS)),
            dma((3, CHUNKS)),
            dma((CHUNKS,)),
            dma((2, tps, CHUNKS)),
            dma((tps,)),
            dma((tps,)),
            dma((tps,)),
            dma((tps,)),
            dma((2,)),
            dma((2,)),
            dma((CHUNKS,)),
            dma((CHUNKS,)),
            dma((2,)),
            dma((4,)),
            dma((4,)),
            dma((2, 4)),
        ],
        compiler_params=pltpu.CompilerParams(
            collective_id=0, has_side_effects=True, vmem_limit_bytes=60 * 2**20
        ),
        cost_estimate=pl.CostEstimate(
            flops=4 * rows * depth * (q_cols + 2 * kv_cols),
            bytes_accessed=2 * depth * (q_cols + 2 * kv_cols),
            transcendentals=0,
        ),
    )(
        hidden_in[0],
        norm_gain,
        bc_weight[0].T,
        dt_weight[0].T,
        doc_ids[None],
        layer_kind[None],
        dt_bias,
        decay_rate,
        skip_gain,
        q_weight[0],
        k_weight[0],
        v_weight[0],
    )
    out, passed = pl.pallas_call(
        deliver,
        out_shape=(shape, shape),
        in_specs=[anywhere] * 2,
        out_specs=(anywhere, anywhere),
        scratch_shapes=[pltpu.VMEM((2, rows, width), BF16), dma((2, 2, 2))],
        compiler_params=pltpu.CompilerParams(vmem_limit_bytes=60 * 2**20),
    )(out, passed)
    return out[None], passed[None]


def solution(mesh):
    in_specs = (
        P("pipe", "ctx", "tp"),
        P("ctx"),
        P("pipe"),
        P("pipe", "tp"),
        P("pipe", "ctx", "tp"),
        P("pipe", "ctx", "tp"),
        P("pipe", "ctx", "tp"),
        P("pipe", "tp", None),
        P("pipe", "tp", None),
        P("pipe", "tp"),
        P("pipe", "tp"),
        P("pipe", "tp"),
    )
    out_specs = (P("pipe", "ctx", "tp"), P("pipe", "ctx", "tp"))
    body = fused if mesh.shape["ctx"] == 2 and mesh.shape["tp"] == 4 else shards
    return jax.shard_map(body, mesh=mesh, in_specs=in_specs, out_specs=out_specs, check_vma=False)
```

```python
import jax
import jax.numpy as jnp
from jax import lax
from jax.experimental import pallas as pl
from jax.experimental.pallas import tpu as pltpu
from jax.sharding import PartitionSpec as P

D = 4096
HD = 128


def entering(x, axis, combine, identity):
    devices, index = (lax.axis_size(axis), lax.axis_index(axis))
    everything = jax.tree.map(
        lambda part, kind: lax.all_gather(part.astype(kind), axis), x, (jnp.bfloat16, jnp.bfloat16)
    )
    start = jax.tree.map(
        lambda part, zero: jnp.broadcast_to(jnp.asarray(zero, part.dtype), part.shape), x, identity
    )

    def turn(k, before):
        reached = k < index
        new = combine(
            before, jax.tree.map(lambda part, own: part[k].astype(own.dtype), everything, x)
        )
        return jax.tree.map(lambda a, b: jnp.where(reached, a, b), new, before)

    return lax.fori_loop(0, devices, turn, start)


def passed_along(x, axis, by):
    devices = lax.axis_size(axis)
    pairs = [(i, i + by) for i in range(devices) if 0 <= i + by < devices]
    return lax.ppermute(x, axis, pairs)


def make_fold(q_rows, q_pos, q_ids, ids_all, groups, head_size, active):
    rows = q_rows.shape[0]
    gsize = rows // groups
    q_top = jnp.max(q_pos.reshape(groups, gsize), axis=1)
    scale = head_size ** (-0.5)

    def update(state, piece_k, piece_v, key_pos, key_ids):
        top, denom, total = state
        scores = (
            jnp.einsum("tkjd,skd->kjts", q_rows, piece_k, preferred_element_type=jnp.float32)
            * scale
        )
        allowed = (key_pos[None, :] <= q_pos[:, None]) & (key_ids[None, :] == q_ids[:, None])
        scores = jnp.where(allowed[None, None], scores, -1e30)
        new_top = jnp.maximum(top, jnp.max(scores, axis=-1))
        probs = jnp.where(allowed[None, None], jnp.exp(scores - new_top[..., None]), 0.0)
        factor = jnp.exp(top - new_top)
        denom = denom * factor + jnp.sum(probs, axis=-1)
        total = total * factor[..., None] + jnp.einsum(
            "kjts,skd->kjtd",
            probs.astype(jnp.bfloat16),
            piece_v,
            preferred_element_type=jnp.float32,
        )
        return (new_top, denom, total)

    def fold(carry, piece, start):
        piece_k, piece_v = piece
        count = piece_k.shape[0]
        block = 512 if count % 512 == 0 else count
        for offset in range(0, count, block):
            key_start = start + offset
            key_pos = key_start + jnp.arange(block)
            key_ids = lax.dynamic_slice_in_dim(ids_all, key_start, block)
            block_k = piece_k[offset : offset + block]
            block_v = piece_v[offset : offset + block]
            low = 0

            def compute(state, low=low):
                return update(state, block_k, block_v, key_pos, key_ids)

            wanted = jnp.logical_and(active, key_start <= q_top[0])
            updated = [lax.cond(wanted, compute, lambda state: state, carry[0])]
            carry = tuple(updated)
        return carry

    def initial(kv_count, group):
        return tuple(
            (
                (
                    jnp.full((kv_count, group, gsize), -1e30, jnp.float32),
                    jnp.zeros((kv_count, group, gsize), jnp.float32),
                    jnp.zeros((kv_count, group, gsize, head_size), jnp.float32),
                )
                for index in range(groups)
            )
        )

    def finish(carry):
        parts = [
            total / jnp.where(denom > 0.0, denom, 1.0)[..., None] for top, denom, total in carry
        ]
        joined = parts[0]
        kv_count, group = (joined.shape[0], joined.shape[1])
        return (
            jnp.transpose(joined, (2, 0, 1, 3))
            .reshape(rows, kv_count * group * head_size)
            .astype(jnp.bfloat16)
        )

    return (fold, initial, finish)


def shards(
    hidden_in,
    doc_ids,
    layer_kind,
    norm_gain,
    q_weight,
    k_weight,
    v_weight,
    bc_weight,
    dt_weight,
    dt_bias,
    decay_rate,
    skip_gain,
):
    current = hidden_in[0]
    rows, width = current.shape
    ctx_pos = lax.axis_index("ctx")
    tp_pos = lax.axis_index("tp")
    ids_all = lax.all_gather(doc_ids, "ctx", axis=0, tiled=True)
    first = ctx_pos * rows
    prev_id = jnp.where(
        ctx_pos > 0,
        lax.dynamic_index_in_dim(ids_all, jnp.maximum(first - 1, 0), 0, keepdims=False),
        -1,
    )
    gain = norm_gain[0]
    head_size = HD
    q_cols = q_weight.shape[2]
    kv_cols = k_weight.shape[2]
    heads_local = q_cols // head_size
    kv_local = kv_cols // head_size
    group = heads_local // kv_local
    is_attention = layer_kind[0] == 1
    hf = current.astype(jnp.float32)
    squares = lax.psum(jnp.sum(hf * hf, axis=1), "tp")
    xn = (hf * lax.rsqrt(squares / D + 1e-05)[:, None] * gain[None, :]).astype(jnp.bfloat16)
    whole = lax.all_gather(xn, "tp", axis=1, tiled=True)
    empty = (
        jnp.zeros((rows, q_cols), jnp.float32),
        jnp.zeros((rows, kv_cols), jnp.float32),
        jnp.zeros((rows, kv_cols), jnp.float32),
    )
    pieces = (
        lax.all_gather(q_weight[0], "ctx", axis=0, tiled=True),
        lax.all_gather(k_weight[0], "ctx", axis=0, tiled=True),
        lax.all_gather(v_weight[0], "ctx", axis=0, tiled=True),
    )

    def really(values):
        return tuple(
            (jnp.dot(whole, piece, preferred_element_type=jnp.float32) for piece in pieces)
        )

    q_sum, k_sum, v_sum = lax.cond(is_attention, really, lambda values: values, empty)
    query = q_sum.astype(jnp.bfloat16).reshape(rows, kv_local, group, head_size)
    keys = k_sum.astype(jnp.bfloat16).reshape(rows, kv_local, head_size)
    values = v_sum.astype(jnp.bfloat16).reshape(rows, kv_local, head_size)
    q_pos = first + jnp.arange(rows)
    fold, initial, finish = make_fold(query, q_pos, doc_ids, ids_all, 1, head_size, is_attention)
    carry = fold(
        initial(kv_local, group),
        (
            lax.all_gather(keys, "ctx", axis=0, tiled=True),
            lax.all_gather(values, "ctx", axis=0, tiled=True),
        ),
        jnp.int32(0),
    )
    attended = finish(carry)
    attention_result = (current.astype(jnp.float32) + attended.astype(jnp.float32)).astype(
        jnp.bfloat16
    )
    ssm_local = dt_bias.shape[1]
    channels = width // ssm_local
    inputs = xn.astype(jnp.float32).reshape(rows, ssm_local, channels)
    maps, step_all = lax.psum(
        (
            jnp.dot(xn, bc_weight[0], preferred_element_type=jnp.float32),
            jnp.dot(xn, dt_weight[0], preferred_element_type=jnp.float32),
        ),
        "tp",
    )
    step = jax.nn.softplus(
        lax.dynamic_slice_in_dim(step_all, tp_pos * ssm_local, ssm_local, 1) + dt_bias[0][None, :]
    )
    state_size = maps.shape[1] // 2
    in_map = maps[:, :state_size]
    out_map = maps[:, state_size:]
    cumulative = jnp.cumsum(-step * decay_rate[0][None, :], axis=0)
    order = jnp.arange(rows)
    pairs = (doc_ids[:, None] == doc_ids[None, :]) & (order[:, None] >= order[None, :])
    exponent = jnp.where(
        pairs[:, :, None], cumulative[:, None, :] - cumulative[None, :, :], -jnp.inf
    )
    intersection = jnp.dot(out_map, in_map.T, precision=lax.Precision.HIGHEST)
    weighted = inputs * step[:, :, None]
    inner = jnp.einsum(
        "tsh,shp->thp",
        jnp.exp(exponent) * intersection[:, :, None],
        weighted,
        precision=lax.Precision.HIGHEST,
    )
    end_weight = (
        jnp.exp(cumulative[-1][None, :] - cumulative)
        * (doc_ids == doc_ids[-1]).astype(jnp.float32)[:, None]
    )
    end_state = jnp.einsum(
        "sh,sn,shp->hnp", end_weight, in_map, weighted, precision=lax.Precision.HIGHEST
    )
    total_decay = jnp.exp(cumulative[-1]) * (doc_ids[-1] == prev_id).astype(jnp.float32)

    def combine(earlier, later):
        return (earlier[0] * later[0], earlier[1] * later[0][:, None, None] + later[1])

    identity = (jnp.ones_like(total_decay), jnp.zeros_like(end_state))
    incoming = entering((total_decay, end_state), "ctx", combine, identity)[1]
    reach = jnp.exp(cumulative) * (doc_ids == prev_id).astype(jnp.float32)[:, None]
    carried = (
        jnp.einsum("tn,hnp->thp", out_map, incoming, precision=lax.Precision.HIGHEST)
        * reach[:, :, None]
    )
    outputs = inner + carried + skip_gain[0][None, :, None] * inputs
    outputs = outputs * lax.rsqrt(jnp.mean(outputs * outputs, axis=2, keepdims=True) + 1e-05)
    state_result = (current.astype(jnp.float32) + outputs.reshape(rows, width)).astype(jnp.bfloat16)
    produced = jnp.where(is_attention, attention_result, state_result)
    moved = passed_along(produced, "pipe", 1)
    return (produced[None], moved[None])


CHUNKS = 4
MESH = pl.DeviceIdType.MESH
F32 = jnp.float32
BF16 = jnp.bfloat16


def dot(a, b):
    return jnp.dot(a, b, preferred_element_type=F32)


def exact(a, b):
    return jnp.dot(a, b, preferred_element_type=F32, precision=lax.Precision.HIGHEST)


def column_of(row, count):
    same = lax.broadcasted_iota(jnp.int32, (count, count), 0) == lax.broadcasted_iota(
        jnp.int32, (count, count), 1
    )
    return jnp.sum(jnp.where(same, row, 0.0), axis=1, keepdims=True)


def kernel(
    h_hbm,
    gain_hbm,
    bc_hbm,
    dt_hbm,
    ids_hbm,
    kind_hbm,
    bias_hbm,
    rate_hbm,
    skip_hbm,
    q_hbm,
    k_hbm,
    v_hbm,
    out_hbm,
    passed_hbm,
    h_ref,
    gain_ref,
    bc_ref,
    dt_ref,
    ids_ref,
    kind_ref,
    bias_ref,
    rate_ref,
    skip_ref,
    blocks,
    weight,
    xn_ref,
    squares_out,
    squares_in,
    sums_out,
    sums_in,
    info_out,
    info_in,
    state_out,
    state_in,
    part_out,
    part_in,
    kvpart_out,
    kvpart_in,
    sums_q,
    kv_all,
    state_res,
    cols_ref,
    rows_ref,
    direct_ref,
    gram_ref,
    prod,
    prev,
    w_sem,
    ahead_sem,
    behind_sem,
    across_sem,
    b_recv,
    squares_ssem,
    squares_rsem,
    sums_ssem,
    sums_rsem,
    small_ssem,
    small_rsem,
    part_ssem,
    part_rsem,
    kvpart_sem,
    pipe_ssem,
    pipe_rsem,
    out_sem,
):
    p, c, t = lax.axis_index("pipe"), lax.axis_index("ctx"), lax.axis_index("tp")
    pipes, tps = lax.axis_size("pipe"), lax.axis_size("tp")
    oc = 1 - c
    rows, width = h_ref.shape
    step_rows = rows // CHUNKS
    heads = bias_ref.shape[1]
    pairs = heads // 2
    channels = width // heads
    n_state = bc_ref.shape[0] // 2
    half = tps // 2
    q_cols = q_hbm.shape[1]
    kv_cols = k_hbm.shape[1]
    all_cols = q_cols + 2 * kv_cols
    q_heads = q_cols // HD

    pairs_in = [
        (h_hbm, h_ref),
        (gain_hbm, gain_ref),
        (bc_hbm, bc_ref),
        (dt_hbm, dt_ref),
        (ids_hbm, ids_ref),
        (kind_hbm, kind_ref),
        (bias_hbm, bias_ref),
        (rate_hbm, rate_ref),
        (skip_hbm, skip_ref),
        (q_hbm, weight.at[:, pl.ds(0, q_cols)]),
        (k_hbm, weight.at[:, pl.ds(q_cols, kv_cols)]),
        (v_hbm, weight.at[:, pl.ds(q_cols + kv_cols, kv_cols)]),
    ]
    loads = [
        pltpu.make_async_copy(source, into, w_sem.at[n])
        for n, (source, into) in enumerate(pairs_in)
    ]
    for load in loads:
        load.start()

    barrier = pltpu.get_barrier_semaphore()
    for other in range(1, tps):
        pl.semaphore_signal(
            barrier, inc=1, device_id={"tp": lax.rem(t + other, tps)}, device_id_type=MESH
        )
    pl.semaphore_signal(barrier, inc=1, device_id={"ctx": oc}, device_id_type=MESH)

    @pl.when(p > 0)
    def _():
        pl.semaphore_signal(barrier, inc=1, device_id={"pipe": p - 1}, device_id_type=MESH)

    @pl.when(p < pipes - 1)
    def _():
        pl.semaphore_signal(barrier, inc=1, device_id={"pipe": p + 1}, device_id_type=MESH)

    loads[0].wait()
    loads[1].wait()
    hf = h_ref[...].astype(F32)
    gain = gain_ref[...]
    hg = (hf * gain).astype(BF16)
    blocks[c, t] = hg
    kv_all[...] = jnp.zeros(kv_all.shape, BF16)
    squares = jnp.sum(hf * hf, axis=1, keepdims=True)
    squares_out[...] = jnp.broadcast_to(squares, (rows, 128)).T[0:8]
    squares_in[t] = squares_out[...]

    neighbours = (p > 0).astype(jnp.int32) + (p < pipes - 1).astype(jnp.int32)
    pl.semaphore_wait(barrier, tps + neighbours)

    def span(ch):
        return pl.ds(ch * step_rows, step_rows)

    turn = 1 - 2 * c
    place = c * (tps - 1) + t * turn

    def block_at(kind, e):
        return (c if kind == "O" else oc), c * (tps - 1) + e * turn

    def block_copy(item, ch, sem, device):
        tok, b = block_at(*item)
        ref = blocks.at[tok, b, span(ch)]
        return pltpu.make_async_remote_copy(
            ref, ref, sem, b_recv.at[tok, b, ch], device_id=device, device_id_type=MESH
        )

    O0, O1, O2, O3, F0, F1 = ("O", 0), ("O", 1), ("O", 2), ("O", 3), ("F", 0), ("F", 1)
    ahead, behind = (O0, O1, F0), (O1, O2, F1)

    def ahead_copy(item, ch):
        return block_copy(item, ch, ahead_sem.at[ahead.index(item), ch], {"tp": t + turn})

    def behind_copy(item, ch):
        return block_copy(item, ch, behind_sem.at[behind.index(item), ch], {"tp": t - turn})

    def across_copy(item, ch):
        return block_copy(item, ch, across_sem.at[ch], {"ctx": oc})

    def own_sends(ch):
        @pl.when(place == 0)
        def _():
            ahead_copy(O0, ch).start()

        @pl.when(place == 1)
        def _():
            behind_copy(O1, ch).start()
            ahead_copy(O1, ch).start()

        @pl.when(place == 2)
        def _():
            across_copy(O2, ch).start()
            behind_copy(O2, ch).start()

        @pl.when(place == 3)
        def _():
            across_copy(O3, ch).start()

    def arrive(item, at, ch, then=()):
        @pl.when(place == at)
        def _():
            block_copy(item, ch, across_sem.at[ch], {"ctx": oc}).wait_recv()
            for onward in then:
                onward(item, ch).start()

    def gathered(out, into, ssem, rsem, k, mine):
        source = out.at[k] if len(out.shape) == 3 else out
        place = t if mine else k
        return pltpu.make_async_remote_copy(
            source,
            into.at[place],
            ssem.at[k],
            rsem.at[place],
            device_id={"tp": k},
            device_id_type=MESH,
        )

    def squares_copy(k, mine):
        return gathered(squares_out, squares_in, squares_ssem, squares_rsem, k, mine)

    def sums_copy(k, mine):
        return gathered(sums_out, sums_in, sums_ssem, sums_rsem, k, mine)

    peers = [lax.rem(t + other, tps) for other in range(1, tps)]
    for k in peers:
        squares_copy(k, True).start()
    for ch in range(CHUNKS // 2):
        own_sends(ch)
    for k in peers:
        squares_copy(k, False).wait_recv()
    squares = squares_in[0]
    for k in range(1, tps):
        squares = squares + squares_in[k]
    r_row = lax.rsqrt(squares / D + 1e-05)
    r_wide = jnp.broadcast_to(r_row[0:1], (128, rows)).T
    xn = (hf * r_wide[:, 0:1] * gain).astype(BF16)
    xn_ref[...] = xn
    dt_at = 2 * n_state
    for load in loads[2:9]:
        load.wait()

    def against(w):
        return lax.dot_general(w, xn, (((1,), (1,)), ((), ())), preferred_element_type=F32)

    packed = jnp.concatenate([against(bc_ref[...]), against(dt_ref[...])], axis=0)
    for k in range(tps):
        dt_row = dt_at + k * heads
        sums_out[k] = jnp.concatenate([packed[:dt_at], packed[dt_row : dt_row + heads]], axis=0)
    sums_in[t] = sums_out[t]
    for k in peers:
        sums_copy(k, True).start()
    ids_row = ids_ref[...].astype(F32)
    info_out[0:8] = r_row
    info_out[8:16] = jnp.broadcast_to(ids_row, (8, rows))
    info_copy = pltpu.make_async_remote_copy(
        info_out,
        info_in,
        small_ssem.at[0],
        small_rsem.at[0],
        device_id={"ctx": oc},
        device_id_type=MESH,
    )
    info_copy.start()
    for ch in range(CHUNKS // 2, CHUNKS):
        own_sends(ch)

    def first_arrivals(ch):
        arrive(F0, 0, ch, (ahead_copy,))
        arrive(O2, 1, ch, (behind_copy, across_copy))
        arrive(O0, 1, ch, (ahead_copy,))
        arrive(F1, 1, ch, (behind_copy,))
        arrive(O1, 2, ch, (ahead_copy,))
        arrive(O1, 0, ch)

    for ch in range(CHUNKS // 2):
        first_arrivals(ch)
    for k in peers:
        sums_copy(k, False).wait_recv()

    total = sums_in[0]
    for k in range(1, tps):
        total = total + sums_in[k]
    maps = total[:dt_at]
    drive = total[dt_at : dt_at + heads] + column_of(bias_ref[...], heads)
    step = jnp.maximum(drive, 0.0) + jnp.log1p(jnp.exp(-jnp.abs(drive)))
    upper = (
        lax.broadcasted_iota(jnp.int32, (rows, rows), 0)
        <= lax.broadcasted_iota(jnp.int32, (rows, rows), 1)
    ).astype(F32)
    cum = exact(-step * column_of(rate_ref[...], heads), upper)
    cols = jnp.concatenate(
        [
            maps,
            cum,
            r_row,
            jnp.broadcast_to(ids_row, (8, rows)),
            step,
            jnp.zeros((128 - dt_at - 2 * heads - 16, rows), F32),
        ],
        axis=0,
    ).T
    cols_ref[...] = cols
    r_at = dt_at + heads
    ids_col = cols[:, r_at + 8 : r_at + 9]
    low = lax.broadcasted_iota(jnp.int32, (rows, rows), 0) > lax.broadcasted_iota(
        jnp.int32, (rows, rows), 1
    )
    allowed = (ids_col == ids_row) & low
    gram_ref[0] = jnp.where(allowed, exact(cols[:, n_state:dt_at], maps[:n_state]), 0.0)
    in_cols, out_cols = cols[:, :n_state], cols[:, n_state:dt_at]
    own_term = jnp.sum(in_cols * out_cols, axis=1, keepdims=True)
    direct_ref[...] = cols[:, r_at + 16 : r_at + 16 + heads] * own_term + skip_ref[...]
    gram_ref[1] = jnp.where(allowed, 0.0, -1e30)
    rows_ref[0:heads] = cum
    rows_ref[heads : 2 * heads] = step
    tail = (
        jnp.exp(cum[:, rows - 1 : rows] - cum)
        * jnp.where(ids_row == ids_row[:, rows - 1 : rows], 1.0, 0.0)
        * step
    )
    left_lanes = lax.broadcasted_iota(jnp.int32, (1, 2 * channels), 1) < channels
    for i in range(pairs):
        x_pair = xn_ref[:, i * 2 * channels : (i + 1) * 2 * channels]
        weights = jnp.concatenate(
            [maps[:n_state] * tail[2 * i + k : 2 * i + k + 1] for k in range(2)], axis=0
        ).astype(BF16)
        ends = dot(weights, x_pair)
        state_out[i] = jnp.where(left_lanes, ends[:n_state], ends[n_state:]).astype(BF16)
    state_copy = pltpu.make_async_remote_copy(
        state_out,
        state_in,
        small_ssem.at[1],
        small_rsem.at[1],
        device_id={"ctx": oc},
        device_id_type=MESH,
    )
    state_copy.start()

    def state_pair(i):
        x_pair = xn_ref[:, i * 2 * channels : (i + 1) * 2 * channels]
        outs, decays = [], []
        reach = jnp.where(
            (cols_ref[:, r_at + 8 : r_at + 9] == info_in[8:9, rows - 1 : rows]) & (c > 0), 1.0, 0.0
        )
        for head in (2 * i, 2 * i + 1):
            cum_col = cols_ref[:, dt_at + head : dt_at + head + 1]
            decay = jnp.exp(cum_col - rows_ref[head : head + 1] + gram_ref[1])
            mixed = decay * gram_ref[0] * rows_ref[heads + head : heads + head + 1]
            outs.append(dot(mixed.astype(BF16), x_pair))
            decays.append(jnp.exp(cum_col) * reach)
        skips = [direct_ref[:, 2 * i + k : 2 * i + k + 1] for k in range(2)]
        carried = dot(cols_ref[:, n_state:dt_at].astype(BF16), state_in[i])
        y = (
            jnp.where(left_lanes, outs[0], outs[1])
            + carried * jnp.where(left_lanes, decays[0], decays[1])
            + jnp.where(left_lanes, skips[0], skips[1]) * x_pair.astype(F32)
        )
        squared = y * y
        first = jnp.sum(jnp.where(left_lanes, squared, 0.0), axis=1, keepdims=True)
        second = jnp.sum(jnp.where(left_lanes, 0.0, squared), axis=1, keepdims=True)
        mean = jnp.where(left_lanes, first, second) / channels
        z = y * lax.rsqrt(mean + 1e-05)
        lanes = slice(i * 2 * channels, (i + 1) * 2 * channels)
        state_res[:, lanes] = (h_ref[:, lanes].astype(F32) + z).astype(BF16)

    first_half = half * c

    def project(x, j, column):
        depth = slice(j * width, (j + 1) * width)
        return dot(x, weight[depth, column : column + 256])

    def project_ours():
        x = [blocks[c, first_half + j] for j in range(half)]
        for column in (*range(q_cols, all_cols, 256), *range(0, q_cols, 256)):
            value = sum([project(x[j], j, column) for j in range(1, half)], project(x[0], 0, column))
            sums_q[c, :, column : column + 256] = value
            if column == q_cols:
                kvpart_out[...] = value.astype(BF16)
                kvpart_copy().start()

    def part_copy(ch):
        return pltpu.make_async_remote_copy(
            part_out.at[span(ch)],
            part_in.at[span(ch)],
            part_ssem.at[ch],
            part_rsem.at[ch],
            device_id={"ctx": oc},
            device_id_type=MESH,
        )

    def kvpart_copy():
        return pltpu.make_async_remote_copy(
            kvpart_out,
            kvpart_in,
            kvpart_sem.at[0],
            kvpart_sem.at[1],
            device_id={"ctx": oc},
            device_id_type=MESH,
        )

    early_block = block_at("F", jnp.where(place == 0, 0, 1))[1]
    late_block = block_at("F", jnp.where(place == 0, 1, 0))[1]

    def weight_rows(block, column):
        start = pl.multiple_of((block - first_half) * width, width)
        return weight[pl.ds(start, width), column : column + 256]

    def project_early():
        x = blocks[oc, early_block]
        for column in range(0, all_cols, 256):
            sums_q[oc, :, column : column + 256] = dot(x, weight_rows(early_block, column))

    def project_late(ch):
        x = blocks[oc, late_block, span(ch)]
        for column in range(0, all_cols, 256):
            lanes = slice(column, column + 256)
            value = sums_q[oc, span(ch), lanes] + dot(x, weight_rows(late_block, column))
            part_out[span(ch), lanes] = value.astype(BF16)
            if column == q_cols:
                sums_q[oc, span(ch), lanes] = value
        part_copy(ch).start()

    for ch in range(CHUNKS // 2, CHUNKS):
        first_arrivals(ch)
    info_copy.wait_recv()
    state_copy.wait_recv()
    done = 0

    def state_until(upto):
        for i in range(done, upto):
            state_pair(i)
        return upto

    for ch in range(CHUNKS):
        arrive(O2, 0, ch, (across_copy,))
        arrive(F0, 1, ch, (ahead_copy,))
        arrive(O0, 2, ch, (ahead_copy,))
        arrive(O1, 3, ch)
        done = state_until(pairs * (ch + 1) // (2 * CHUNKS))
    for load in loads[9:]:
        load.wait()
    for ch in range(CHUNKS):
        arrive(F0, 2, ch, (ahead_copy,))
        done = state_until(pairs * (CHUNKS + ch + 1) // (2 * CHUNKS))
    for ch in range(CHUNKS):
        arrive(O0, 3, ch)
    project_ours()
    for ch in range(CHUNKS):
        arrive(F1, 2, ch)
        arrive(F1, 3, ch)
    project_early()
    for ch in range(CHUNKS):
        arrive(F1, 0, ch)
        arrive(F0, 3, ch)
        project_late(ch)

    kvpart_copy().wait_recv()
    their_r = jnp.broadcast_to(info_in[0:1], (128, rows)).T[:, 0:1]
    kv_all[oc] = ((sums_q[oc, :, q_cols:] + kvpart_in[...].astype(F32)) * their_r).astype(BF16)
    my_ids, their_ids = ids_row, info_in[8:9]
    at_first = jnp.where(c == 0, my_ids, their_ids)
    at_second = jnp.where(c == 0, their_ids, my_ids)
    key_ids = jnp.concatenate([at_first, at_second], axis=1)
    key_pos = lax.broadcasted_iota(jnp.int32, (step_rows, 2 * rows), 1)
    query_at = lax.broadcasted_iota(jnp.int32, (step_rows, 2 * rows), 0)
    attention = jnp.broadcast_to(kind_ref[...] == 1, (step_rows, width))

    def pipe_copy(ch):
        return pltpu.make_async_remote_copy(
            prod.at[ch],
            prev.at[ch],
            pipe_ssem.at[ch],
            pipe_rsem.at[ch],
            device_id={"pipe": p + 1},
            device_id_type=MESH,
        )

    def out_copy(ch):
        return pltpu.make_async_copy(prod.at[ch], out_hbm.at[span(ch)], out_sem.at[0, ch])

    def passed_copy(ch):
        return pltpu.make_async_copy(prev.at[ch], passed_hbm.at[span(ch)], out_sem.at[1, ch])

    for ch in range(CHUNKS):
        part_copy(ch).wait_recv()
        here = slice(ch * step_rows, (ch + 1) * step_rows)
        ours = sums_q[c, span(ch)] + part_in[span(ch)].astype(F32)
        ours = (ours * cols_ref[here, r_at : r_at + 1]).astype(BF16)
        kv_all[c, span(ch)] = ours[:, q_cols:]
        query = jnp.concatenate(
            [ours[:, head * HD : (head + 1) * HD] for head in range(q_heads)], axis=0
        )
        keys = kv_all[:, :, :HD].reshape(2 * rows, HD)
        values = kv_all[:, :, HD:].reshape(2 * rows, HD)
        scores = lax.dot_general(
            query, keys, (((1,), (1,)), ((), ())), preferred_element_type=F32
        ) * (HD ** (-0.5))
        wanted = (key_pos <= c * rows + ch * step_rows + query_at) & (
            key_ids == cols_ref[here, r_at + 8 : r_at + 9]
        )
        barred = jnp.where(wanted, 0.0, -1e30)
        scores = scores + jnp.concatenate([barred] * q_heads, axis=0)
        top = jnp.max(scores, axis=1, keepdims=True)
        probs = jnp.exp(scores - top)
        denom = jnp.sum(probs, axis=1, keepdims=True)
        mixed = (dot(probs.astype(BF16), values) / denom).astype(BF16).astype(F32)
        attended = jnp.concatenate(
            [mixed[head * step_rows : (head + 1) * step_rows] for head in range(q_heads)], axis=1
        )
        attended = (h_ref[span(ch)].astype(F32) + attended).astype(BF16).astype(F32)
        prod[ch] = jnp.where(attention, attended, state_res[span(ch)].astype(F32)).astype(BF16)
        out_copy(ch).start()

        @pl.when(p < pipes - 1)
        def _(ch=ch):
            pipe_copy(ch).start()

    for ch in range(CHUNKS):
        across_copy(O2, ch).wait_send()

        @pl.when(place < 3)
        def _(ch=ch):
            ahead_copy(F0, ch).wait_send()
            ahead_copy(O0, ch).wait_send()

        @pl.when((place == 1) | (place == 2))
        def _(ch=ch):
            ahead_copy(O1, ch).wait_send()
            behind_copy(O2, ch).wait_send()

        @pl.when(place == 1)
        def _(ch=ch):
            behind_copy(O1, ch).wait_send()
            behind_copy(F1, ch).wait_send()

        part_copy(ch).wait_send()
    kvpart_copy().wait_send()
    for k in peers:
        squares_copy(k, True).wait_send()
        sums_copy(k, True).wait_send()
    info_copy.wait_send()
    state_copy.wait_send()

    @pl.when(p == 0)
    def _():
        prev[...] = jnp.zeros(prev.shape, BF16)

    for k in range(CHUNKS):

        @pl.when(p > 0)
        def _(k=k):
            pipe_copy(k).wait_recv()

        passed_copy(k).start()
    for k in range(CHUNKS):
        out_copy(k).wait()
        passed_copy(k).wait()

    @pl.when(p < pipes - 1)
    def _():
        for k in range(CHUNKS):
            pipe_copy(k).wait_send()


def deliver(out_from, passed_from, out_to, passed_to, held, sem):
    rows = held.shape[1] // 2
    arriving, leaving = [], []
    for n, (source, into) in enumerate(((out_from, out_to), (passed_from, passed_to))):
        for k in range(2):
            part = pl.ds(k * rows, rows)
            place = held.at[n, part]
            arriving.append(pltpu.make_async_copy(source.at[part], place, sem.at[0, n, k]))
            leaving.append(pltpu.make_async_copy(place, into.at[part], sem.at[1, n, k]))
    for copy in arriving:
        copy.start()
    for before, after in zip(arriving, leaving):
        before.wait()
        after.start()
    for copy in leaving:
        copy.wait()


def fused(
    hidden_in,
    doc_ids,
    layer_kind,
    norm_gain,
    q_weight,
    k_weight,
    v_weight,
    bc_weight,
    dt_weight,
    dt_bias,
    decay_rate,
    skip_gain,
):
    _, rows, width = hidden_in.shape
    depth, q_cols = q_weight.shape[1:]
    kv_cols = k_weight.shape[2]
    heads = dt_bias.shape[1]
    n_state = bc_weight.shape[2] // 2
    tps = lax.axis_size("tp")
    anywhere = pl.BlockSpec(memory_space=pl.ANY)
    small = 2 * n_state + heads
    dma = pltpu.SemaphoreType.DMA
    shape = jax.ShapeDtypeStruct((rows, width), BF16)
    out, passed = pl.pallas_call(
        kernel,
        out_shape=(shape, shape),
        in_specs=[anywhere] * 12,
        out_specs=(anywhere, anywhere),
        scratch_shapes=[
            pltpu.VMEM((rows, width), BF16),
            pltpu.VMEM((1, width), F32),
            pltpu.VMEM((2 * n_state, width), BF16),
            pltpu.VMEM((heads * tps, width), BF16),
            pltpu.VMEM((1, rows), jnp.int32),
            pltpu.VMEM((1, 1), jnp.int32),
            pltpu.VMEM((1, heads), F32),
            pltpu.VMEM((1, heads), F32),
            pltpu.VMEM((1, heads), F32),
            pltpu.VMEM((2, tps, rows, width), BF16),
            pltpu.VMEM((depth, q_cols + 2 * kv_cols), BF16),
            pltpu.VMEM((rows, width), BF16),
            pltpu.VMEM((8, rows), F32),
            pltpu.VMEM((tps, 8, rows), F32),
            pltpu.VMEM((tps, small, rows), F32),
            pltpu.VMEM((tps, small, rows), F32),
            pltpu.VMEM((16, rows), F32),
            pltpu.VMEM((16, rows), F32),
            pltpu.VMEM((heads // 2, n_state, 2 * width // heads), BF16),
            pltpu.VMEM((heads // 2, n_state, 2 * width // heads), BF16),
            pltpu.VMEM((rows, q_cols + 2 * kv_cols), BF16),
            pltpu.VMEM((rows, q_cols + 2 * kv_cols), BF16),
            pltpu.VMEM((rows, 2 * kv_cols), BF16),
            pltpu.VMEM((rows, 2 * kv_cols), BF16),
            pltpu.VMEM((2, rows, q_cols + 2 * kv_cols), F32),
            pltpu.VMEM((2, rows, 2 * kv_cols), BF16),
            pltpu.VMEM((rows, width), BF16),
            pltpu.VMEM((rows, 128), F32),
            pltpu.VMEM((2 * heads, rows), F32),
            pltpu.VMEM((rows, heads), F32),
            pltpu.VMEM((2, rows, rows), F32),
            pltpu.VMEM((CHUNKS, rows // CHUNKS, width), BF16),
            pltpu.VMEM((CHUNKS, rows // CHUNKS, width), BF16),
            dma((12,)),
            dma((3, CHUNKS)),
            dma((3, CHUNKS)),
            dma((CHUNKS,)),
            dma((2, tps, CHUNKS)),
            dma((tps,)),
            dma((tps,)),
            dma((tps,)),
            dma((tps,)),
            dma((2,)),
            dma((2,)),
            dma((CHUNKS,)),
            dma((CHUNKS,)),
            dma((2,)),
            dma((CHUNKS,)),
            dma((CHUNKS,)),
            dma((2, CHUNKS)),
        ],
        compiler_params=pltpu.CompilerParams(
            collective_id=0, has_side_effects=True, vmem_limit_bytes=60 * 2**20
        ),
        cost_estimate=pl.CostEstimate(
            flops=4 * rows * depth * (q_cols + 2 * kv_cols),
            bytes_accessed=2 * depth * (q_cols + 2 * kv_cols),
            transcendentals=0,
        ),
    )(
        hidden_in[0],
        norm_gain,
        bc_weight[0].T,
        dt_weight[0].T,
        doc_ids[None],
        layer_kind[None],
        dt_bias,
        decay_rate,
        skip_gain,
        q_weight[0],
        k_weight[0],
        v_weight[0],
    )
    out, passed = pl.pallas_call(
        deliver,
        out_shape=(shape, shape),
        in_specs=[anywhere] * 2,
        out_specs=(anywhere, anywhere),
        scratch_shapes=[pltpu.VMEM((2, rows, width), BF16), dma((2, 2, 2))],
        compiler_params=pltpu.CompilerParams(vmem_limit_bytes=60 * 2**20),
    )(out, passed)
    return out[None], passed[None]


def solution(mesh):
    in_specs = (
        P("pipe", "ctx", "tp"),
        P("ctx"),
        P("pipe"),
        P("pipe", "tp"),
        P("pipe", "ctx", "tp"),
        P("pipe", "ctx", "tp"),
        P("pipe", "ctx", "tp"),
        P("pipe", "tp", None),
        P("pipe", "tp", None),
        P("pipe", "tp"),
        P("pipe", "tp"),
        P("pipe", "tp"),
    )
    out_specs = (P("pipe", "ctx", "tp"), P("pipe", "ctx", "tp"))
    body = fused if mesh.shape["ctx"] == 2 and mesh.shape["tp"] == 4 else shards
    return jax.shard_map(body, mesh=mesh, in_specs=in_specs, out_specs=out_specs, check_vma=False)
```

```python
import jax
import jax.numpy as jnp
from jax import lax
from jax.experimental import pallas as pl
from jax.experimental.pallas import tpu as pltpu
from jax.sharding import PartitionSpec as P

D = 4096
HD = 128


def entering(x, axis, combine, identity):
    devices, index = (lax.axis_size(axis), lax.axis_index(axis))
    everything = jax.tree.map(
        lambda part, kind: lax.all_gather(part.astype(kind), axis), x, (jnp.bfloat16, jnp.bfloat16)
    )
    start = jax.tree.map(
        lambda part, zero: jnp.broadcast_to(jnp.asarray(zero, part.dtype), part.shape), x, identity
    )

    def turn(k, before):
        reached = k < index
        new = combine(
            before, jax.tree.map(lambda part, own: part[k].astype(own.dtype), everything, x)
        )
        return jax.tree.map(lambda a, b: jnp.where(reached, a, b), new, before)

    return lax.fori_loop(0, devices, turn, start)


def passed_along(x, axis, by):
    devices = lax.axis_size(axis)
    pairs = [(i, i + by) for i in range(devices) if 0 <= i + by < devices]
    return lax.ppermute(x, axis, pairs)


def make_fold(q_rows, q_pos, q_ids, ids_all, groups, head_size, active):
    rows = q_rows.shape[0]
    gsize = rows // groups
    q_top = jnp.max(q_pos.reshape(groups, gsize), axis=1)
    scale = head_size ** (-0.5)

    def update(state, piece_k, piece_v, key_pos, key_ids):
        top, denom, total = state
        scores = (
            jnp.einsum("tkjd,skd->kjts", q_rows, piece_k, preferred_element_type=jnp.float32)
            * scale
        )
        allowed = (key_pos[None, :] <= q_pos[:, None]) & (key_ids[None, :] == q_ids[:, None])
        scores = jnp.where(allowed[None, None], scores, -1e30)
        new_top = jnp.maximum(top, jnp.max(scores, axis=-1))
        probs = jnp.where(allowed[None, None], jnp.exp(scores - new_top[..., None]), 0.0)
        factor = jnp.exp(top - new_top)
        denom = denom * factor + jnp.sum(probs, axis=-1)
        total = total * factor[..., None] + jnp.einsum(
            "kjts,skd->kjtd",
            probs.astype(jnp.bfloat16),
            piece_v,
            preferred_element_type=jnp.float32,
        )
        return (new_top, denom, total)

    def fold(carry, piece, start):
        piece_k, piece_v = piece
        count = piece_k.shape[0]
        block = 512 if count % 512 == 0 else count
        for offset in range(0, count, block):
            key_start = start + offset
            key_pos = key_start + jnp.arange(block)
            key_ids = lax.dynamic_slice_in_dim(ids_all, key_start, block)
            block_k = piece_k[offset : offset + block]
            block_v = piece_v[offset : offset + block]
            low = 0

            def compute(state, low=low):
                return update(state, block_k, block_v, key_pos, key_ids)

            wanted = jnp.logical_and(active, key_start <= q_top[0])
            updated = [lax.cond(wanted, compute, lambda state: state, carry[0])]
            carry = tuple(updated)
        return carry

    def initial(kv_count, group):
        return tuple(
            (
                (
                    jnp.full((kv_count, group, gsize), -1e30, jnp.float32),
                    jnp.zeros((kv_count, group, gsize), jnp.float32),
                    jnp.zeros((kv_count, group, gsize, head_size), jnp.float32),
                )
                for index in range(groups)
            )
        )

    def finish(carry):
        parts = [
            total / jnp.where(denom > 0.0, denom, 1.0)[..., None] for top, denom, total in carry
        ]
        joined = parts[0]
        kv_count, group = (joined.shape[0], joined.shape[1])
        return (
            jnp.transpose(joined, (2, 0, 1, 3))
            .reshape(rows, kv_count * group * head_size)
            .astype(jnp.bfloat16)
        )

    return (fold, initial, finish)


def shards(
    hidden_in,
    doc_ids,
    layer_kind,
    norm_gain,
    q_weight,
    k_weight,
    v_weight,
    bc_weight,
    dt_weight,
    dt_bias,
    decay_rate,
    skip_gain,
):
    current = hidden_in[0]
    rows, width = current.shape
    ctx_pos = lax.axis_index("ctx")
    tp_pos = lax.axis_index("tp")
    ids_all = lax.all_gather(doc_ids, "ctx", axis=0, tiled=True)
    first = ctx_pos * rows
    prev_id = jnp.where(
        ctx_pos > 0,
        lax.dynamic_index_in_dim(ids_all, jnp.maximum(first - 1, 0), 0, keepdims=False),
        -1,
    )
    gain = norm_gain[0]
    head_size = HD
    q_cols = q_weight.shape[2]
    kv_cols = k_weight.shape[2]
    heads_local = q_cols // head_size
    kv_local = kv_cols // head_size
    group = heads_local // kv_local
    is_attention = layer_kind[0] == 1
    hf = current.astype(jnp.float32)
    squares = lax.psum(jnp.sum(hf * hf, axis=1), "tp")
    xn = (hf * lax.rsqrt(squares / D + 1e-05)[:, None] * gain[None, :]).astype(jnp.bfloat16)
    whole = lax.all_gather(xn, "tp", axis=1, tiled=True)
    empty = (
        jnp.zeros((rows, q_cols), jnp.float32),
        jnp.zeros((rows, kv_cols), jnp.float32),
        jnp.zeros((rows, kv_cols), jnp.float32),
    )
    pieces = (
        lax.all_gather(q_weight[0], "ctx", axis=0, tiled=True),
        lax.all_gather(k_weight[0], "ctx", axis=0, tiled=True),
        lax.all_gather(v_weight[0], "ctx", axis=0, tiled=True),
    )

    def really(values):
        return tuple(
            (jnp.dot(whole, piece, preferred_element_type=jnp.float32) for piece in pieces)
        )

    q_sum, k_sum, v_sum = lax.cond(is_attention, really, lambda values: values, empty)
    query = q_sum.astype(jnp.bfloat16).reshape(rows, kv_local, group, head_size)
    keys = k_sum.astype(jnp.bfloat16).reshape(rows, kv_local, head_size)
    values = v_sum.astype(jnp.bfloat16).reshape(rows, kv_local, head_size)
    q_pos = first + jnp.arange(rows)
    fold, initial, finish = make_fold(query, q_pos, doc_ids, ids_all, 1, head_size, is_attention)
    carry = fold(
        initial(kv_local, group),
        (
            lax.all_gather(keys, "ctx", axis=0, tiled=True),
            lax.all_gather(values, "ctx", axis=0, tiled=True),
        ),
        jnp.int32(0),
    )
    attended = finish(carry)
    attention_result = (current.astype(jnp.float32) + attended.astype(jnp.float32)).astype(
        jnp.bfloat16
    )
    ssm_local = dt_bias.shape[1]
    channels = width // ssm_local
    inputs = xn.astype(jnp.float32).reshape(rows, ssm_local, channels)
    maps, step_all = lax.psum(
        (
            jnp.dot(xn, bc_weight[0], preferred_element_type=jnp.float32),
            jnp.dot(xn, dt_weight[0], preferred_element_type=jnp.float32),
        ),
        "tp",
    )
    step = jax.nn.softplus(
        lax.dynamic_slice_in_dim(step_all, tp_pos * ssm_local, ssm_local, 1) + dt_bias[0][None, :]
    )
    state_size = maps.shape[1] // 2
    in_map = maps[:, :state_size]
    out_map = maps[:, state_size:]
    cumulative = jnp.cumsum(-step * decay_rate[0][None, :], axis=0)
    order = jnp.arange(rows)
    pairs = (doc_ids[:, None] == doc_ids[None, :]) & (order[:, None] >= order[None, :])
    exponent = jnp.where(
        pairs[:, :, None], cumulative[:, None, :] - cumulative[None, :, :], -jnp.inf
    )
    intersection = jnp.dot(out_map, in_map.T, precision=lax.Precision.HIGHEST)
    weighted = inputs * step[:, :, None]
    inner = jnp.einsum(
        "tsh,shp->thp",
        jnp.exp(exponent) * intersection[:, :, None],
        weighted,
        precision=lax.Precision.HIGHEST,
    )
    end_weight = (
        jnp.exp(cumulative[-1][None, :] - cumulative)
        * (doc_ids == doc_ids[-1]).astype(jnp.float32)[:, None]
    )
    end_state = jnp.einsum(
        "sh,sn,shp->hnp", end_weight, in_map, weighted, precision=lax.Precision.HIGHEST
    )
    total_decay = jnp.exp(cumulative[-1]) * (doc_ids[-1] == prev_id).astype(jnp.float32)

    def combine(earlier, later):
        return (earlier[0] * later[0], earlier[1] * later[0][:, None, None] + later[1])

    identity = (jnp.ones_like(total_decay), jnp.zeros_like(end_state))
    incoming = entering((total_decay, end_state), "ctx", combine, identity)[1]
    reach = jnp.exp(cumulative) * (doc_ids == prev_id).astype(jnp.float32)[:, None]
    carried = (
        jnp.einsum("tn,hnp->thp", out_map, incoming, precision=lax.Precision.HIGHEST)
        * reach[:, :, None]
    )
    outputs = inner + carried + skip_gain[0][None, :, None] * inputs
    outputs = outputs * lax.rsqrt(jnp.mean(outputs * outputs, axis=2, keepdims=True) + 1e-05)
    state_result = (current.astype(jnp.float32) + outputs.reshape(rows, width)).astype(jnp.bfloat16)
    produced = jnp.where(is_attention, attention_result, state_result)
    moved = passed_along(produced, "pipe", 1)
    return (produced[None], moved[None])


CHUNKS = 4
MESH = pl.DeviceIdType.MESH
F32 = jnp.float32
BF16 = jnp.bfloat16


def dot(a, b):
    return jnp.dot(a, b, preferred_element_type=F32)


def exact(a, b):
    return jnp.dot(a, b, preferred_element_type=F32, precision=lax.Precision.HIGHEST)


def column_of(row, count):
    same = lax.broadcasted_iota(jnp.int32, (count, count), 0) == lax.broadcasted_iota(
        jnp.int32, (count, count), 1
    )
    return jnp.sum(jnp.where(same, row, 0.0), axis=1, keepdims=True)


def kernel(
    h_hbm,
    gain_hbm,
    bc_hbm,
    dt_hbm,
    ids_hbm,
    kind_hbm,
    bias_hbm,
    rate_hbm,
    skip_hbm,
    q_hbm,
    k_hbm,
    v_hbm,
    out_hbm,
    passed_hbm,
    h_ref,
    gain_ref,
    bc_ref,
    dt_ref,
    ids_ref,
    kind_ref,
    bias_ref,
    rate_ref,
    skip_ref,
    blocks,
    weight,
    xn_ref,
    squares_out,
    squares_in,
    sums_out,
    sums_in,
    info_out,
    info_in,
    state_out,
    state_in,
    part_out,
    part_in,
    kvpart_out,
    kvpart_in,
    sums_q,
    kv_all,
    state_res,
    cols_ref,
    rows_ref,
    direct_ref,
    gram_ref,
    prod,
    prev,
    w_sem,
    ahead_sem,
    behind_sem,
    across_sem,
    b_recv,
    squares_ssem,
    squares_rsem,
    sums_ssem,
    sums_rsem,
    small_ssem,
    small_rsem,
    part_ssem,
    part_rsem,
    kvpart_sem,
    pipe_ssem,
    pipe_rsem,
    out_sem,
):
    p, c, t = lax.axis_index("pipe"), lax.axis_index("ctx"), lax.axis_index("tp")
    pipes, tps = lax.axis_size("pipe"), lax.axis_size("tp")
    oc = 1 - c
    rows, width = h_ref.shape
    step_rows = rows // CHUNKS
    heads = bias_ref.shape[1]
    pairs = heads // 2
    channels = width // heads
    n_state = bc_ref.shape[0] // 2
    half = tps // 2
    q_cols = q_hbm.shape[1]
    kv_cols = k_hbm.shape[1]
    all_cols = q_cols + 2 * kv_cols
    q_heads = q_cols // HD

    pairs_in = [
        (h_hbm, h_ref),
        (gain_hbm, gain_ref),
        (bc_hbm, bc_ref),
        (dt_hbm, dt_ref),
        (ids_hbm, ids_ref),
        (kind_hbm, kind_ref),
        (bias_hbm, bias_ref),
        (rate_hbm, rate_ref),
        (skip_hbm, skip_ref),
        (q_hbm, weight.at[:, pl.ds(0, q_cols)]),
        (k_hbm, weight.at[:, pl.ds(q_cols, kv_cols)]),
        (v_hbm, weight.at[:, pl.ds(q_cols + kv_cols, kv_cols)]),
    ]
    loads = [
        pltpu.make_async_copy(source, into, w_sem.at[n])
        for n, (source, into) in enumerate(pairs_in)
    ]
    for load in loads:
        load.start()

    barrier = pltpu.get_barrier_semaphore()
    for other in range(1, tps):
        pl.semaphore_signal(
            barrier, inc=1, device_id={"tp": lax.rem(t + other, tps)}, device_id_type=MESH
        )
    pl.semaphore_signal(barrier, inc=1, device_id={"ctx": oc}, device_id_type=MESH)

    @pl.when(p > 0)
    def _():
        pl.semaphore_signal(barrier, inc=1, device_id={"pipe": p - 1}, device_id_type=MESH)

    @pl.when(p < pipes - 1)
    def _():
        pl.semaphore_signal(barrier, inc=1, device_id={"pipe": p + 1}, device_id_type=MESH)

    loads[0].wait()
    loads[1].wait()
    hf = h_ref[...].astype(F32)
    gain = gain_ref[...]
    hg = (hf * gain).astype(BF16)
    blocks[c, t] = hg
    kv_all[...] = jnp.zeros(kv_all.shape, BF16)
    squares = jnp.sum(hf * hf, axis=1, keepdims=True)
    squares_out[...] = jnp.broadcast_to(squares, (rows, 128)).T[0:8]
    squares_in[t] = squares_out[...]

    neighbours = (p > 0).astype(jnp.int32) + (p < pipes - 1).astype(jnp.int32)
    pl.semaphore_wait(barrier, tps + neighbours)

    def span(ch):
        return pl.ds(ch * step_rows, step_rows)

    turn = 1 - 2 * c
    place = c * (tps - 1) + t * turn

    def block_at(kind, e):
        return (c if kind == "O" else oc), c * (tps - 1) + e * turn

    def block_copy(item, ch, sem, device):
        tok, b = block_at(*item)
        ref = blocks.at[tok, b, span(ch)]
        return pltpu.make_async_remote_copy(
            ref, ref, sem, b_recv.at[tok, b, ch], device_id=device, device_id_type=MESH
        )

    O0, O1, O2, O3, F0, F1 = ("O", 0), ("O", 1), ("O", 2), ("O", 3), ("F", 0), ("F", 1)
    ahead, behind = (O0, O1, F0), (O1, O2, F1)

    def ahead_copy(item, ch):
        return block_copy(item, ch, ahead_sem.at[ahead.index(item), ch], {"tp": t + turn})

    def behind_copy(item, ch):
        return block_copy(item, ch, behind_sem.at[behind.index(item), ch], {"tp": t - turn})

    def across_copy(item, ch):
        return block_copy(item, ch, across_sem.at[ch], {"ctx": oc})

    def own_sends(ch):
        @pl.when(place == 0)
        def _():
            ahead_copy(O0, ch).start()

        @pl.when(place == 1)
        def _():
            behind_copy(O1, ch).start()
            ahead_copy(O1, ch).start()

        @pl.when(place == 2)
        def _():
            across_copy(O2, ch).start()
            behind_copy(O2, ch).start()

        @pl.when(place == 3)
        def _():
            across_copy(O3, ch).start()

    def arrive(item, at, ch, then=()):
        @pl.when(place == at)
        def _():
            block_copy(item, ch, across_sem.at[ch], {"ctx": oc}).wait_recv()
            for onward in then:
                onward(item, ch).start()

    def gathered(out, into, ssem, rsem, k, mine):
        source = out.at[k] if len(out.shape) == 3 else out
        place = t if mine else k
        return pltpu.make_async_remote_copy(
            source,
            into.at[place],
            ssem.at[k],
            rsem.at[place],
            device_id={"tp": k},
            device_id_type=MESH,
        )

    def squares_copy(k, mine):
        return gathered(squares_out, squares_in, squares_ssem, squares_rsem, k, mine)

    def sums_copy(k, mine):
        return gathered(sums_out, sums_in, sums_ssem, sums_rsem, k, mine)

    peers = [lax.rem(t + other, tps) for other in range(1, tps)]
    for k in peers:
        squares_copy(k, True).start()
    for ch in range(CHUNKS // 2):
        own_sends(ch)
    for k in peers:
        squares_copy(k, False).wait_recv()
    squares = squares_in[0]
    for k in range(1, tps):
        squares = squares + squares_in[k]
    r_row = lax.rsqrt(squares / D + 1e-05)
    r_wide = jnp.broadcast_to(r_row[0:1], (128, rows)).T
    xn = (hf * r_wide[:, 0:1] * gain).astype(BF16)
    xn_ref[...] = xn
    dt_at = 2 * n_state
    for load in loads[2:9]:
        load.wait()

    def against(w):
        return lax.dot_general(w, xn, (((1,), (1,)), ((), ())), preferred_element_type=F32)

    packed = jnp.concatenate([against(bc_ref[...]), against(dt_ref[...])], axis=0)
    for k in range(tps):
        dt_row = dt_at + k * heads
        sums_out[k] = jnp.concatenate([packed[:dt_at], packed[dt_row : dt_row + heads]], axis=0)
    sums_in[t] = sums_out[t]
    for k in peers:
        sums_copy(k, True).start()
    ids_row = ids_ref[...].astype(F32)
    info_out[0:8] = r_row
    info_out[8:16] = jnp.broadcast_to(ids_row, (8, rows))
    info_copy = pltpu.make_async_remote_copy(
        info_out,
        info_in,
        small_ssem.at[0],
        small_rsem.at[0],
        device_id={"ctx": oc},
        device_id_type=MESH,
    )
    info_copy.start()
    for ch in range(CHUNKS // 2, CHUNKS):
        own_sends(ch)

    def first_arrivals(ch):
        arrive(F0, 0, ch, (ahead_copy,))
        arrive(O2, 1, ch, (behind_copy, across_copy))
        arrive(O0, 1, ch, (ahead_copy,))
        arrive(F1, 1, ch, (behind_copy,))
        arrive(O1, 2, ch, (ahead_copy,))
        arrive(O1, 0, ch)

    for ch in range(CHUNKS // 2):
        first_arrivals(ch)
    for k in peers:
        sums_copy(k, False).wait_recv()

    total = sums_in[0]
    for k in range(1, tps):
        total = total + sums_in[k]
    maps = total[:dt_at]
    drive = total[dt_at : dt_at + heads] + column_of(bias_ref[...], heads)
    step = jnp.maximum(drive, 0.0) + jnp.log1p(jnp.exp(-jnp.abs(drive)))
    upper = (
        lax.broadcasted_iota(jnp.int32, (rows, rows), 0)
        <= lax.broadcasted_iota(jnp.int32, (rows, rows), 1)
    ).astype(F32)
    cum = exact(-step * column_of(rate_ref[...], heads), upper)
    cols = jnp.concatenate(
        [
            maps,
            cum,
            r_row,
            jnp.broadcast_to(ids_row, (8, rows)),
            step,
            jnp.zeros((128 - dt_at - 2 * heads - 16, rows), F32),
        ],
        axis=0,
    ).T
    cols_ref[...] = cols
    r_at = dt_at + heads
    ids_col = cols[:, r_at + 8 : r_at + 9]
    low = lax.broadcasted_iota(jnp.int32, (rows, rows), 0) > lax.broadcasted_iota(
        jnp.int32, (rows, rows), 1
    )
    allowed = (ids_col == ids_row) & low
    gram_ref[0] = jnp.where(allowed, exact(cols[:, n_state:dt_at], maps[:n_state]), 0.0)
    in_cols, out_cols = cols[:, :n_state], cols[:, n_state:dt_at]
    own_term = jnp.sum(in_cols * out_cols, axis=1, keepdims=True)
    direct_ref[...] = cols[:, r_at + 16 : r_at + 16 + heads] * own_term + skip_ref[...]
    gram_ref[1] = jnp.where(allowed, 0.0, -1e30)
    rows_ref[0:heads] = cum
    rows_ref[heads : 2 * heads] = step
    tail = (
        jnp.exp(cum[:, rows - 1 : rows] - cum)
        * jnp.where(ids_row == ids_row[:, rows - 1 : rows], 1.0, 0.0)
        * step
    )
    left_lanes = lax.broadcasted_iota(jnp.int32, (1, 2 * channels), 1) < channels
    for i in range(pairs):
        x_pair = xn_ref[:, i * 2 * channels : (i + 1) * 2 * channels]
        weights = jnp.concatenate(
            [maps[:n_state] * tail[2 * i + k : 2 * i + k + 1] for k in range(2)], axis=0
        ).astype(BF16)
        ends = dot(weights, x_pair)
        state_out[i] = jnp.where(left_lanes, ends[:n_state], ends[n_state:]).astype(BF16)
    state_copy = pltpu.make_async_remote_copy(
        state_out,
        state_in,
        small_ssem.at[1],
        small_rsem.at[1],
        device_id={"ctx": oc},
        device_id_type=MESH,
    )
    state_copy.start()

    def state_pair(i):
        x_pair = xn_ref[:, i * 2 * channels : (i + 1) * 2 * channels]
        outs, decays = [], []
        reach = jnp.where(
            (cols_ref[:, r_at + 8 : r_at + 9] == info_in[8:9, rows - 1 : rows]) & (c > 0), 1.0, 0.0
        )
        for head in (2 * i, 2 * i + 1):
            cum_col = cols_ref[:, dt_at + head : dt_at + head + 1]
            decay = jnp.exp(cum_col - rows_ref[head : head + 1] + gram_ref[1])
            mixed = decay * gram_ref[0] * rows_ref[heads + head : heads + head + 1]
            outs.append(dot(mixed.astype(BF16), x_pair))
            decays.append(jnp.exp(cum_col) * reach)
        skips = [direct_ref[:, 2 * i + k : 2 * i + k + 1] for k in range(2)]
        carried = dot(cols_ref[:, n_state:dt_at].astype(BF16), state_in[i])
        y = (
            jnp.where(left_lanes, outs[0], outs[1])
            + carried * jnp.where(left_lanes, decays[0], decays[1])
            + jnp.where(left_lanes, skips[0], skips[1]) * x_pair.astype(F32)
        )
        squared = y * y
        first = jnp.sum(jnp.where(left_lanes, squared, 0.0), axis=1, keepdims=True)
        second = jnp.sum(jnp.where(left_lanes, 0.0, squared), axis=1, keepdims=True)
        mean = jnp.where(left_lanes, first, second) / channels
        z = y * lax.rsqrt(mean + 1e-05)
        lanes = slice(i * 2 * channels, (i + 1) * 2 * channels)
        state_res[:, lanes] = (h_ref[:, lanes].astype(F32) + z).astype(BF16)

    first_half = half * c

    def part_copy(ch):
        return pltpu.make_async_remote_copy(
            part_out.at[span(ch)],
            part_in.at[span(ch)],
            part_ssem.at[ch],
            part_rsem.at[ch],
            device_id={"ctx": oc},
            device_id_type=MESH,
        )

    def kvpart_copy():
        return pltpu.make_async_remote_copy(
            kvpart_out,
            kvpart_in,
            kvpart_sem.at[0],
            kvpart_sem.at[1],
            device_id={"ctx": oc},
            device_id_type=MESH,
        )

    early_block = block_at("F", jnp.where(place == 0, 0, 1))[1]
    late_block = block_at("F", jnp.where(place == 0, 1, 0))[1]

    def weight_rows(block, column):
        start = pl.multiple_of((block - first_half) * width, width)
        return weight[pl.ds(start, width), column : column + 256]

    first_block = block_at("O", jnp.where(place == 0, 0, 1))[1]
    second_block = block_at("O", jnp.where(place == 0, 1, 0))[1]

    def project_first():
        x = blocks[c, first_block]
        for column in range(0, all_cols, 256):
            sums_q[c, :, column : column + 256] = dot(x, weight_rows(first_block, column))

    def project_second():
        x = blocks[c, second_block]
        for column in (*range(q_cols, all_cols, 256), *range(0, q_cols, 256)):
            lanes = slice(column, column + 256)
            value = sums_q[c, :, lanes] + dot(x, weight_rows(second_block, column))
            sums_q[c, :, lanes] = value
            if column == q_cols:
                kvpart_out[...] = value.astype(BF16)
                kvpart_copy().start()

    def project_early():
        x = blocks[oc, early_block]
        for column in range(0, all_cols, 256):
            sums_q[oc, :, column : column + 256] = dot(x, weight_rows(early_block, column))

    def project_late(ch):
        x = blocks[oc, late_block, span(ch)]
        for column in range(0, all_cols, 256):
            lanes = slice(column, column + 256)
            value = sums_q[oc, span(ch), lanes] + dot(x, weight_rows(late_block, column))
            part_out[span(ch), lanes] = value.astype(BF16)
            if column == q_cols:
                sums_q[oc, span(ch), lanes] = value
        part_copy(ch).start()

    for ch in range(CHUNKS // 2, CHUNKS):
        first_arrivals(ch)
    info_copy.wait_recv()
    state_copy.wait_recv()
    done = 0

    def state_until(upto):
        for i in range(done, upto):
            state_pair(i)
        return upto

    for ch in range(CHUNKS):
        arrive(O2, 0, ch, (across_copy,))
        arrive(F0, 1, ch, (ahead_copy,))
        arrive(O0, 2, ch, (ahead_copy,))
        arrive(O1, 3, ch)
        done = state_until(pairs * (ch + 1) // (2 * CHUNKS))
    for load in loads[9:]:
        load.wait()
    project_first()
    for ch in range(CHUNKS):
        arrive(F0, 2, ch, (ahead_copy,))
        done = state_until(pairs * (CHUNKS + ch + 1) // (2 * CHUNKS))
    for ch in range(CHUNKS):
        arrive(O0, 3, ch)
    project_second()
    for ch in range(CHUNKS):
        arrive(F1, 2, ch)
        arrive(F1, 3, ch)
    project_early()
    for ch in range(CHUNKS):
        arrive(F1, 0, ch)
        arrive(F0, 3, ch)
        project_late(ch)

    kvpart_copy().wait_recv()
    their_r = jnp.broadcast_to(info_in[0:1], (128, rows)).T[:, 0:1]
    kv_all[oc] = ((sums_q[oc, :, q_cols:] + kvpart_in[...].astype(F32)) * their_r).astype(BF16)
    my_ids, their_ids = ids_row, info_in[8:9]
    at_first = jnp.where(c == 0, my_ids, their_ids)
    at_second = jnp.where(c == 0, their_ids, my_ids)
    key_ids = jnp.concatenate([at_first, at_second], axis=1)
    key_pos = lax.broadcasted_iota(jnp.int32, (step_rows, 2 * rows), 1)
    query_at = lax.broadcasted_iota(jnp.int32, (step_rows, 2 * rows), 0)
    attention = jnp.broadcast_to(kind_ref[...] == 1, (step_rows, width))

    def pipe_copy(ch):
        return pltpu.make_async_remote_copy(
            prod.at[ch],
            prev.at[ch],
            pipe_ssem.at[ch],
            pipe_rsem.at[ch],
            device_id={"pipe": p + 1},
            device_id_type=MESH,
        )

    def out_copy(ch):
        return pltpu.make_async_copy(prod.at[ch], out_hbm.at[span(ch)], out_sem.at[0, ch])

    def passed_copy(ch):
        return pltpu.make_async_copy(prev.at[ch], passed_hbm.at[span(ch)], out_sem.at[1, ch])

    for ch in range(CHUNKS):
        part_copy(ch).wait_recv()
        here = slice(ch * step_rows, (ch + 1) * step_rows)
        ours = sums_q[c, span(ch)] + part_in[span(ch)].astype(F32)
        ours = (ours * cols_ref[here, r_at : r_at + 1]).astype(BF16)
        kv_all[c, span(ch)] = ours[:, q_cols:]
        query = jnp.concatenate(
            [ours[:, head * HD : (head + 1) * HD] for head in range(q_heads)], axis=0
        )
        keys = kv_all[:, :, :HD].reshape(2 * rows, HD)
        values = kv_all[:, :, HD:].reshape(2 * rows, HD)
        scores = lax.dot_general(
            query, keys, (((1,), (1,)), ((), ())), preferred_element_type=F32
        ) * (HD ** (-0.5))
        wanted = (key_pos <= c * rows + ch * step_rows + query_at) & (
            key_ids == cols_ref[here, r_at + 8 : r_at + 9]
        )
        barred = jnp.where(wanted, 0.0, -1e30)
        scores = scores + jnp.concatenate([barred] * q_heads, axis=0)
        top = jnp.max(scores, axis=1, keepdims=True)
        probs = jnp.exp(scores - top)
        denom = jnp.sum(probs, axis=1, keepdims=True)
        mixed = (dot(probs.astype(BF16), values) / denom).astype(BF16).astype(F32)
        attended = jnp.concatenate(
            [mixed[head * step_rows : (head + 1) * step_rows] for head in range(q_heads)], axis=1
        )
        attended = (h_ref[span(ch)].astype(F32) + attended).astype(BF16).astype(F32)
        prod[ch] = jnp.where(attention, attended, state_res[span(ch)].astype(F32)).astype(BF16)
        out_copy(ch).start()

        @pl.when(p < pipes - 1)
        def _(ch=ch):
            pipe_copy(ch).start()

    for ch in range(CHUNKS):
        across_copy(O2, ch).wait_send()

        @pl.when(place < 3)
        def _(ch=ch):
            ahead_copy(F0, ch).wait_send()
            ahead_copy(O0, ch).wait_send()

        @pl.when((place == 1) | (place == 2))
        def _(ch=ch):
            ahead_copy(O1, ch).wait_send()
            behind_copy(O2, ch).wait_send()

        @pl.when(place == 1)
        def _(ch=ch):
            behind_copy(O1, ch).wait_send()
            behind_copy(F1, ch).wait_send()

        part_copy(ch).wait_send()
    kvpart_copy().wait_send()
    for k in peers:
        squares_copy(k, True).wait_send()
        sums_copy(k, True).wait_send()
    info_copy.wait_send()
    state_copy.wait_send()

    @pl.when(p == 0)
    def _():
        prev[...] = jnp.zeros(prev.shape, BF16)

    for k in range(CHUNKS):

        @pl.when(p > 0)
        def _(k=k):
            pipe_copy(k).wait_recv()

        passed_copy(k).start()
    for k in range(CHUNKS):
        out_copy(k).wait()
        passed_copy(k).wait()

    @pl.when(p < pipes - 1)
    def _():
        for k in range(CHUNKS):
            pipe_copy(k).wait_send()


def deliver(out_from, passed_from, out_to, passed_to, held, sem):
    rows = held.shape[1] // 2
    arriving, leaving = [], []
    for n, (source, into) in enumerate(((out_from, out_to), (passed_from, passed_to))):
        for k in range(2):
            part = pl.ds(k * rows, rows)
            place = held.at[n, part]
            arriving.append(pltpu.make_async_copy(source.at[part], place, sem.at[0, n, k]))
            leaving.append(pltpu.make_async_copy(place, into.at[part], sem.at[1, n, k]))
    for copy in arriving:
        copy.start()
    for before, after in zip(arriving, leaving):
        before.wait()
        after.start()
    for copy in leaving:
        copy.wait()


def fused(
    hidden_in,
    doc_ids,
    layer_kind,
    norm_gain,
    q_weight,
    k_weight,
    v_weight,
    bc_weight,
    dt_weight,
    dt_bias,
    decay_rate,
    skip_gain,
):
    _, rows, width = hidden_in.shape
    depth, q_cols = q_weight.shape[1:]
    kv_cols = k_weight.shape[2]
    heads = dt_bias.shape[1]
    n_state = bc_weight.shape[2] // 2
    tps = lax.axis_size("tp")
    anywhere = pl.BlockSpec(memory_space=pl.ANY)
    small = 2 * n_state + heads
    dma = pltpu.SemaphoreType.DMA
    shape = jax.ShapeDtypeStruct((rows, width), BF16)
    out, passed = pl.pallas_call(
        kernel,
        out_shape=(shape, shape),
        in_specs=[anywhere] * 12,
        out_specs=(anywhere, anywhere),
        scratch_shapes=[
            pltpu.VMEM((rows, width), BF16),
            pltpu.VMEM((1, width), F32),
            pltpu.VMEM((2 * n_state, width), BF16),
            pltpu.VMEM((heads * tps, width), BF16),
            pltpu.VMEM((1, rows), jnp.int32),
            pltpu.VMEM((1, 1), jnp.int32),
            pltpu.VMEM((1, heads), F32),
            pltpu.VMEM((1, heads), F32),
            pltpu.VMEM((1, heads), F32),
            pltpu.VMEM((2, tps, rows, width), BF16),
            pltpu.VMEM((depth, q_cols + 2 * kv_cols), BF16),
            pltpu.VMEM((rows, width), BF16),
            pltpu.VMEM((8, rows), F32),
            pltpu.VMEM((tps, 8, rows), F32),
            pltpu.VMEM((tps, small, rows), F32),
            pltpu.VMEM((tps, small, rows), F32),
            pltpu.VMEM((16, rows), F32),
            pltpu.VMEM((16, rows), F32),
            pltpu.VMEM((heads // 2, n_state, 2 * width // heads), BF16),
            pltpu.VMEM((heads // 2, n_state, 2 * width // heads), BF16),
            pltpu.VMEM((rows, q_cols + 2 * kv_cols), BF16),
            pltpu.VMEM((rows, q_cols + 2 * kv_cols), BF16),
            pltpu.VMEM((rows, 2 * kv_cols), BF16),
            pltpu.VMEM((rows, 2 * kv_cols), BF16),
            pltpu.VMEM((2, rows, q_cols + 2 * kv_cols), F32),
            pltpu.VMEM((2, rows, 2 * kv_cols), BF16),
            pltpu.VMEM((rows, width), BF16),
            pltpu.VMEM((rows, 128), F32),
            pltpu.VMEM((2 * heads, rows), F32),
            pltpu.VMEM((rows, heads), F32),
            pltpu.VMEM((2, rows, rows), F32),
            pltpu.VMEM((CHUNKS, rows // CHUNKS, width), BF16),
            pltpu.VMEM((CHUNKS, rows // CHUNKS, width), BF16),
            dma((12,)),
            dma((3, CHUNKS)),
            dma((3, CHUNKS)),
            dma((CHUNKS,)),
            dma((2, tps, CHUNKS)),
            dma((tps,)),
            dma((tps,)),
            dma((tps,)),
            dma((tps,)),
            dma((2,)),
            dma((2,)),
            dma((CHUNKS,)),
            dma((CHUNKS,)),
            dma((2,)),
            dma((CHUNKS,)),
            dma((CHUNKS,)),
            dma((2, CHUNKS)),
        ],
        compiler_params=pltpu.CompilerParams(
            collective_id=0, has_side_effects=True, vmem_limit_bytes=60 * 2**20
        ),
        cost_estimate=pl.CostEstimate(
            flops=4 * rows * depth * (q_cols + 2 * kv_cols),
            bytes_accessed=2 * depth * (q_cols + 2 * kv_cols),
            transcendentals=0,
        ),
    )(
        hidden_in[0],
        norm_gain,
        bc_weight[0].T,
        dt_weight[0].T,
        doc_ids[None],
        layer_kind[None],
        dt_bias,
        decay_rate,
        skip_gain,
        q_weight[0],
        k_weight[0],
        v_weight[0],
    )
    out, passed = pl.pallas_call(
        deliver,
        out_shape=(shape, shape),
        in_specs=[anywhere] * 2,
        out_specs=(anywhere, anywhere),
        scratch_shapes=[pltpu.VMEM((2, rows, width), BF16), dma((2, 2, 2))],
        compiler_params=pltpu.CompilerParams(vmem_limit_bytes=60 * 2**20),
    )(out, passed)
    return out[None], passed[None]


def solution(mesh):
    in_specs = (
        P("pipe", "ctx", "tp"),
        P("ctx"),
        P("pipe"),
        P("pipe", "tp"),
        P("pipe", "ctx", "tp"),
        P("pipe", "ctx", "tp"),
        P("pipe", "ctx", "tp"),
        P("pipe", "tp", None),
        P("pipe", "tp", None),
        P("pipe", "tp"),
        P("pipe", "tp"),
        P("pipe", "tp"),
    )
    out_specs = (P("pipe", "ctx", "tp"), P("pipe", "ctx", "tp"))
    body = fused if mesh.shape["ctx"] == 2 and mesh.shape["tp"] == 4 else shards
    return jax.shard_map(body, mesh=mesh, in_specs=in_specs, out_specs=out_specs, check_vma=False)
```

```python
import jax
import jax.numpy as jnp
from jax import lax
from jax.experimental import pallas as pl
from jax.experimental.pallas import tpu as pltpu
from jax.sharding import PartitionSpec as P

D = 4096
HD = 128


def entering(x, axis, combine, identity):
    devices, index = (lax.axis_size(axis), lax.axis_index(axis))
    everything = jax.tree.map(
        lambda part, kind: lax.all_gather(part.astype(kind), axis), x, (jnp.bfloat16, jnp.bfloat16)
    )
    start = jax.tree.map(
        lambda part, zero: jnp.broadcast_to(jnp.asarray(zero, part.dtype), part.shape), x, identity
    )

    def turn(k, before):
        reached = k < index
        new = combine(
            before, jax.tree.map(lambda part, own: part[k].astype(own.dtype), everything, x)
        )
        return jax.tree.map(lambda a, b: jnp.where(reached, a, b), new, before)

    return lax.fori_loop(0, devices, turn, start)


def passed_along(x, axis, by):
    devices = lax.axis_size(axis)
    pairs = [(i, i + by) for i in range(devices) if 0 <= i + by < devices]
    return lax.ppermute(x, axis, pairs)


def make_fold(q_rows, q_pos, q_ids, ids_all, groups, head_size, active):
    rows = q_rows.shape[0]
    gsize = rows // groups
    q_top = jnp.max(q_pos.reshape(groups, gsize), axis=1)
    scale = head_size ** (-0.5)

    def update(state, piece_k, piece_v, key_pos, key_ids):
        top, denom, total = state
        scores = (
            jnp.einsum("tkjd,skd->kjts", q_rows, piece_k, preferred_element_type=jnp.float32)
            * scale
        )
        allowed = (key_pos[None, :] <= q_pos[:, None]) & (key_ids[None, :] == q_ids[:, None])
        scores = jnp.where(allowed[None, None], scores, -1e30)
        new_top = jnp.maximum(top, jnp.max(scores, axis=-1))
        probs = jnp.where(allowed[None, None], jnp.exp(scores - new_top[..., None]), 0.0)
        factor = jnp.exp(top - new_top)
        denom = denom * factor + jnp.sum(probs, axis=-1)
        total = total * factor[..., None] + jnp.einsum(
            "kjts,skd->kjtd",
            probs.astype(jnp.bfloat16),
            piece_v,
            preferred_element_type=jnp.float32,
        )
        return (new_top, denom, total)

    def fold(carry, piece, start):
        piece_k, piece_v = piece
        count = piece_k.shape[0]
        block = 512 if count % 512 == 0 else count
        for offset in range(0, count, block):
            key_start = start + offset
            key_pos = key_start + jnp.arange(block)
            key_ids = lax.dynamic_slice_in_dim(ids_all, key_start, block)
            block_k = piece_k[offset : offset + block]
            block_v = piece_v[offset : offset + block]
            low = 0

            def compute(state, low=low):
                return update(state, block_k, block_v, key_pos, key_ids)

            wanted = jnp.logical_and(active, key_start <= q_top[0])
            updated = [lax.cond(wanted, compute, lambda state: state, carry[0])]
            carry = tuple(updated)
        return carry

    def initial(kv_count, group):
        return tuple(
            (
                (
                    jnp.full((kv_count, group, gsize), -1e30, jnp.float32),
                    jnp.zeros((kv_count, group, gsize), jnp.float32),
                    jnp.zeros((kv_count, group, gsize, head_size), jnp.float32),
                )
                for index in range(groups)
            )
        )

    def finish(carry):
        parts = [
            total / jnp.where(denom > 0.0, denom, 1.0)[..., None] for top, denom, total in carry
        ]
        joined = parts[0]
        kv_count, group = (joined.shape[0], joined.shape[1])
        return (
            jnp.transpose(joined, (2, 0, 1, 3))
            .reshape(rows, kv_count * group * head_size)
            .astype(jnp.bfloat16)
        )

    return (fold, initial, finish)


def shards(
    hidden_in,
    doc_ids,
    layer_kind,
    norm_gain,
    q_weight,
    k_weight,
    v_weight,
    bc_weight,
    dt_weight,
    dt_bias,
    decay_rate,
    skip_gain,
):
    current = hidden_in[0]
    rows, width = current.shape
    ctx_pos = lax.axis_index("ctx")
    tp_pos = lax.axis_index("tp")
    ids_all = lax.all_gather(doc_ids, "ctx", axis=0, tiled=True)
    first = ctx_pos * rows
    prev_id = jnp.where(
        ctx_pos > 0,
        lax.dynamic_index_in_dim(ids_all, jnp.maximum(first - 1, 0), 0, keepdims=False),
        -1,
    )
    gain = norm_gain[0]
    head_size = HD
    q_cols = q_weight.shape[2]
    kv_cols = k_weight.shape[2]
    heads_local = q_cols // head_size
    kv_local = kv_cols // head_size
    group = heads_local // kv_local
    is_attention = layer_kind[0] == 1
    hf = current.astype(jnp.float32)
    squares = lax.psum(jnp.sum(hf * hf, axis=1), "tp")
    xn = (hf * lax.rsqrt(squares / D + 1e-05)[:, None] * gain[None, :]).astype(jnp.bfloat16)
    whole = lax.all_gather(xn, "tp", axis=1, tiled=True)
    empty = (
        jnp.zeros((rows, q_cols), jnp.float32),
        jnp.zeros((rows, kv_cols), jnp.float32),
        jnp.zeros((rows, kv_cols), jnp.float32),
    )
    pieces = (
        lax.all_gather(q_weight[0], "ctx", axis=0, tiled=True),
        lax.all_gather(k_weight[0], "ctx", axis=0, tiled=True),
        lax.all_gather(v_weight[0], "ctx", axis=0, tiled=True),
    )

    def really(values):
        return tuple(
            (jnp.dot(whole, piece, preferred_element_type=jnp.float32) for piece in pieces)
        )

    q_sum, k_sum, v_sum = lax.cond(is_attention, really, lambda values: values, empty)
    query = q_sum.astype(jnp.bfloat16).reshape(rows, kv_local, group, head_size)
    keys = k_sum.astype(jnp.bfloat16).reshape(rows, kv_local, head_size)
    values = v_sum.astype(jnp.bfloat16).reshape(rows, kv_local, head_size)
    q_pos = first + jnp.arange(rows)
    fold, initial, finish = make_fold(query, q_pos, doc_ids, ids_all, 1, head_size, is_attention)
    carry = fold(
        initial(kv_local, group),
        (
            lax.all_gather(keys, "ctx", axis=0, tiled=True),
            lax.all_gather(values, "ctx", axis=0, tiled=True),
        ),
        jnp.int32(0),
    )
    attended = finish(carry)
    attention_result = (current.astype(jnp.float32) + attended.astype(jnp.float32)).astype(
        jnp.bfloat16
    )
    ssm_local = dt_bias.shape[1]
    channels = width // ssm_local
    inputs = xn.astype(jnp.float32).reshape(rows, ssm_local, channels)
    maps, step_all = lax.psum(
        (
            jnp.dot(xn, bc_weight[0], preferred_element_type=jnp.float32),
            jnp.dot(xn, dt_weight[0], preferred_element_type=jnp.float32),
        ),
        "tp",
    )
    step = jax.nn.softplus(
        lax.dynamic_slice_in_dim(step_all, tp_pos * ssm_local, ssm_local, 1) + dt_bias[0][None, :]
    )
    state_size = maps.shape[1] // 2
    in_map = maps[:, :state_size]
    out_map = maps[:, state_size:]
    cumulative = jnp.cumsum(-step * decay_rate[0][None, :], axis=0)
    order = jnp.arange(rows)
    pairs = (doc_ids[:, None] == doc_ids[None, :]) & (order[:, None] >= order[None, :])
    exponent = jnp.where(
        pairs[:, :, None], cumulative[:, None, :] - cumulative[None, :, :], -jnp.inf
    )
    intersection = jnp.dot(out_map, in_map.T, precision=lax.Precision.HIGHEST)
    weighted = inputs * step[:, :, None]
    inner = jnp.einsum(
        "tsh,shp->thp",
        jnp.exp(exponent) * intersection[:, :, None],
        weighted,
        precision=lax.Precision.HIGHEST,
    )
    end_weight = (
        jnp.exp(cumulative[-1][None, :] - cumulative)
        * (doc_ids == doc_ids[-1]).astype(jnp.float32)[:, None]
    )
    end_state = jnp.einsum(
        "sh,sn,shp->hnp", end_weight, in_map, weighted, precision=lax.Precision.HIGHEST
    )
    total_decay = jnp.exp(cumulative[-1]) * (doc_ids[-1] == prev_id).astype(jnp.float32)

    def combine(earlier, later):
        return (earlier[0] * later[0], earlier[1] * later[0][:, None, None] + later[1])

    identity = (jnp.ones_like(total_decay), jnp.zeros_like(end_state))
    incoming = entering((total_decay, end_state), "ctx", combine, identity)[1]
    reach = jnp.exp(cumulative) * (doc_ids == prev_id).astype(jnp.float32)[:, None]
    carried = (
        jnp.einsum("tn,hnp->thp", out_map, incoming, precision=lax.Precision.HIGHEST)
        * reach[:, :, None]
    )
    outputs = inner + carried + skip_gain[0][None, :, None] * inputs
    outputs = outputs * lax.rsqrt(jnp.mean(outputs * outputs, axis=2, keepdims=True) + 1e-05)
    state_result = (current.astype(jnp.float32) + outputs.reshape(rows, width)).astype(jnp.bfloat16)
    produced = jnp.where(is_attention, attention_result, state_result)
    moved = passed_along(produced, "pipe", 1)
    return (produced[None], moved[None])


CHUNKS = 4
MESH = pl.DeviceIdType.MESH
F32 = jnp.float32
BF16 = jnp.bfloat16


def dot(a, b):
    return jnp.dot(a, b, preferred_element_type=F32)


def exact(a, b):
    return jnp.dot(a, b, preferred_element_type=F32, precision=lax.Precision.HIGHEST)


def column_of(row, count):
    same = lax.broadcasted_iota(jnp.int32, (count, count), 0) == lax.broadcasted_iota(
        jnp.int32, (count, count), 1
    )
    return jnp.sum(jnp.where(same, row, 0.0), axis=1, keepdims=True)


def kernel(
    h_hbm,
    gain_hbm,
    bc_hbm,
    dt_hbm,
    ids_hbm,
    kind_hbm,
    bias_hbm,
    rate_hbm,
    skip_hbm,
    q_hbm,
    k_hbm,
    v_hbm,
    out_hbm,
    passed_hbm,
    h_ref,
    gain_ref,
    bc_ref,
    dt_ref,
    ids_ref,
    kind_ref,
    bias_ref,
    rate_ref,
    skip_ref,
    blocks,
    weight,
    xn_ref,
    squares_out,
    squares_in,
    sums_out,
    sums_in,
    info_out,
    info_in,
    state_out,
    state_in,
    part_out,
    part_in,
    kvpart_out,
    kvpart_in,
    sums_q,
    kv_all,
    state_res,
    cols_ref,
    rows_ref,
    direct_ref,
    gram_ref,
    prod,
    prev,
    w_sem,
    ahead_sem,
    behind_sem,
    across_sem,
    b_recv,
    squares_ssem,
    squares_rsem,
    sums_ssem,
    sums_rsem,
    small_ssem,
    small_rsem,
    part_ssem,
    part_rsem,
    kvpart_sem,
    pipe_ssem,
    pipe_rsem,
    out_sem,
):
    p, c, t = lax.axis_index("pipe"), lax.axis_index("ctx"), lax.axis_index("tp")
    pipes, tps = lax.axis_size("pipe"), lax.axis_size("tp")
    oc = 1 - c
    rows, width = h_ref.shape
    step_rows = rows // CHUNKS
    heads = bias_ref.shape[1]
    pairs = heads // 2
    channels = width // heads
    n_state = bc_ref.shape[0] // 2
    half = tps // 2
    q_cols = q_hbm.shape[1]
    kv_cols = k_hbm.shape[1]
    all_cols = q_cols + 2 * kv_cols
    q_heads = q_cols // HD

    pairs_in = [
        (h_hbm, h_ref),
        (gain_hbm, gain_ref),
        (bc_hbm, bc_ref),
        (dt_hbm, dt_ref),
        (ids_hbm, ids_ref),
        (kind_hbm, kind_ref),
        (bias_hbm, bias_ref),
        (rate_hbm, rate_ref),
        (skip_hbm, skip_ref),
        (q_hbm, weight.at[:, pl.ds(0, q_cols)]),
        (k_hbm, weight.at[:, pl.ds(q_cols, kv_cols)]),
        (v_hbm, weight.at[:, pl.ds(q_cols + kv_cols, kv_cols)]),
    ]
    loads = [
        pltpu.make_async_copy(source, into, w_sem.at[n])
        for n, (source, into) in enumerate(pairs_in)
    ]
    for load in loads:
        load.start()

    barrier = pltpu.get_barrier_semaphore()
    for other in range(1, tps):
        pl.semaphore_signal(
            barrier, inc=1, device_id={"tp": lax.rem(t + other, tps)}, device_id_type=MESH
        )
    pl.semaphore_signal(barrier, inc=1, device_id={"ctx": oc}, device_id_type=MESH)

    @pl.when(p > 0)
    def _():
        pl.semaphore_signal(barrier, inc=1, device_id={"pipe": p - 1}, device_id_type=MESH)

    @pl.when(p < pipes - 1)
    def _():
        pl.semaphore_signal(barrier, inc=1, device_id={"pipe": p + 1}, device_id_type=MESH)

    loads[0].wait()
    loads[1].wait()
    hf = h_ref[...].astype(F32)
    gain = gain_ref[...]
    hg = (hf * gain).astype(BF16)
    blocks[c, t] = hg
    kv_all[...] = jnp.zeros(kv_all.shape, BF16)
    squares = jnp.sum(hf * hf, axis=1, keepdims=True)
    squares_out[...] = jnp.broadcast_to(squares, (rows, 128)).T[0:8]
    squares_in[t] = squares_out[...]

    neighbours = (p > 0).astype(jnp.int32) + (p < pipes - 1).astype(jnp.int32)
    pl.semaphore_wait(barrier, tps + neighbours)

    def span(ch):
        return pl.ds(ch * step_rows, step_rows)

    turn = 1 - 2 * c
    place = c * (tps - 1) + t * turn

    def block_at(kind, e):
        return (c if kind == "O" else oc), c * (tps - 1) + e * turn

    def block_copy(item, ch, sem, device):
        tok, b = block_at(*item)
        ref = blocks.at[tok, b, span(ch)]
        return pltpu.make_async_remote_copy(
            ref, ref, sem, b_recv.at[tok, b, ch], device_id=device, device_id_type=MESH
        )

    O0, O1, O2, O3, F0, F1 = ("O", 0), ("O", 1), ("O", 2), ("O", 3), ("F", 0), ("F", 1)
    ahead, behind = (O0, O1, F0), (O1, O2, F1)

    def ahead_copy(item, ch):
        return block_copy(item, ch, ahead_sem.at[ahead.index(item), ch], {"tp": t + turn})

    def behind_copy(item, ch):
        return block_copy(item, ch, behind_sem.at[behind.index(item), ch], {"tp": t - turn})

    def across_copy(item, ch):
        return block_copy(item, ch, across_sem.at[ch], {"ctx": oc})

    def own_sends(ch):
        @pl.when(place == 0)
        def _():
            ahead_copy(O0, ch).start()

        @pl.when(place == 1)
        def _():
            behind_copy(O1, ch).start()
            ahead_copy(O1, ch).start()

        @pl.when(place == 2)
        def _():
            across_copy(O2, ch).start()
            behind_copy(O2, ch).start()

        @pl.when(place == 3)
        def _():
            across_copy(O3, ch).start()

    def arrive(item, at, ch, then=()):
        @pl.when(place == at)
        def _():
            block_copy(item, ch, across_sem.at[ch], {"ctx": oc}).wait_recv()
            for onward in then:
                onward(item, ch).start()

    def gathered(out, into, ssem, rsem, k, mine):
        source = out.at[k] if len(out.shape) == 3 else out
        place = t if mine else k
        return pltpu.make_async_remote_copy(
            source,
            into.at[place],
            ssem.at[k],
            rsem.at[place],
            device_id={"tp": k},
            device_id_type=MESH,
        )

    def squares_copy(k, mine):
        return gathered(squares_out, squares_in, squares_ssem, squares_rsem, k, mine)

    def sums_copy(k, mine):
        return gathered(sums_out, sums_in, sums_ssem, sums_rsem, k, mine)

    peers = [lax.rem(t + other, tps) for other in range(1, tps)]
    for k in peers:
        squares_copy(k, True).start()
    for ch in range(CHUNKS // 2):
        own_sends(ch)
    for k in peers:
        squares_copy(k, False).wait_recv()
    squares = squares_in[0]
    for k in range(1, tps):
        squares = squares + squares_in[k]
    r_row = lax.rsqrt(squares / D + 1e-05)
    r_wide = jnp.broadcast_to(r_row[0:1], (128, rows)).T
    xn = (hf * r_wide[:, 0:1] * gain).astype(BF16)
    xn_ref[...] = xn
    dt_at = 2 * n_state
    for load in loads[2:9]:
        load.wait()

    def against(w):
        return lax.dot_general(w, xn, (((1,), (1,)), ((), ())), preferred_element_type=F32)

    packed = jnp.concatenate([against(bc_ref[...]), against(dt_ref[...])], axis=0)
    for k in range(tps):
        dt_row = dt_at + k * heads
        sums_out[k] = jnp.concatenate([packed[:dt_at], packed[dt_row : dt_row + heads]], axis=0)
    sums_in[t] = sums_out[t]
    for k in peers:
        sums_copy(k, True).start()
    ids_row = ids_ref[...].astype(F32)
    info_out[0:8] = r_row
    info_out[8:16] = jnp.broadcast_to(ids_row, (8, rows))
    info_copy = pltpu.make_async_remote_copy(
        info_out,
        info_in,
        small_ssem.at[0],
        small_rsem.at[0],
        device_id={"ctx": oc},
        device_id_type=MESH,
    )
    info_copy.start()
    for ch in range(CHUNKS // 2, CHUNKS):
        own_sends(ch)

    def first_arrivals(ch):
        arrive(F0, 0, ch, (ahead_copy,))
        arrive(O2, 1, ch, (behind_copy, across_copy))
        arrive(O0, 1, ch, (ahead_copy,))
        arrive(F1, 1, ch, (behind_copy,))
        arrive(O1, 2, ch, (ahead_copy,))
        arrive(O1, 0, ch)

    for ch in range(CHUNKS // 2):
        first_arrivals(ch)
    for k in peers:
        sums_copy(k, False).wait_recv()
    first_arrivals(CHUNKS // 2)

    total = sums_in[0]
    for k in range(1, tps):
        total = total + sums_in[k]
    maps = total[:dt_at]
    drive = total[dt_at : dt_at + heads] + column_of(bias_ref[...], heads)
    step = jnp.maximum(drive, 0.0) + jnp.log1p(jnp.exp(-jnp.abs(drive)))
    upper = (
        lax.broadcasted_iota(jnp.int32, (rows, rows), 0)
        <= lax.broadcasted_iota(jnp.int32, (rows, rows), 1)
    ).astype(F32)
    cum = exact(-step * column_of(rate_ref[...], heads), upper)
    cols = jnp.concatenate(
        [
            maps,
            cum,
            r_row,
            jnp.broadcast_to(ids_row, (8, rows)),
            step,
            jnp.zeros((128 - dt_at - 2 * heads - 16, rows), F32),
        ],
        axis=0,
    ).T
    cols_ref[...] = cols
    r_at = dt_at + heads
    ids_col = cols[:, r_at + 8 : r_at + 9]
    low = lax.broadcasted_iota(jnp.int32, (rows, rows), 0) > lax.broadcasted_iota(
        jnp.int32, (rows, rows), 1
    )
    allowed = (ids_col == ids_row) & low
    gram_ref[0] = jnp.where(allowed, exact(cols[:, n_state:dt_at], maps[:n_state]), 0.0)
    in_cols, out_cols = cols[:, :n_state], cols[:, n_state:dt_at]
    own_term = jnp.sum(in_cols * out_cols, axis=1, keepdims=True)
    direct_ref[...] = cols[:, r_at + 16 : r_at + 16 + heads] * own_term + skip_ref[...]
    gram_ref[1] = jnp.where(allowed, 0.0, -1e30)
    rows_ref[0:heads] = cum
    rows_ref[heads : 2 * heads] = step
    tail = (
        jnp.exp(cum[:, rows - 1 : rows] - cum)
        * jnp.where(ids_row == ids_row[:, rows - 1 : rows], 1.0, 0.0)
        * step
    )
    left_lanes = lax.broadcasted_iota(jnp.int32, (1, 2 * channels), 1) < channels
    for i in range(pairs):
        x_pair = xn_ref[:, i * 2 * channels : (i + 1) * 2 * channels]
        weights = jnp.concatenate(
            [maps[:n_state] * tail[2 * i + k : 2 * i + k + 1] for k in range(2)], axis=0
        ).astype(BF16)
        ends = dot(weights, x_pair)
        state_out[i] = jnp.where(left_lanes, ends[:n_state], ends[n_state:]).astype(BF16)
    state_copy = pltpu.make_async_remote_copy(
        state_out,
        state_in,
        small_ssem.at[1],
        small_rsem.at[1],
        device_id={"ctx": oc},
        device_id_type=MESH,
    )
    state_copy.start()

    def state_pair(i):
        x_pair = xn_ref[:, i * 2 * channels : (i + 1) * 2 * channels]
        outs, decays = [], []
        reach = jnp.where(
            (cols_ref[:, r_at + 8 : r_at + 9] == info_in[8:9, rows - 1 : rows]) & (c > 0), 1.0, 0.0
        )
        for head in (2 * i, 2 * i + 1):
            cum_col = cols_ref[:, dt_at + head : dt_at + head + 1]
            decay = jnp.exp(cum_col - rows_ref[head : head + 1] + gram_ref[1])
            mixed = decay * gram_ref[0] * rows_ref[heads + head : heads + head + 1]
            outs.append(dot(mixed.astype(BF16), x_pair))
            decays.append(jnp.exp(cum_col) * reach)
        skips = [direct_ref[:, 2 * i + k : 2 * i + k + 1] for k in range(2)]
        carried = dot(cols_ref[:, n_state:dt_at].astype(BF16), state_in[i])
        y = (
            jnp.where(left_lanes, outs[0], outs[1])
            + carried * jnp.where(left_lanes, decays[0], decays[1])
            + jnp.where(left_lanes, skips[0], skips[1]) * x_pair.astype(F32)
        )
        squared = y * y
        first = jnp.sum(jnp.where(left_lanes, squared, 0.0), axis=1, keepdims=True)
        second = jnp.sum(jnp.where(left_lanes, 0.0, squared), axis=1, keepdims=True)
        mean = jnp.where(left_lanes, first, second) / channels
        z = y * lax.rsqrt(mean + 1e-05)
        lanes = slice(i * 2 * channels, (i + 1) * 2 * channels)
        state_res[:, lanes] = (h_ref[:, lanes].astype(F32) + z).astype(BF16)

    first_half = half * c

    def part_copy(ch):
        return pltpu.make_async_remote_copy(
            part_out.at[span(ch)],
            part_in.at[span(ch)],
            part_ssem.at[ch],
            part_rsem.at[ch],
            device_id={"ctx": oc},
            device_id_type=MESH,
        )

    def kvpart_copy():
        return pltpu.make_async_remote_copy(
            kvpart_out,
            kvpart_in,
            kvpart_sem.at[0],
            kvpart_sem.at[1],
            device_id={"ctx": oc},
            device_id_type=MESH,
        )

    early_block = block_at("F", jnp.where(place == 0, 0, 1))[1]
    late_block = block_at("F", jnp.where(place == 0, 1, 0))[1]

    def weight_rows(block, column):
        start = pl.multiple_of((block - first_half) * width, width)
        return weight[pl.ds(start, width), column : column + 256]

    first_block = block_at("O", jnp.where(place == 0, 0, 1))[1]
    second_block = block_at("O", jnp.where(place == 0, 1, 0))[1]

    def project_first():
        x = blocks[c, first_block]
        for column in range(0, all_cols, 256):
            sums_q[c, :, column : column + 256] = dot(x, weight_rows(first_block, column))

    def project_second():
        x = blocks[c, second_block]
        for column in (*range(q_cols, all_cols, 256), *range(0, q_cols, 256)):
            lanes = slice(column, column + 256)
            value = sums_q[c, :, lanes] + dot(x, weight_rows(second_block, column))
            sums_q[c, :, lanes] = value
            if column == q_cols:
                kvpart_out[...] = value.astype(BF16)
                kvpart_copy().start()

    def project_early():
        x = blocks[oc, early_block]
        for column in range(0, all_cols, 256):
            sums_q[oc, :, column : column + 256] = dot(x, weight_rows(early_block, column))

    def project_late(ch):
        x = blocks[oc, late_block, span(ch)]
        for column in range(0, all_cols, 256):
            lanes = slice(column, column + 256)
            value = sums_q[oc, span(ch), lanes] + dot(x, weight_rows(late_block, column))
            part_out[span(ch), lanes] = value.astype(BF16)
            if column == q_cols:
                sums_q[oc, span(ch), lanes] = value
        part_copy(ch).start()

    for ch in range(CHUNKS // 2 + 1, CHUNKS):
        first_arrivals(ch)
    info_copy.wait_recv()
    state_copy.wait_recv()
    done = 0

    def state_until(upto):
        for i in range(done, upto):
            state_pair(i)
        return upto

    for ch in range(CHUNKS):
        arrive(O2, 0, ch, (across_copy,))
        arrive(F0, 1, ch, (ahead_copy,))
        arrive(O0, 2, ch, (ahead_copy,))
        arrive(O1, 3, ch)
        done = state_until(pairs * (ch + 1) // (2 * CHUNKS))
    for load in loads[9:]:
        load.wait()
    project_first()
    for ch in range(CHUNKS):
        arrive(F0, 2, ch, (ahead_copy,))
        done = state_until(pairs * (CHUNKS + ch + 1) // (2 * CHUNKS))
    for ch in range(CHUNKS):
        arrive(O0, 3, ch)
    project_second()
    for ch in range(CHUNKS):
        arrive(F1, 2, ch)
        arrive(F1, 3, ch)
    project_early()
    for ch in range(CHUNKS):
        arrive(F1, 0, ch)
        arrive(F0, 3, ch)
        project_late(ch)

    kvpart_copy().wait_recv()
    their_r = jnp.broadcast_to(info_in[0:1], (128, rows)).T[:, 0:1]
    kv_all[oc] = ((sums_q[oc, :, q_cols:] + kvpart_in[...].astype(F32)) * their_r).astype(BF16)
    my_ids, their_ids = ids_row, info_in[8:9]
    at_first = jnp.where(c == 0, my_ids, their_ids)
    at_second = jnp.where(c == 0, their_ids, my_ids)
    key_ids = jnp.concatenate([at_first, at_second], axis=1)
    key_pos = lax.broadcasted_iota(jnp.int32, (step_rows, 2 * rows), 1)
    query_at = lax.broadcasted_iota(jnp.int32, (step_rows, 2 * rows), 0)
    attention = jnp.broadcast_to(kind_ref[...] == 1, (step_rows, width))

    def pipe_copy(ch):
        return pltpu.make_async_remote_copy(
            prod.at[ch],
            prev.at[ch],
            pipe_ssem.at[ch],
            pipe_rsem.at[ch],
            device_id={"pipe": p + 1},
            device_id_type=MESH,
        )

    def out_copy(ch):
        return pltpu.make_async_copy(prod.at[ch], out_hbm.at[span(ch)], out_sem.at[0, ch])

    def passed_copy(ch):
        return pltpu.make_async_copy(prev.at[ch], passed_hbm.at[span(ch)], out_sem.at[1, ch])

    for ch in range(CHUNKS):
        part_copy(ch).wait_recv()
        here = slice(ch * step_rows, (ch + 1) * step_rows)
        ours = sums_q[c, span(ch)] + part_in[span(ch)].astype(F32)
        ours = (ours * cols_ref[here, r_at : r_at + 1]).astype(BF16)
        kv_all[c, span(ch)] = ours[:, q_cols:]
        query = jnp.concatenate(
            [ours[:, head * HD : (head + 1) * HD] for head in range(q_heads)], axis=0
        )
        keys = kv_all[:, :, :HD].reshape(2 * rows, HD)
        values = kv_all[:, :, HD:].reshape(2 * rows, HD)
        scores = lax.dot_general(
            query, keys, (((1,), (1,)), ((), ())), preferred_element_type=F32
        ) * (HD ** (-0.5))
        wanted = (key_pos <= c * rows + ch * step_rows + query_at) & (
            key_ids == cols_ref[here, r_at + 8 : r_at + 9]
        )
        barred = jnp.where(wanted, 0.0, -1e30)
        scores = scores + jnp.concatenate([barred] * q_heads, axis=0)
        top = jnp.max(scores, axis=1, keepdims=True)
        probs = jnp.exp(scores - top)
        denom = jnp.sum(probs, axis=1, keepdims=True)
        mixed = (dot(probs.astype(BF16), values) / denom).astype(BF16).astype(F32)
        attended = jnp.concatenate(
            [mixed[head * step_rows : (head + 1) * step_rows] for head in range(q_heads)], axis=1
        )
        attended = (h_ref[span(ch)].astype(F32) + attended).astype(BF16).astype(F32)
        prod[ch] = jnp.where(attention, attended, state_res[span(ch)].astype(F32)).astype(BF16)
        out_copy(ch).start()

        @pl.when(p < pipes - 1)
        def _(ch=ch):
            pipe_copy(ch).start()

    for ch in range(CHUNKS):
        across_copy(O2, ch).wait_send()

        @pl.when(place < 3)
        def _(ch=ch):
            ahead_copy(F0, ch).wait_send()
            ahead_copy(O0, ch).wait_send()

        @pl.when((place == 1) | (place == 2))
        def _(ch=ch):
            ahead_copy(O1, ch).wait_send()
            behind_copy(O2, ch).wait_send()

        @pl.when(place == 1)
        def _(ch=ch):
            behind_copy(O1, ch).wait_send()
            behind_copy(F1, ch).wait_send()

        part_copy(ch).wait_send()
    kvpart_copy().wait_send()
    for k in peers:
        squares_copy(k, True).wait_send()
        sums_copy(k, True).wait_send()
    info_copy.wait_send()
    state_copy.wait_send()

    @pl.when(p == 0)
    def _():
        prev[...] = jnp.zeros(prev.shape, BF16)

    for k in range(CHUNKS):

        @pl.when(p > 0)
        def _(k=k):
            pipe_copy(k).wait_recv()

        passed_copy(k).start()
    for k in range(CHUNKS):
        out_copy(k).wait()
        passed_copy(k).wait()

    @pl.when(p < pipes - 1)
    def _():
        for k in range(CHUNKS):
            pipe_copy(k).wait_send()


def deliver(out_from, passed_from, out_to, passed_to, held, sem):
    rows = held.shape[1] // 2
    arriving, leaving = [], []
    for n, (source, into) in enumerate(((out_from, out_to), (passed_from, passed_to))):
        for k in range(2):
            part = pl.ds(k * rows, rows)
            place = held.at[n, part]
            arriving.append(pltpu.make_async_copy(source.at[part], place, sem.at[0, n, k]))
            leaving.append(pltpu.make_async_copy(place, into.at[part], sem.at[1, n, k]))
    for copy in arriving:
        copy.start()
    for before, after in zip(arriving, leaving):
        before.wait()
        after.start()
    for copy in leaving:
        copy.wait()


def fused(
    hidden_in,
    doc_ids,
    layer_kind,
    norm_gain,
    q_weight,
    k_weight,
    v_weight,
    bc_weight,
    dt_weight,
    dt_bias,
    decay_rate,
    skip_gain,
):
    _, rows, width = hidden_in.shape
    depth, q_cols = q_weight.shape[1:]
    kv_cols = k_weight.shape[2]
    heads = dt_bias.shape[1]
    n_state = bc_weight.shape[2] // 2
    tps = lax.axis_size("tp")
    anywhere = pl.BlockSpec(memory_space=pl.ANY)
    small = 2 * n_state + heads
    dma = pltpu.SemaphoreType.DMA
    shape = jax.ShapeDtypeStruct((rows, width), BF16)
    out, passed = pl.pallas_call(
        kernel,
        out_shape=(shape, shape),
        in_specs=[anywhere] * 12,
        out_specs=(anywhere, anywhere),
        scratch_shapes=[
            pltpu.VMEM((rows, width), BF16),
            pltpu.VMEM((1, width), F32),
            pltpu.VMEM((2 * n_state, width), BF16),
            pltpu.VMEM((heads * tps, width), BF16),
            pltpu.VMEM((1, rows), jnp.int32),
            pltpu.VMEM((1, 1), jnp.int32),
            pltpu.VMEM((1, heads), F32),
            pltpu.VMEM((1, heads), F32),
            pltpu.VMEM((1, heads), F32),
            pltpu.VMEM((2, tps, rows, width), BF16),
            pltpu.VMEM((depth, q_cols + 2 * kv_cols), BF16),
            pltpu.VMEM((rows, width), BF16),
            pltpu.VMEM((8, rows), F32),
            pltpu.VMEM((tps, 8, rows), F32),
            pltpu.VMEM((tps, small, rows), F32),
            pltpu.VMEM((tps, small, rows), F32),
            pltpu.VMEM((16, rows), F32),
            pltpu.VMEM((16, rows), F32),
            pltpu.VMEM((heads // 2, n_state, 2 * width // heads), BF16),
            pltpu.VMEM((heads // 2, n_state, 2 * width // heads), BF16),
            pltpu.VMEM((rows, q_cols + 2 * kv_cols), BF16),
            pltpu.VMEM((rows, q_cols + 2 * kv_cols), BF16),
            pltpu.VMEM((rows, 2 * kv_cols), BF16),
            pltpu.VMEM((rows, 2 * kv_cols), BF16),
            pltpu.VMEM((2, rows, q_cols + 2 * kv_cols), F32),
            pltpu.VMEM((2, rows, 2 * kv_cols), BF16),
            pltpu.VMEM((rows, width), BF16),
            pltpu.VMEM((rows, 128), F32),
            pltpu.VMEM((2 * heads, rows), F32),
            pltpu.VMEM((rows, heads), F32),
            pltpu.VMEM((2, rows, rows), F32),
            pltpu.VMEM((CHUNKS, rows // CHUNKS, width), BF16),
            pltpu.VMEM((CHUNKS, rows // CHUNKS, width), BF16),
            dma((12,)),
            dma((3, CHUNKS)),
            dma((3, CHUNKS)),
            dma((CHUNKS,)),
            dma((2, tps, CHUNKS)),
            dma((tps,)),
            dma((tps,)),
            dma((tps,)),
            dma((tps,)),
            dma((2,)),
            dma((2,)),
            dma((CHUNKS,)),
            dma((CHUNKS,)),
            dma((2,)),
            dma((CHUNKS,)),
            dma((CHUNKS,)),
            dma((2, CHUNKS)),
        ],
        compiler_params=pltpu.CompilerParams(
            collective_id=0, has_side_effects=True, vmem_limit_bytes=60 * 2**20
        ),
        cost_estimate=pl.CostEstimate(
            flops=4 * rows * depth * (q_cols + 2 * kv_cols),
            bytes_accessed=2 * depth * (q_cols + 2 * kv_cols),
            transcendentals=0,
        ),
    )(
        hidden_in[0],
        norm_gain,
        bc_weight[0].T,
        dt_weight[0].T,
        doc_ids[None],
        layer_kind[None],
        dt_bias,
        decay_rate,
        skip_gain,
        q_weight[0],
        k_weight[0],
        v_weight[0],
    )
    out, passed = pl.pallas_call(
        deliver,
        out_shape=(shape, shape),
        in_specs=[anywhere] * 2,
        out_specs=(anywhere, anywhere),
        scratch_shapes=[pltpu.VMEM((2, rows, width), BF16), dma((2, 2, 2))],
        compiler_params=pltpu.CompilerParams(vmem_limit_bytes=60 * 2**20),
    )(out, passed)
    return out[None], passed[None]


def solution(mesh):
    in_specs = (
        P("pipe", "ctx", "tp"),
        P("ctx"),
        P("pipe"),
        P("pipe", "tp"),
        P("pipe", "ctx", "tp"),
        P("pipe", "ctx", "tp"),
        P("pipe", "ctx", "tp"),
        P("pipe", "tp", None),
        P("pipe", "tp", None),
        P("pipe", "tp"),
        P("pipe", "tp"),
        P("pipe", "tp"),
    )
    out_specs = (P("pipe", "ctx", "tp"), P("pipe", "ctx", "tp"))
    body = fused if mesh.shape["ctx"] == 2 and mesh.shape["tp"] == 4 else shards
    return jax.shard_map(body, mesh=mesh, in_specs=in_specs, out_specs=out_specs, check_vma=False)
```
